32 devices in a mesh: groups: 2 (over y), gz: 4 (over z), dev: 2 (over x), xy: 2 (over core).
Axes of the slice: x: 2, y: 2, z: 4, core: 2. Of those that a mesh axis runs over, the one named last changes fastest.
Arguments:
- fields: float32 [12, 8, 64, 256], P('groups', 'dev', 'gz', 'xy'), parts along dimension 0, may hold values from -6 to 6
- spectra: float32 [24, 8, 64, 256], P('groups', 'dev', 'gz', 'xy'), parts along dimension 0, may hold values from -6 to 6
- permittivity: float32 [16, 64, 256], P(('groups', 'dev'), 'gz', 'xy'), parts along dimension 0, may hold values from 1 to 12
- phase_start: float32 [2], P('groups'), parts along dimension 0, may hold values from -3.140625 to 3.140625
- wall_owner: int32 [4, 4], P('gz'), may hold values from 0 to 3, as said below
- cap_owner: int32 [2, 32], replicated, may hold values from 0 to 3, as said below
- dir_index: int32 [2048], replicated, may hold values from 0 to 4095
- target: float32 [4096], P('groups'), parts along dimension 0, may hold values from 1 to 12
- aim_mask: int32 [4096], P('groups'), parts along dimension 0, may hold values 0 or 1
Outputs:
- fields_out: float32 [12, 8, 64, 256], P('groups', 'dev', 'gz', 'xy'), parts along dimension 0
- spectra_out: float32 [24, 8, 64, 256], P('groups', 'dev', 'gz', 'xy'), parts along dimension 0
- owned_currents: float32 [8, 2, 2, 20, 128], P(('groups', 'gz'), 'dev', 'xy'), parts along dimension 0
- intensity: float32 [4096], P(('groups', 'gz', 'dev', 'xy')), parts along dimension 0
- adjoint_currents: float32 [8, 2, 2, 36, 128], P(('groups', 'gz'), 'dev', 'xy'), parts along dimension 0
The draws below stay inside these ranges and needn't reach their ends.
There are 2 independent parts, one for each index of `groups`. The reference program is written for one: setup_inputs(seed, part) draws one part's arguments, and reference() takes and returns one part's arrays. A program takes and returns all parts, laid end to end along the dimension named above; an argument that names none is the same for every part. Nothing has to cross between parts.
Inputs may be any that keep to these rules, and one draw needn't show every extreme that they name: `wall_owner`: entry [s, j] names the index of gz that owns wall patch j of slab s; every index owns exactly 4 wall patches of a column, and a slab gives one index at most 1 of them. `cap_owner`: row 0 names the owner on gz of each patch of the lower cap, row 1 of the upper cap; each index owns exactly 8 patches of each cap, so that every index owns exactly 20 patches of a column.
All inputs are finite; a program needn't handle non-finite values.
Results may differ from the reference program's by a relative error of at most 0.0003.
Values sent between devices are 32-bit elements; how exact they have to be, the bound alone decides.
No kernel may reach another device: no remote copies, remote signals or barrier semaphores. Data moves between devices by JAX's collectives and lax.ppermute only.
A program may use at most 64 MiB of HBM per device.

```python
import math
import jax
import jax.numpy as jnp
from jax import lax

CX = 128
CY = 4
CZ = 16
PATCH = 16
XB = 8
ZB = 4
STEPS = 3
NDIR = 2048
THETAS = 64
NX = 256
NY = 8
NZ = 64
WALLP = 4
CAPP = 32
OWNED = 20
NSURF = 5120
N_GZ = 4
N_DEV = 2
N_XY = 2


def draw_wall_owner(key, part):
    offsets = jax.random.permutation(jax.random.fold_in(key, 11), N_GZ)
    sources = jnp.arange(N_GZ, dtype=jnp.int32)
    patches = jnp.arange(WALLP, dtype=jnp.int32)
    return ((sources[:, None] + offsets[patches % N_GZ][None, :]) % N_GZ).astype(jnp.int32)


def draw_cap_owner(key, part):
    lower = jax.random.permutation(jax.random.fold_in(key, 21), CAPP) % N_GZ
    upper = jax.random.permutation(jax.random.fold_in(key, 22), CAPP) % N_GZ
    return jnp.stack([lower, upper]).astype(jnp.int32)


def with_ends(entries, stream_key, low, high):
    longest = entries.shape.index(max(entries.shape))
    spots = []
    for shift in (0, 1):
        where = [jax.random.randint(jax.random.fold_in(stream_key, axis), (), 0, length) for axis, length in enumerate(entries.shape)]
        where[longest] = (where[longest] + shift) % entries.shape[longest]
        spots.append(tuple(where))
    return entries.at[spots[0]].set(low).at[spots[1]].set(high)


def levels(own_key, dims, cuts, least, top_value):
    factor_of = 1.0
    for axis_at, shards_of in cuts:
        heights = jax.random.uniform(jax.random.fold_in(jax.random.fold_in(own_key, 6), axis_at), (shards_of,), jnp.float32, least / len(cuts), top_value / len(cuts))
        factor_of = factor_of * jnp.repeat(jnp.exp(heights), dims[axis_at] // shards_of).reshape((-1,) + (1,) * (len(dims) - 1 - axis_at))
    return factor_of


def gaussian(stream_key, shape, deviation, limit, shards=(), held_as=jnp.bfloat16):
    drawn = deviation * jax.random.normal(stream_key, shape, jnp.float32)
    if shards:
        drawn = drawn * levels(stream_key, shape, shards, -0.22, 0.18)
    return jnp.clip(drawn, -limit, limit).astype(held_as)


def setup_inputs(seed: int = 0, part: int = 0) -> dict:
    streams_of = jax.random.split(jax.random.key(seed), 10)
    own_keys = jax.random.split(jax.random.fold_in(streams_of[9], part), 10)
    return {
        "fields": gaussian(own_keys[0], (6, NY, NZ, NX), 1.0, 6.0, ((1, 2), (2, 4), (3, 2)), jnp.float32),
        "spectra": gaussian(own_keys[1], (12, NY, NZ, NX), 1.0, 6.0, ((1, 2), (2, 4), (3, 2)), jnp.float32),
        "permittivity": jnp.clip(jnp.exp(math.log(12.0) - 2.4849066 * jax.random.uniform(own_keys[2], (NY, NZ, NX), jnp.float32) ** levels(own_keys[2], (NY, NZ, NX), ((0, 2), (1, 4), (2, 2)), -0.2, 0.2)), 1.0, 12.0),
        "phase_start": jnp.clip(jax.random.uniform(own_keys[3], (1,), jnp.float32, -3.140625, 3.140625), -3.140625, 3.140625),
        "wall_owner": draw_wall_owner(jax.random.fold_in(streams_of[9], 71), part),
        "cap_owner": draw_cap_owner(jax.random.fold_in(streams_of[9], 71), part),
        "dir_index": with_ends(jax.random.randint(streams_of[6], (NDIR,), 0, THETAS * THETAS), jax.random.fold_in(streams_of[6], 1), 0, (THETAS * THETAS) - 1).astype(jnp.int32),
        "target": jnp.clip(jax.random.uniform(own_keys[7], (NDIR,), jnp.float32, 1.0, 12.0), 1.0, 12.0),
        "aim_mask": with_ends((jax.random.randint(own_keys[8], (NDIR,), 0, 4) < 3).astype(jnp.int32), jax.random.fold_in(own_keys[8], 1), 0, 1),
    }


COURANT = 0.5
ANGULAR_STEP = 0.3
WAVE_NUMBER = 0.6
HIGHEST = lax.Precision.HIGHEST
CURRENT_SIGNS = (-1.0, 1.0, 1.0, -1.0)
X_PICKS = (5, 4, 2, 1)
Z_PICKS = (4, 3, 1, 0)

def ahead_diff(values, axis_number):
    length = values.shape[axis_number]
    shifted = jnp.concatenate([lax.slice_in_dim(values, 1, length, axis=axis_number), jnp.zeros_like(lax.slice_in_dim(values, 0, 1, axis=axis_number))], axis=axis_number)
    return shifted - values

def behind_diff(values, axis_number):
    length = values.shape[axis_number]
    shifted = jnp.concatenate([jnp.zeros_like(lax.slice_in_dim(values, 0, 1, axis=axis_number)), lax.slice_in_dim(values, 0, length - 1, axis=axis_number)], axis=axis_number)
    return values - shifted

def spectral_update(spectra_now, electric, magnetic, phase_start, step_number):
    angle_half = phase_start[0] + ANGULAR_STEP * (step_number + 0.5)
    angle_full = phase_start[0] + ANGULAR_STEP * (step_number + 1.0)
    return jnp.concatenate([spectra_now[0:3] + electric * jnp.cos(angle_full), spectra_now[3:6] + magnetic * jnp.cos(angle_half), spectra_now[6:9] - electric * jnp.sin(angle_full), spectra_now[9:12] - magnetic * jnp.sin(angle_half)])

def face_values(spectral_plane, facing, chosen):
    real_part = [CURRENT_SIGNS[number] * facing * spectral_plane[chosen[number]] for number in range(4)]
    imag_part = [CURRENT_SIGNS[number] * facing * spectral_plane[6 + chosen[number]] for number in range(4)]
    return jnp.stack(real_part + imag_part)

def to_vectors(record_values, x_flag):
    z_flag = 1.0 - x_flag
    stacked_rows = []
    for offset in (0, 4):
        tangent_one = record_values[offset]
        tangent_two = record_values[offset + 1]
        moment_one = record_values[offset + 2]
        moment_two = record_values[offset + 3]
        stacked_rows += [z_flag * tangent_one, x_flag * tangent_one + z_flag * tangent_two, x_flag * tangent_two, z_flag * moment_one, x_flag * moment_one + z_flag * moment_two, x_flag * moment_two]
    return jnp.stack(stacked_rows)

def to_record(gradient, x_flag):
    z_flag = 1.0 - x_flag
    stacked_rows = []
    for offset in (0, 6):
        stacked_rows += [x_flag * gradient[offset + 1] + z_flag * gradient[offset], x_flag * gradient[offset + 2] + z_flag * gradient[offset + 1], x_flag * gradient[offset + 4] + z_flag * gradient[offset + 3], x_flag * gradient[offset + 5] + z_flag * gradient[offset + 4]]
    return jnp.stack(stacked_rows)

def direction_frames(dir_index):
    polar_row = (dir_index // THETAS).astype(jnp.float32)
    azimuth_col = (dir_index % THETAS).astype(jnp.float32)
    polar_angle = jnp.pi * (polar_row + 0.5) / THETAS
    azimuth = 2.0 * jnp.pi * azimuth_col / THETAS
    sin_polar = jnp.sin(polar_angle)
    cos_polar = jnp.cos(polar_angle)
    sin_azim = jnp.sin(azimuth)
    cos_azim = jnp.cos(azimuth)
    unit_vectors = jnp.stack([sin_polar * cos_azim, sin_polar * sin_azim, cos_polar], axis=1)
    theta_hat = jnp.stack([cos_polar * cos_azim, cos_polar * sin_azim, -sin_polar], axis=1)
    phi_hat = jnp.stack([-sin_azim, cos_azim, jnp.zeros_like(sin_azim)], axis=1)
    return (unit_vectors, theta_hat, phi_hat)

def steering(unit_block, positions):
    angle_table = WAVE_NUMBER * (positions[0][:, None] * unit_block[None, :, 0] + positions[1][:, None] * unit_block[None, :, 1] + positions[2][:, None] * unit_block[None, :, 2])
    return (jnp.cos(angle_table), jnp.sin(angle_table))

def far_block(unit_block, currents, positions):
    cosine_table, sine_table = steering(unit_block, positions)
    real_part = jnp.dot(currents[:6], cosine_table, precision=HIGHEST) - jnp.dot(currents[6:], sine_table, precision=HIGHEST)
    imag_part = jnp.dot(currents[:6], sine_table, precision=HIGHEST) + jnp.dot(currents[6:], cosine_table, precision=HIGHEST)
    return jnp.concatenate([real_part, imag_part], axis=0)

def adjoint_block(unit_block, slope_block, positions):
    cosine_table, sine_table = steering(unit_block, positions)
    real_part = jnp.dot(slope_block[:6], cosine_table.T, precision=HIGHEST) + jnp.dot(slope_block[6:], sine_table.T, precision=HIGHEST)
    imag_part = jnp.dot(slope_block[6:], cosine_table.T, precision=HIGHEST) - jnp.dot(slope_block[:6], sine_table.T, precision=HIGHEST)
    return jnp.concatenate([real_part, imag_part], axis=0)

def intensity_and_slope(far_total, theta_hat, phi_hat, target, aim_mask):
    theta_rows = theta_hat.T
    phi_rows = phi_hat.T

    def project(vectors, frame_rows):
        return lax.optimization_barrier(jnp.sum(vectors * frame_rows, axis=0))
    e_theta_re = -(project(far_total[3:6], phi_rows) + project(far_total[0:3], theta_rows))
    e_phi_re = project(far_total[3:6], theta_rows) - project(far_total[0:3], phi_rows)
    e_theta_im = -(project(far_total[9:12], phi_rows) + project(far_total[6:9], theta_rows))
    e_phi_im = project(far_total[9:12], theta_rows) - project(far_total[6:9], phi_rows)
    intensity = e_theta_re * e_theta_re + e_theta_im * e_theta_im + e_phi_re * e_phi_re + e_phi_im * e_phi_im
    residual = aim_mask.astype(jnp.float32) * (intensity - target)
    slope_theta_re = 2.0 * residual * e_theta_re
    slope_phi_re = 2.0 * residual * e_phi_re
    slope_theta_im = 2.0 * residual * e_theta_im
    slope_phi_im = 2.0 * residual * e_phi_im
    n_re = -slope_theta_re * theta_rows - slope_phi_re * phi_rows
    l_re = -slope_theta_re * phi_rows + slope_phi_re * theta_rows
    n_im = -slope_theta_im * theta_rows - slope_phi_im * phi_rows
    l_im = -slope_theta_im * phi_rows + slope_phi_im * theta_rows
    return (intensity, jnp.concatenate([n_re, l_re, n_im, l_im], axis=0))

def arrange(wall_values, cap_values):
    walls = wall_values.reshape(N_XY, 8, N_DEV, CY, N_GZ, CZ).transpose(4, 2, 0, 1, 3, 5)
    walls = walls.reshape(N_GZ, N_DEV, N_XY, 8, WALLP, PATCH).transpose(0, 1, 2, 4, 3, 5).reshape(N_GZ, N_DEV, N_XY, WALLP, 8 * PATCH)
    caps = cap_values.reshape(2, 8, N_DEV, CY, N_XY, CX).transpose(0, 2, 4, 1, 3, 5)
    caps = caps.reshape(2, N_DEV, N_XY, 8, CAPP, PATCH).transpose(0, 1, 2, 4, 3, 5).reshape(2, N_DEV, N_XY, CAPP, 8 * PATCH)
    middle = jnp.zeros((N_GZ - 2, N_DEV, N_XY, CAPP, 8 * PATCH), jnp.float32)
    cap_rows = jnp.concatenate([caps[0:1], middle, caps[1:2]], axis=0)
    return jnp.concatenate([walls, cap_rows], axis=3)

def gather_owned(records, wall_owner, cap_owner):
    flat_walls = records[:, :, :, :WALLP].transpose(0, 3, 1, 2, 4).reshape(N_GZ * WALLP, N_DEV, N_XY, 8 * PATCH)
    caps_lower = records[0, :, :, WALLP:].transpose(2, 0, 1, 3)
    caps_upper = records[N_GZ - 1, :, :, WALLP:].transpose(2, 0, 1, 3)
    flat_records = jnp.concatenate([flat_walls, caps_lower, caps_upper], axis=0)
    owner_flat = jnp.concatenate([wall_owner.reshape(N_GZ * WALLP), cap_owner[0], cap_owner[1]]).astype(jnp.int32)
    total = N_GZ * WALLP + 2 * CAPP
    flat_order = jnp.arange(total, dtype=jnp.int32)
    earlier_same = (owner_flat[:, None] == owner_flat[None, :]) & (flat_order[None, :] < flat_order[:, None])
    slot_rank = lax.optimization_barrier(jnp.sum(earlier_same.astype(jnp.int32), axis=1)).astype(jnp.int32)
    owner_range = jnp.arange(N_GZ, dtype=jnp.int32)
    place_range = jnp.arange(OWNED, dtype=jnp.int32)
    matches = (owner_flat[None, None, :] == owner_range[:, None, None]) & (slot_rank[None, None, :] == place_range[None, :, None])
    selector = jnp.where(matches, 1.0, 0.0).astype(jnp.float32)
    return jnp.einsum('okg,gdhr->odhkr', selector, flat_records, precision=HIGHEST)

def reference(fields, spectra, permittivity, phase_start, wall_owner, cap_owner, dir_index, target, aim_mask):
    step_rate = COURANT / permittivity
    electric_list = [fields[0], fields[1], fields[2]]
    magnetic_list = [fields[3], fields[4], fields[5]]
    spectra_now = spectra
    for step_number in range(STEPS):
        magn_x = magnetic_list[0] - COURANT * (ahead_diff(electric_list[2], 0) - ahead_diff(electric_list[1], 1))
        magn_y = magnetic_list[1] - COURANT * (ahead_diff(electric_list[0], 1) - ahead_diff(electric_list[2], 2))
        magn_z = magnetic_list[2] - COURANT * (ahead_diff(electric_list[1], 2) - ahead_diff(electric_list[0], 0))
        magnetic_list = [magn_x, magn_y, magn_z]
        elec_x = electric_list[0] + step_rate * (behind_diff(magn_z, 0) - behind_diff(magn_y, 1))
        elec_y = electric_list[1] + step_rate * (behind_diff(magn_x, 1) - behind_diff(magn_z, 2))
        elec_z = electric_list[2] + step_rate * (behind_diff(magn_y, 2) - behind_diff(magn_x, 0))
        electric_list = [elec_x, elec_y, elec_z]
        spectra_now = spectral_update(spectra_now, jnp.stack(electric_list), jnp.stack(magnetic_list), phase_start, step_number)
    fields_out = jnp.stack(electric_list + magnetic_list)
    wall_values = jnp.stack([face_values(spectra_now[:, :, :, XB], -1.0, X_PICKS), face_values(spectra_now[:, :, :, NX - 1 - XB], 1.0, X_PICKS)])
    cap_values = jnp.stack([face_values(spectra_now[:, :, ZB, :], -1.0, Z_PICKS), face_values(spectra_now[:, :, NZ - 1 - ZB, :], 1.0, Z_PICKS)])
    records = arrange(wall_values, cap_values)
    owned_currents = gather_owned(records, wall_owner, cap_owner)
    wall_points = 2 * NY * NZ
    cap_points = 2 * NY * NX
    point_values = jnp.concatenate([wall_values.transpose(1, 0, 2, 3).reshape(8, wall_points), cap_values.transpose(1, 0, 2, 3).reshape(8, cap_points)], axis=1)
    x_flag = jnp.concatenate([jnp.ones((wall_points,), jnp.float32), jnp.zeros((cap_points,), jnp.float32)])
    y_grid = jnp.arange(NY, dtype=jnp.float32) - (NY - 1) / 2.0
    z_grid = jnp.arange(NZ, dtype=jnp.float32) - (NZ - 1) / 2.0
    x_grid = jnp.arange(NX, dtype=jnp.float32) - (NX - 1) / 2.0
    wall_x = jnp.array([XB, NX - 1 - XB], dtype=jnp.float32) - (NX - 1) / 2.0
    cap_z = jnp.array([ZB, NZ - 1 - ZB], dtype=jnp.float32) - (NZ - 1) / 2.0
    wall_shape = (2, NY, NZ)
    cap_shape = (2, NY, NX)
    wall_positions = jnp.stack([jnp.broadcast_to(wall_x[:, None, None], wall_shape), jnp.broadcast_to(y_grid[None, :, None], wall_shape), jnp.broadcast_to(z_grid[None, None, :], wall_shape)]).reshape(3, wall_points)
    cap_positions = jnp.stack([jnp.broadcast_to(x_grid[None, None, :], cap_shape), jnp.broadcast_to(y_grid[None, :, None], cap_shape), jnp.broadcast_to(cap_z[:, None, None], cap_shape)]).reshape(3, cap_points)
    positions = jnp.concatenate([wall_positions, cap_positions], axis=1)
    norm_scale = 1.0 / math.sqrt(2.0 * NSURF)
    currents = to_vectors(point_values, x_flag) * norm_scale
    unit_vectors, theta_hat, phi_hat = direction_frames(dir_index)
    block_rows = 128
    unit_blocks = unit_vectors.reshape(NDIR // block_rows, block_rows, 3)

    def far_of_block(unit_block):
        return far_block(unit_block, currents, positions)
    far_total = lax.map(far_of_block, unit_blocks).transpose(1, 0, 2).reshape(12, NDIR)
    intensity, slope_total = intensity_and_slope(far_total, theta_hat, phi_hat, target, aim_mask)
    slope_blocks = slope_total.reshape(12, NDIR // block_rows, block_rows).transpose(1, 0, 2)

    def add_block(carry_sum, pieces):
        return (carry_sum + adjoint_block(pieces[0], pieces[1], positions), None)
    gradient, ignored = lax.scan(add_block, jnp.zeros((12, NSURF), jnp.float32), (unit_blocks, slope_blocks))
    point_adjoint = to_record(gradient * norm_scale, x_flag)
    adjoint_walls = point_adjoint[:, :wall_points].reshape(8, 2, NY, NZ).transpose(1, 0, 2, 3)
    adjoint_caps = point_adjoint[:, wall_points:].reshape(8, 2, NY, NX).transpose(1, 0, 2, 3)
    adjoint_currents = arrange(adjoint_walls, adjoint_caps)
    return (fields_out, spectra_now, owned_currents, intensity, adjoint_currents)
```

```python
import functools
import math

import jax
import jax.numpy as jnp
from jax import lax
from jax.experimental import pallas as pl
from jax.experimental.pallas import tpu as pltpu
from jax.sharding import PartitionSpec as P

PATCH = 16
XB = 8
ZB = 4
STEPS = 3
THETAS = 64
COURANT = 0.5
ANGULAR_STEP = 0.3
WAVE_NUMBER = 0.6
CURRENT_SIGNS = (-1.0, 1.0, 1.0, -1.0)
X_PICKS = (5, 4, 2, 1)
Z_PICKS = (4, 3, 1, 0)
LANES = 128
HALO = STEPS
F32 = jnp.float32
BF16 = jnp.bfloat16
VMEM = pl.BlockSpec(memory_space=pltpu.VMEM)
SMEM = pl.BlockSpec(memory_space=pltpu.SMEM)


def up8(rows):
    return -(-rows // 8) * 8


def sincos(angle):
    turns = jnp.floor(angle * (2.0 / math.pi) + 0.5)
    r = angle - turns * 1.5703125
    r = r - turns * 4.837512969970703125e-4
    r = r - turns * 7.54978995489188e-8
    r2 = r * r
    s = r + r * r2 * (-1.6666654611e-1 + r2 * (8.3321608736e-3 + r2 * -1.9515295891e-4))
    c = 1.0 - 0.5 * r2 + r2 * r2 * (
        4.166664568298827e-2 + r2 * (-1.388731625493765e-3 + r2 * 2.443315711809948e-5)
    )
    quarter = turns.astype(jnp.int32)
    odd = (quarter & 1) == 1
    sine = jnp.where(odd, c, s)
    cosine = jnp.where(odd, s, c)
    sine = jnp.where((quarter & 2) == 2, -sine, sine)
    cosine = jnp.where(((quarter + 1) & 2) == 2, -cosine, cosine)
    return sine, cosine


def split(values):
    high = values.astype(BF16)
    return high, (values - high.astype(F32)).astype(BF16)


def rows_iota(shape):
    return lax.broadcasted_iota(jnp.int32, shape, 0)


def lanes_iota(shape):
    return lax.broadcasted_iota(jnp.int32, shape, len(shape) - 1)


class Sizes:
    def __init__(self, block, directions, caps):
        self.gz, self.dev, self.xy = (lax.axis_size(a) for a in ("gz", "dev", "xy"))
        self.y, self.z, self.x = block
        self.both_y = self.dev > 2
        self.rows = self.y + HALO * (2 if self.both_y else 1)
        self.nx, self.ny, self.nz = self.x * self.xy, self.y * self.dev, self.z * self.gz
        self.dirs = directions
        self.tiles = directions // LANES
        self.walls = self.y * self.z // PATCH
        self.caps = caps
        self.share = caps // self.gz
        self.chunk = up8(2 + self.share)
        self.far_rows = 4 * self.tiles
        self.norm = 1.0 / math.sqrt(2.0 * (2 * self.ny * self.nz + 2 * self.ny * self.nx))
        self.y_rows = 7 * HALO * self.z
        self.z_rows = up8(7 * self.y * HALO)
        self.e_rows = up8(7 * HALO * HALO)
        y_kinds = 2 if self.both_y else 1
        sizes = [self.y_rows] * y_kinds + [self.z_rows] * 2 + [self.e_rows] * (2 * y_kinds)
        self.starts = [sum(sizes[:i]) for i in range(len(sizes))]
        self.halo_rows = sum(sizes)
        self.y_kinds = y_kinds


def pack_kernel(n, f_ref, eps_ref, *outs):
    own, y_outs, z_outs, e_outs = (
        outs[0],
        outs[1 : 1 + n.y_kinds],
        outs[1 + n.y_kinds : 3 + n.y_kinds],
        outs[3 + n.y_kinds :],
    )
    gz_even = lax.axis_index("gz") % 2 == 0
    dev_even = lax.axis_index("dev") % 2 == 0
    for c in range(7):
        for y in range(n.y):
            value = f_ref[c, y] if c < 6 else COURANT / eps_ref[y]
            own[pl.ds((c * n.y + y) * n.z, n.z), :] = value
    for c in range(7):
        at = lambda y: own[pl.ds((c * n.y + y) * n.z, n.z), :]
        for kind in range(n.y_kinds):
            top = dev_even if kind == 0 else jnp.logical_not(dev_even)
            for r in range(HALO):
                value = jnp.where(top, at(n.y - HALO + r), at(r))
                y_outs[kind][pl.ds((c * HALO + r) * n.z, n.z), :] = value
                for z_kind in range(2):
                    z_top = gz_even if z_kind == 0 else jnp.logical_not(gz_even)
                    edge = jnp.where(z_top, value[n.z - HALO :], value[:HALO])
                    e_outs[kind * 2 + z_kind][pl.ds((c * HALO + r) * HALO, HALO), :] = edge
        for z_kind in range(2):
            z_top = gz_even if z_kind == 0 else jnp.logical_not(gz_even)
            for y in range(n.y):
                value = at(y)
                edge = jnp.where(z_top, value[n.z - HALO :], value[:HALO])
                z_outs[z_kind][pl.ds((c * n.y + y) * HALO, HALO), :] = edge


def table_kernel(n, dir_ref, owner_ref, hi_ref, lo_ref, v_ref, place_ref, count_ref):
    gz, dev, xy = (lax.axis_index(a) for a in ("gz", "dev", "xy"))
    index = dir_ref[...]
    bits = THETAS.bit_length() - 1
    polar = (index >> bits).astype(F32)
    azimuth = (index & (THETAS - 1)).astype(F32)
    sin_t, cos_t = sincos(math.pi * (polar + 0.5) / THETAS)
    sin_f, cos_f = sincos(2.0 * math.pi * azimuth / THETAS)
    kx = WAVE_NUMBER * (sin_t * cos_f)
    ky = WAVE_NUMBER * (sin_t * sin_f)
    kz = WAVE_NUMBER * cos_t
    theta = (cos_t * cos_f, cos_t * sin_f, -sin_t)
    phi = (-sin_f, cos_f, jnp.zeros_like(sin_f))
    is_end = jnp.logical_or(gz == 0, gz == n.gz - 1)
    cap_scale = jnp.where(is_end, n.norm, 0.0).astype(F32)
    x_first = (xy * n.x).astype(F32) - (n.nx - 1) / 2.0
    y_first = (dev * n.y).astype(F32) - (n.ny - 1) / 2.0
    z_first = (gz * n.z).astype(F32) - (n.nz - 1) / 2.0
    x_wall = x_first + jnp.where(xy == 0, XB, n.x - 1 - XB).astype(F32)
    z_cap = z_first + jnp.where(gz == 0, ZB, n.z - 1 - ZB).astype(F32)
    row8 = rows_iota((8, LANES))
    row16 = rows_iota((16, LANES))
    fine_x = row8.astype(F32)
    low = row8 < 4
    comp = row8 & 3

    def weights(rows):
        picked = jnp.where(comp == 2, rows[2], rows[3])
        return jnp.where(comp == 0, rows[0], jnp.where(comp == 1, rows[1], picked))

    for t in range(n.tiles):
        lanes = slice(t * LANES, (t + 1) * LANES)
        a, b, c = (v[t : t + 1, :] for v in (kx, ky, kz))
        th = [v[t : t + 1, :] for v in theta]
        ph = [v[t : t + 1, :] for v in phi]
        sf, cf = sincos(a * fine_x)
        for pair in range(n.x // 16):
            if pair % 8 == 0:
                base_x = x_first + 8.0 * 16.0 * (pair // 8)
                coarse_s, coarse_c = sincos(a * (row16.astype(F32) * 8.0 + base_x))
            cosine, sine = [], []
            for h in (2 * (pair % 8), 2 * (pair % 8) + 1):
                cc, cs = coarse_c[h : h + 1, :], coarse_s[h : h + 1, :]
                cosine.append(cc * cf - cs * sf)
                sine.append(cs * cf + cc * sf)
            for part, rows in ((0, cosine), (n.x, sine)):
                high, rest = split(jnp.concatenate(rows, axis=0))
                hi_ref[part + pair * 16 : part + pair * 16 + 16, lanes] = high
                lo_ref[part + pair * 16 : part + pair * 16 + 16, lanes] = rest
        zs, zc = sincos(c * (row16.astype(F32) + z_first))
        for part, rows in ((2 * n.x, zc), (2 * n.x + n.z, zs)):
            high, rest = split(rows)
            hi_ref[part : part + 16, lanes] = high
            lo_ref[part : part + 16, lanes] = rest
        y_of = comp.astype(F32) + y_first
        base_s, base_c = sincos(b * y_of + jnp.where(low, c * z_cap, a * x_wall))
        for face in range(2):
            i, j = ((0, 1), (1, 2))[face]
            scale = cap_scale if face == 0 else n.norm
            w_theta = weights([-th[i], -th[j], -ph[i], -ph[j]]) * scale
            w_phi = weights([-ph[i], -ph[j], th[i], th[j]]) * scale
            for y in range(n.y):
                r = face * 4 + y
                bc, bs = base_c[r : r + 1, :], base_s[r : r + 1, :]
                one = jnp.where(low, bc, -bs)
                two = jnp.where(low, bs, bc)
                for kind, value in enumerate(
                    (one * w_theta, one * w_phi, two * w_theta, two * w_phi)
                ):
                    at = ((face * 4 + kind) * n.y + y) * 8
                    v_ref[at : at + 8, lanes] = value
    for o in range(n.gz):
        count_ref[o] = 0
    which = jnp.where(gz == 0, 0, 1)

    def place(q, carry):
        owner = owner_ref[which, q]
        rank = count_ref[owner]
        count_ref[owner] = rank + 1
        place_ref[q] = owner * n.chunk + 2 + rank
        return carry

    lax.fori_loop(0, n.caps, place, 0)


def block_transpose(values):
    row, block = rows_iota((8, LANES)), lanes_iota((8, LANES)) // PATCH
    for bit in (1, 2, 4):
        wide = PATCH * bit
        ahead = pltpu.roll(pltpu.roll(values, 8 - bit, 0), wide, 1)
        behind = pltpu.roll(pltpu.roll(values, bit, 0), LANES - wide, 1)
        row_bit, block_bit = (row & bit) != 0, (block & bit) != 0
        moved = jnp.where(row_bit, behind, ahead)
        values = jnp.where(row_bit == block_bit, values, moved)
    return values


def turn(values):
    swapped = pltpu.roll(values, 4, 0)
    return jnp.where(rows_iota(values.shape) < 4, -swapped, swapped)


def main_kernel(
    n, own_ref, other_ref, halo_ref, far_halo_ref, spectra_ref, phase_ref, wall_owner_ref, place_ref,
    hi_ref, lo_ref, v_ref, fields_out, spectra_out, far_out, chunk_out, a_ref, m_ref,
):
    gz, dev, xy = (lax.axis_index(a) for a in ("gz", "dev", "xy"))
    gz_even, dev_even = gz % 2 == 0, dev % 2 == 0
    deep = n.z + 8
    lo_ok, hi_ok = gz > 0, gz < n.gz - 1
    if n.both_y:
        y_own = HALO
        y_slots = (
            (0, jnp.logical_not(dev_even), dev > 0),
            (HALO + n.y, dev_even, dev < n.dev - 1),
        )
    else:
        y_own = jnp.where(dev_even, 0, HALO)
        y_slots = ((jnp.where(dev_even, n.y, 0), None, None),)
    pad = jnp.zeros((8 - 2 * HALO, LANES), F32)

    def choose(ref, starts, use_first, length):
        if use_first is None:
            return ref[pl.ds(starts[0], length), :]
        return jnp.where(
            use_first, ref[pl.ds(starts[0], length), :], ref[pl.ds(starts[1], length), :]
        )

    kinds = n.y_kinds
    for half, (block, halo) in enumerate(((own_ref, halo_ref), (other_ref, far_halo_ref))):
        at_x = xy if half == 0 else 1 - xy
        lanes = pl.ds(pl.multiple_of(at_x * n.x, n.x), n.x)

        def rim(first, second):
            high = jnp.where(gz_even, first, second)
            low = jnp.where(gz_even, second, first)
            return jnp.concatenate(
                [jnp.where(hi_ok, high, 0.0), pad, jnp.where(lo_ok, low, 0.0)], axis=0
            )

        for c in range(7):
            for y in range(n.y):
                a_ref[c, y_own + y, 0 : n.z, lanes] = block[pl.ds((c * n.y + y) * n.z, n.z), :]
                at = (c * n.y + y) * HALO
                first = halo[pl.ds(n.starts[kinds] + at, HALO), :]
                second = halo[pl.ds(n.starts[kinds + 1] + at, HALO), :]
                a_ref[c, y_own + y, n.z : deep, lanes] = rim(first, second)
            for start, use_first, ok in y_slots:
                for r in range(HALO):
                    at = (c * HALO + r) * n.z
                    body = choose(halo, [n.starts[k] + at for k in range(kinds)], use_first, n.z)
                    at = (c * HALO + r) * HALO
                    edges = [
                        choose(
                            halo,
                            [n.starts[kinds + 2 + 2 * k + e] + at for k in range(kinds)],
                            use_first,
                            HALO,
                        )
                        for e in range(2)
                    ]
                    edge = rim(*edges)
                    if ok is not None:
                        body, edge = jnp.where(ok, body, 0.0), jnp.where(ok, edge, 0.0)
                    a_ref[c, start + r, 0 : n.z, lanes] = body
                    a_ref[c, start + r, n.z : deep, lanes] = edge

    shape = (deep, n.nx)
    z_row, x_lane = rows_iota(shape), lanes_iota(shape)
    keep = jnp.where(z_row < n.z + HALO, COURANT, jnp.where(lo_ok & (z_row >= deep - HALO), COURANT, 0.0))
    keep = keep.astype(F32)
    last_x, first_x = x_lane == n.nx - 1, x_lane == 0

    def z_next(v):
        return pltpu.roll(v, deep - 1, 0)

    def z_before(v):
        return pltpu.roll(v, 1, 0)

    def x_next(v):
        return jnp.where(last_x, 0.0, pltpu.roll(v, n.nx - 1, 1))

    def x_before(v):
        return jnp.where(first_x, 0.0, pltpu.roll(v, 1, 1))

    angle_row = rows_iota((8, LANES))
    step_of = (angle_row // 2).astype(F32)
    part_of = jnp.where((angle_row & 1) == 0, 0.5, 1.0)
    sines, cosines = sincos(phase_ref[0] + ANGULAR_STEP * (step_of + part_of))
    own_lanes = pl.ds(pl.multiple_of(xy * n.x, n.x), n.x)
    for step in range(STEPS):
        for y in range(n.rows):
            ex, ey, ez = (a_ref[c, y] for c in range(3))
            if y + 1 < n.rows:
                ex_y, ez_y = a_ref[0, y + 1] - ex, a_ref[2, y + 1] - ez
            else:
                ex_y, ez_y = -ex, -ez
            rate = keep
            if n.both_y and y < HALO:
                rate = jnp.where(dev == 0, 0.0, keep)
            a_ref[3, y] = a_ref[3, y] - rate * (ez_y - (z_next(ey) - ey))
            a_ref[4, y] = a_ref[4, y] - rate * ((z_next(ex) - ex) - (x_next(ez) - ez))
            a_ref[5, y] = a_ref[5, y] - rate * ((x_next(ey) - ey) - ex_y)
        for y in range(n.rows):
            hx, hy, hz = (a_ref[c, y] for c in range(3, 6))
            rate = a_ref[6, y]
            if y > 0:
                hx_y, hz_y = hx - a_ref[3, y - 1], hz - a_ref[5, y - 1]
            else:
                hx_y, hz_y = hx, hz
            a_ref[0, y] = a_ref[0, y] + rate * (hz_y - (hy - z_before(hy)))
            a_ref[1, y] = a_ref[1, y] + rate * ((hx - z_before(hx)) - (hz - x_before(hz)))
            a_ref[2, y] = a_ref[2, y] + rate * ((hy - x_before(hy)) - hx_y)
        source = spectra_ref if step == 0 else spectra_out
        for c in range(6):
            row = 2 * step + (1 if c < 3 else 0)
            cosine, sine = cosines[row : row + 1, :], sines[row : row + 1, :]
            for y in range(n.y):
                value = a_ref[c, y_own + y, 0 : n.z, own_lanes]
                spectra_out[c, y] = source[c, y] + value * cosine
                spectra_out[6 + c, y] = source[6 + c, y] - value * sine
                if step == STEPS - 1:
                    fields_out[c, y] = value

    facing_x = jnp.where(xy == 0, -1.0, 1.0).astype(F32)
    facing_z = jnp.where(gz == 0, -1.0, 1.0).astype(F32)
    row8, lane = rows_iota((8, LANES)), lanes_iota((8, LANES))
    sign = jnp.where(((row8 & 3) == 0) | ((row8 & 3) == 3), -1.0, 1.0).astype(F32)
    own_block = lane // PATCH == row8
    block_sign = jnp.sum(jnp.where(own_block, sign, 0.0), axis=0, keepdims=True)
    cap_left, cap_right, wall_left = [], [], []
    chunk_out[...] = jnp.zeros_like(chunk_out)
    for y in range(n.y):
        plane = [
            jnp.where(gz == 0, spectra_out[p, y, ZB : ZB + 1, :], spectra_out[p, y, n.z - 1 - ZB : n.z - ZB, :])
            for p in [k + 6 * im for im in range(2) for k in Z_PICKS]
        ]
        current = jnp.concatenate(plane, axis=0) * (sign * facing_z)
        cap_left.append(current)
        cap_right.append(turn(current))
        m_ref[y * 8 : y * 8 + 8, :] = block_transpose(current)
        stack = jnp.concatenate(
            [spectra_out[k + 6 * im, y] for im in range(2) for k in X_PICKS], axis=0
        )
        across = stack.T
        record = jnp.where(xy == 0, across[XB : XB + 1, :], across[n.x - 1 - XB : n.x - XB, :])
        record = record * (block_sign * facing_x)
        for o in range(n.gz):
            mine = wall_owner_ref[0, y] == o
            at = o * n.chunk
            chunk_out[at : at + 1, :] += jnp.where(mine, record, 0.0)
            chunk_out[at + 1 : at + 2, :] += jnp.where(mine, 1.0, 0.0).astype(F32)
        spread = jnp.where(own_block, record, 0.0)
        for wide in (16, 32, 64):
            spread = spread + pltpu.roll(spread, wide, 1)
        wall_left.append(jnp.where(lane < n.z, spread, turn(spread))[:, : 2 * n.z])
    for q in range(n.caps):
        chunk_out[pl.ds(place_ref[q], 1), :] = m_ref[q : q + 1, :]
    cap = jnp.concatenate(
        [jnp.concatenate(cap_left, axis=0), jnp.concatenate(cap_right, axis=0)], axis=1
    )
    wall = jnp.concatenate(wall_left, axis=0)
    dot = functools.partial(jnp.dot, preferred_element_type=F32)
    wide = min(512, n.dirs)
    for first in range(0, n.dirs, wide):
        sums = []
        for left, rows in ((cap, slice(0, 2 * n.x)), (wall, slice(2 * n.x, 2 * n.x + 2 * n.z))):
            left_hi, left_lo = split(left)
            high, rest = hi_ref[rows, first : first + wide], lo_ref[rows, first : first + wide]
            sums.append(dot(left_hi, high) + (dot(left_lo, high) + dot(left_hi, rest)))
        for t in range(wide // LANES):
            lanes = slice(first + t * LANES, first + (t + 1) * LANES)
            tile = first // LANES + t
            for kind in range(4):
                total = None
                for face in range(2):
                    for y in range(n.y):
                        at = ((face * 4 + kind) * n.y + y) * 8
                        term = v_ref[at : at + 8, lanes] * sums[face][
                            y * 8 : y * 8 + 8, t * LANES : (t + 1) * LANES
                        ]
                        total = term if total is None else total + term
                far_out[kind * n.tiles + tile : kind * n.tiles + tile + 1, :] = jnp.sum(
                    total, axis=0, keepdims=True
                )


def adjoint_kernel(n, far_ref, target_ref, mask_ref, hi_ref, lo_ref, v_ref, intensity_out, owned_out, adjoint_out):
    gz, dev, xy = (lax.axis_index(a) for a in ("gz", "dev", "xy"))
    block = n.far_rows + n.chunk
    parts = []
    for kind in range(4):
        total = None
        for k in range(n.gz):
            at = k * block + kind * n.tiles
            term = far_ref[at : at + n.tiles, :]
            total = term if total is None else total + term
        parts.append(total)
    theta_re, phi_re, theta_im, phi_im = parts
    intensity = theta_re * theta_re + theta_im * theta_im + phi_re * phi_re + phi_im * phi_im
    intensity_out[...] = intensity
    slope = 2.0 * (mask_ref[...].astype(F32) * (intensity - target_ref[...]))
    slopes = [slope * part for part in parts]

    faces = [[], []]
    for face in range(2):
        for t in range(n.tiles):
            lanes = slice(t * LANES, (t + 1) * LANES)
            rows = []
            for y in range(n.y):
                total = None
                for kind in range(4):
                    at = ((face * 4 + kind) * n.y + y) * 8
                    term = v_ref[at : at + 8, lanes] * slopes[kind][t : t + 1, :]
                    total = term if total is None else total + term
                rows.append(total)
            faces[face].append(jnp.concatenate(rows, axis=0))
    dot = functools.partial(
        lax.dot_general,
        dimension_numbers=(((1,), (1,)), ((), ())),
        preferred_element_type=F32,
    )
    sums = []
    for face, rows in ((0, slice(0, 2 * n.x)), (1, slice(2 * n.x, 2 * n.x + 2 * n.z))):
        left_hi, left_lo = split(jnp.concatenate(faces[face], axis=1))
        high, rest = hi_ref[rows, :], lo_ref[rows, :]
        sums.append(dot(left_hi, high) + (dot(left_lo, high) + dot(left_hi, rest)))
    cap, wall = sums
    row8, lane = rows_iota((8, LANES)), lanes_iota((8, LANES))
    own_block = lane // PATCH == row8
    for y in range(n.y):
        at = slice(y * 8, y * 8 + 8)
        gradient = cap[at, : n.x] - turn(cap[at, n.x :])
        adjoint_out[n.walls + y * 8 : n.walls + y * 8 + 8, :] = block_transpose(gradient)
        gradient = wall[at, : n.z] - turn(wall[at, n.z :])
        spread = jnp.concatenate([gradient] * (LANES // n.z), axis=1)
        adjoint_out[y : y + 1, :] = jnp.sum(
            jnp.where(own_block, spread, 0.0), axis=0, keepdims=True
        )
    walls = [jnp.zeros((1, LANES), F32) for _ in range(n.walls)]
    rank = jnp.zeros((1, LANES), F32)
    for s in range(n.gz):
        at = pl.multiple_of((gz ^ s) * block + n.far_rows, 8)
        rows = far_ref[pl.ds(at, 8), :]
        record, flag = rows[0:1, :], rows[1:2, :] > 0.5
        for r in range(n.walls):
            walls[r] = jnp.where(flag & (rank == float(r)), record, walls[r])
        rank = rank + rows[1:2, :]
    for r in range(n.walls):
        owned_out[r : r + 1, :] = walls[r]
    for cap_at, s in enumerate((0, n.gz - 1)):
        at = pl.multiple_of((gz ^ s) * block + n.far_rows, 8)
        rows = far_ref[pl.ds(at, n.chunk), :]
        owned_out[n.walls + cap_at * n.share : n.walls + (cap_at + 1) * n.share, :] = rows[2 : 2 + n.share, :]


def partner(kind, i, n):
    up = (i % 2 == 0) == (kind == 0)
    return (i + 1) % n if up else (i - 1) % n


def exchange(values, axes, image):
    sizes = [lax.axis_size(a) for a in axes]
    pairs = []
    for source in range(math.prod(sizes)):
        rest, where = source, []
        for size in reversed(sizes):
            where.insert(0, rest % size)
            rest //= size
        target = 0
        for size, at in zip(sizes, image(*where)):
            target = target * size + at
        pairs.append((source, target))
    return lax.ppermute(values, axes if len(axes) > 1 else axes[0], pairs)


def local(
    fields, spectra, permittivity, phase_start, wall_owner, cap_owner, dir_index, target, aim_mask
):
    n = Sizes(permittivity.shape, dir_index.shape[0], cap_owner.shape[1])
    gz = lax.axis_index("gz")

    def out(*shape, dtype=F32):
        return jax.ShapeDtypeStruct(shape, dtype)

    own_rows = 7 * n.y * n.z
    packed = pl.pallas_call(
        functools.partial(pack_kernel, n),
        name="pack",
        out_shape=[out(own_rows, n.x)]
        + [out(n.y_rows, n.x)] * n.y_kinds
        + [out(n.z_rows, n.x)] * 2
        + [out(n.e_rows, n.x)] * (2 * n.y_kinds),
        in_specs=[VMEM] * 2,
        out_specs=[VMEM] * (3 + 3 * n.y_kinds),
    )(fields, permittivity)
    own, y_send = packed[0], packed[1 : 1 + n.y_kinds]
    z_send, e_send = packed[1 + n.y_kinds : 3 + n.y_kinds], packed[3 + n.y_kinds :]
    y_got = [
        exchange(v, ("dev",), lambda d, k=k: (partner(k, d, n.dev),)) for k, v in enumerate(y_send)
    ]
    e_got = [
        exchange(
            v,
            ("gz", "dev"),
            lambda g, d, k=k: (partner(k % 2, g, n.gz), partner(k // 2, d, n.dev)),
        )
        for k, v in enumerate(e_send)
    ]
    z_got = [
        exchange(v, ("gz",), lambda g, k=k: (partner(k, g, n.gz),)) for k, v in enumerate(z_send)
    ]
    other = exchange(own, ("xy",), lambda x: (x ^ 1,))
    halo = jnp.concatenate([*y_got, *z_got, *e_got])
    far_halo = exchange(halo, ("xy",), lambda x: (x ^ 1,))

    table_rows, v_rows = 2 * n.x + 2 * n.z, 8 * n.y * 8
    high, rest, v, place = pl.pallas_call(
        functools.partial(table_kernel, n),
        name="tables",
        out_shape=[
            out(table_rows, n.dirs, dtype=BF16),
            out(table_rows, n.dirs, dtype=BF16),
            out(v_rows, n.dirs),
            out(n.caps, dtype=jnp.int32),
        ],
        in_specs=[VMEM, SMEM],
        out_specs=[VMEM] * 3 + [SMEM],
        scratch_shapes=[pltpu.SMEM((n.gz,), jnp.int32)],
        compiler_params=pltpu.CompilerParams(vmem_limit_bytes=24 << 20),
    )(dir_index.reshape(n.tiles, LANES), cap_owner)

    block = tuple(permittivity.shape)
    fields_out, spectra_out, far, chunk = pl.pallas_call(
        functools.partial(main_kernel, n),
        name="window",
        out_shape=[
            out(6, *block),
            out(12, *block),
            out(n.far_rows, LANES),
            out(n.gz * n.chunk, LANES),
        ],
        in_specs=[VMEM] * 5 + [SMEM] * 3 + [VMEM] * 3,
        out_specs=[VMEM] * 4,
        scratch_shapes=[
            pltpu.VMEM((7, n.rows, n.z + 8, n.nx), F32),
            pltpu.VMEM((n.caps, LANES), F32),
        ],
        compiler_params=pltpu.CompilerParams(vmem_limit_bytes=24 << 20),
    )(own, other, halo, far_halo, spectra, phase_start, wall_owner, place, high, rest, v)

    for axis in ("xy", "dev"):
        size = lax.axis_size(axis)
        got = [exchange(far, (axis,), lambda i, k=k: (i ^ k,)) for k in range(1, size)]
        for term in got:
            far = far + term
    payload = [
        jnp.concatenate([far, lax.dynamic_slice_in_dim(chunk, (gz ^ k) * n.chunk, n.chunk)])
        for k in range(n.gz)
    ]
    got = [exchange(payload[k], ("gz",), lambda g, k=k: (g ^ k,)) for k in range(1, n.gz)]
    gathered = jnp.concatenate([payload[0], *got])

    intensity_all, owned, adjoint = pl.pallas_call(
        functools.partial(adjoint_kernel, n),
        name="adjoint",
        out_shape=[
            out(n.tiles, LANES),
            out(n.walls + 2 * n.share, LANES),
            out(n.walls + n.caps, LANES),
        ],
        in_specs=[VMEM] * 6,
        out_specs=[VMEM] * 3,
        compiler_params=pltpu.CompilerParams(vmem_limit_bytes=24 << 20),
    )(gathered, target.reshape(n.tiles, LANES), aim_mask.reshape(n.tiles, LANES), high, rest, v)
    joined = (gz * n.dev + lax.axis_index("dev")) * n.xy + lax.axis_index("xy")
    share = n.dirs // (n.gz * n.dev * n.xy)
    intensity = lax.dynamic_slice_in_dim(intensity_all.reshape(n.dirs), joined * share, share)
    return fields_out, spectra_out, owned[None, None, None], intensity, adjoint[None, None, None]


def solution(mesh):
    placed = (
        P("groups", "dev", "gz", "xy"),
        P("groups", "dev", "gz", "xy"),
        P(("groups", "dev"), "gz", "xy"),
        P("groups"),
        P("gz", None),
        P(),
        P(),
        P("groups"),
        P("groups"),
    )
    return jax.shard_map(
        local,
        mesh=mesh,
        in_specs=placed,
        out_specs=(
            P("groups", "dev", "gz", "xy"),
            P("groups", "dev", "gz", "xy"),
            P(("groups", "gz"), "dev", "xy", None, None),
            P(("groups", "gz", "dev", "xy")),
            P(("groups", "gz"), "dev", "xy", None, None),
        ),
        check_vma=False,
    )
```

```python
import functools
import math

import jax
import jax.numpy as jnp
from jax import lax
from jax.experimental import pallas as pl
from jax.experimental.pallas import tpu as pltpu
from jax.sharding import PartitionSpec as P

PATCH = 16
XB = 8
ZB = 4
STEPS = 3
THETAS = 64
COURANT = 0.5
ANGULAR_STEP = 0.3
WAVE_NUMBER = 0.6
CURRENT_SIGNS = (-1.0, 1.0, 1.0, -1.0)
X_PICKS = (5, 4, 2, 1)
Z_PICKS = (4, 3, 1, 0)
LANES = 128
HALO = STEPS
F32 = jnp.float32
BF16 = jnp.bfloat16
VMEM = pl.BlockSpec(memory_space=pltpu.VMEM)
SMEM = pl.BlockSpec(memory_space=pltpu.SMEM)


def up8(rows):
    return -(-rows // 8) * 8


def sincos(angle):
    turns = jnp.floor(angle * (2.0 / math.pi) + 0.5)
    r = angle - turns * 1.5703125
    r = r - turns * 4.837512969970703125e-4
    r = r - turns * 7.54978995489188e-8
    r2 = r * r
    s = r + r * r2 * (-1.6666654611e-1 + r2 * (8.3321608736e-3 + r2 * -1.9515295891e-4))
    c = 1.0 - 0.5 * r2 + r2 * r2 * (
        4.166664568298827e-2 + r2 * (-1.388731625493765e-3 + r2 * 2.443315711809948e-5)
    )
    quarter = turns.astype(jnp.int32)
    odd = (quarter & 1) == 1
    sine = jnp.where(odd, c, s)
    cosine = jnp.where(odd, s, c)
    sine = jnp.where((quarter & 2) == 2, -sine, sine)
    cosine = jnp.where(((quarter + 1) & 2) == 2, -cosine, cosine)
    return sine, cosine


def split(values):
    high = values.astype(BF16)
    return high, (values - high.astype(F32)).astype(BF16)


def rows_iota(shape):
    return lax.broadcasted_iota(jnp.int32, shape, 0)


def lanes_iota(shape):
    return lax.broadcasted_iota(jnp.int32, shape, len(shape) - 1)


class Sizes:
    def __init__(self, block, directions, caps):
        self.gz, self.dev, self.xy = (lax.axis_size(a) for a in ("gz", "dev", "xy"))
        self.y, self.z, self.x = block
        self.both_y = self.dev > 2
        self.rows = self.y + HALO * (2 if self.both_y else 1)
        self.nx, self.ny, self.nz = self.x * self.xy, self.y * self.dev, self.z * self.gz
        self.dirs = directions
        self.tiles = directions // LANES
        self.table_rows = 2 * self.x + 2 * self.z
        self.walls = self.y * self.z // PATCH
        self.caps = caps
        self.share = caps // self.gz
        self.own_dirs = directions // (self.gz * self.dev * self.xy)
        self.chunk = up8(2 + self.share)
        self.far_rows = 4 * self.tiles
        self.norm = 1.0 / math.sqrt(2.0 * (2 * self.ny * self.nz + 2 * self.ny * self.nx))
        self.y_rows = 7 * HALO * self.z
        self.z_rows = up8(7 * self.y * HALO)
        self.e_rows = up8(7 * HALO * HALO)
        y_kinds = 2 if self.both_y else 1
        sizes = [self.y_rows] * y_kinds + [2 * self.z_rows] + [2 * self.e_rows] * y_kinds
        self.starts = [sum(sizes[:i]) for i in range(len(sizes))]
        self.halo_rows = sum(sizes)
        self.y_kinds = y_kinds


def pack_kernel(n, f_ref, eps_ref, own, *y_outs):
    dev_even = lax.axis_index("dev") % 2 == 0
    for c in range(7):
        at = []
        for y in range(n.y):
            value = f_ref[c, y] if c < 6 else COURANT / eps_ref[y]
            own[pl.ds((c * n.y + y) * n.z, n.z), :] = value
            at.append(value)
        for kind in range(n.y_kinds):
            top = dev_even if kind == 0 else jnp.logical_not(dev_even)
            for r in range(HALO):
                value = jnp.where(top, at[n.y - HALO + r], at[r])
                y_outs[kind][pl.ds((c * HALO + r) * n.z, n.z), :] = value


def edge_kernel(n, own_ref, other_ref, z_out, *e_outs):
    xy = lax.axis_index("xy")
    dev_even = lax.axis_index("dev") % 2 == 0
    z_top = lax.axis_index("gz") % 2 == xy % 2
    for half in range(2):
        mine = xy == half

        def at(c, y):
            rows = pl.ds((c * n.y + y) * n.z, n.z)
            value = jnp.where(mine, own_ref[rows, :], other_ref[rows, :])
            return jnp.where(z_top, value[n.z - HALO :], value[:HALO])

        for c in range(7):
            edges = [at(c, y) for y in range(n.y)]
            for y in range(n.y):
                z_out[pl.ds(half * n.z_rows + (c * n.y + y) * HALO, HALO), :] = edges[y]
            for kind in range(n.y_kinds):
                top = dev_even if kind == 0 else jnp.logical_not(dev_even)
                for r in range(HALO):
                    edge = jnp.where(top, edges[n.y - HALO + r], edges[r])
                    e_outs[kind][pl.ds(half * n.e_rows + (c * HALO + r) * HALO, HALO), :] = edge


def table_kernel(
    n, dir_ref, owner_ref, wall_owner_ref, phase_ref, hi_lo_ref, v_ref, place_ref, turn_ref, count_ref
):
    gz, dev, xy = (lax.axis_index(a) for a in ("gz", "dev", "xy"))
    hi_ref, lo_ref = halves(n, hi_lo_ref)
    index = dir_ref[...]
    bits = THETAS.bit_length() - 1
    polar = (index >> bits).astype(F32)
    azimuth = (index & (THETAS - 1)).astype(F32)
    sin_t, cos_t = sincos(math.pi * (polar + 0.5) / THETAS)
    sin_f, cos_f = sincos(2.0 * math.pi * azimuth / THETAS)
    kx = WAVE_NUMBER * (sin_t * cos_f)
    ky = WAVE_NUMBER * (sin_t * sin_f)
    kz = WAVE_NUMBER * cos_t
    theta = (cos_t * cos_f, cos_t * sin_f, -sin_t)
    phi = (-sin_f, cos_f, jnp.zeros_like(sin_f))
    is_end = jnp.logical_or(gz == 0, gz == n.gz - 1)
    cap_scale = jnp.where(is_end, n.norm, 0.0).astype(F32)
    x_first = (xy * n.x).astype(F32) - (n.nx - 1) / 2.0
    y_first = (dev * n.y).astype(F32) - (n.ny - 1) / 2.0
    z_first = (gz * n.z).astype(F32) - (n.nz - 1) / 2.0
    x_wall = x_first + jnp.where(xy == 0, XB, n.x - 1 - XB).astype(F32)
    z_cap = z_first + jnp.where(gz == 0, ZB, n.z - 1 - ZB).astype(F32)
    row8 = rows_iota((8, LANES))
    row16 = rows_iota((16, LANES))
    fine_x = row8.astype(F32)
    low = row8 < 4
    comp = row8 & 3

    def weights(rows):
        picked = jnp.where(comp == 2, rows[2], rows[3])
        return jnp.where(comp == 0, rows[0], jnp.where(comp == 1, rows[1], picked))

    for t in range(n.tiles):
        lanes = slice(t * LANES, (t + 1) * LANES)
        a, b, c = (v[t : t + 1, :] for v in (kx, ky, kz))
        th = [v[t : t + 1, :] for v in theta]
        ph = [v[t : t + 1, :] for v in phi]
        sf, cf = sincos(a * fine_x)
        for pair in range(n.x // 16):
            if pair % 8 == 0:
                base_x = x_first + 8.0 * 16.0 * (pair // 8)
                coarse_s, coarse_c = sincos(a * (row16.astype(F32) * 8.0 + base_x))
            cosine, sine = [], []
            for h in (2 * (pair % 8), 2 * (pair % 8) + 1):
                cc, cs = coarse_c[h : h + 1, :], coarse_s[h : h + 1, :]
                cosine.append(cc * cf - cs * sf)
                sine.append(cs * cf + cc * sf)
            for part, rows in ((0, cosine), (n.x, sine)):
                high, rest = split(jnp.concatenate(rows, axis=0))
                hi_ref[part + pair * 16 : part + pair * 16 + 16, lanes] = high
                lo_ref[part + pair * 16 : part + pair * 16 + 16, lanes] = rest
        zs, zc = sincos(c * (row16.astype(F32) + z_first))
        for part, rows in ((2 * n.x, zc), (2 * n.x + n.z, zs)):
            high, rest = split(rows)
            hi_ref[part : part + 16, lanes] = high
            lo_ref[part : part + 16, lanes] = rest
        y_of = comp.astype(F32) + y_first
        base_s, base_c = sincos(b * y_of + jnp.where(low, c * z_cap, a * x_wall))
        for face in range(2):
            i, j = ((0, 1), (1, 2))[face]
            scale = cap_scale if face == 0 else n.norm
            w_theta = weights([-th[i], -th[j], -ph[i], -ph[j]]) * scale
            w_phi = weights([-ph[i], -ph[j], th[i], th[j]]) * scale
            for y in range(n.y):
                r = face * 4 + y
                bc, bs = base_c[r : r + 1, :], base_s[r : r + 1, :]
                factor = jnp.where(low, bc, -bs)
                for kind, value in enumerate((factor * w_theta, factor * w_phi)):
                    at = ((face * 2 + kind) * n.y + y) * 8
                    v_ref[at : at + 8, lanes] = value
    for o in range(n.gz):
        count_ref[o] = 0
    which = jnp.where(gz == 0, 0, 1)

    def place(q, carry):
        owner = owner_ref[which, q]
        rank = count_ref[owner]
        count_ref[owner] = rank + 1
        place_ref[q] = owner * n.chunk + 2 + rank
        return carry

    lax.fori_loop(0, n.caps, place, 0)
    for j in range(n.walls):
        place_ref[n.caps + j] = wall_owner_ref[0, j]
    step_of = (row8 // 2).astype(F32)
    part_of = jnp.where((row8 & 1) == 0, 0.5, 1.0)
    sines, cosines = sincos(phase_ref[0] + ANGULAR_STEP * (step_of + part_of))
    turn_ref[0:8, :] = cosines
    turn_ref[8:16, :] = sines


def halves(n, hi_lo_ref):
    return hi_lo_ref.at[0 : n.table_rows], hi_lo_ref.at[n.table_rows : 2 * n.table_rows]


def block_transpose(values):
    row, block = rows_iota((8, LANES)), lanes_iota((8, LANES)) // PATCH
    for bit in (1, 2, 4):
        wide = PATCH * bit
        ahead = pltpu.roll(pltpu.roll(values, 8 - bit, 0), wide, 1)
        behind = pltpu.roll(pltpu.roll(values, bit, 0), LANES - wide, 1)
        row_bit, block_bit = (row & bit) != 0, (block & bit) != 0
        moved = jnp.where(row_bit, behind, ahead)
        values = jnp.where(row_bit == block_bit, values, moved)
    return values


def turn(values):
    swapped = pltpu.roll(values, 4, 0)
    return jnp.where(rows_iota(values.shape) < 4, -swapped, swapped)


def main_kernel(
    n, own_ref, other_ref, halo_ref, far_halo_ref, spectra_hbm, place_ref, turn_ref, hi_lo_ref, v_ref,
    fields_hbm, spectra_out_hbm, far_out, chunk_out, a_ref, m_ref, fields_out, spectra_out, sems,
):
    hi_ref, lo_ref = halves(n, hi_lo_ref)
    spectra_in = pltpu.make_async_copy(spectra_hbm, spectra_out, sems.at[0])
    spectra_in.start()
    gz, dev, xy = (lax.axis_index(a) for a in ("gz", "dev", "xy"))
    gz_even, dev_even = gz % 2 == 0, dev % 2 == 0
    deep = n.z + 8
    lo_ok, hi_ok = gz > 0, gz < n.gz - 1
    if n.both_y:
        y_own = HALO
        y_slots = (
            (0, jnp.logical_not(dev_even), dev > 0),
            (HALO + n.y, dev_even, dev < n.dev - 1),
        )
    else:
        y_own = jnp.where(dev_even, 0, HALO)
        y_slots = ((jnp.where(dev_even, n.y, 0), None, None),)
    pad = jnp.zeros((8 - 2 * HALO, LANES), F32)
    near_is_high = gz % 2 == xy % 2

    def choose(ref, starts, use_first, length):
        if use_first is None:
            return ref[pl.ds(starts[0], length), :]
        return jnp.where(
            use_first, ref[pl.ds(starts[0], length), :], ref[pl.ds(starts[1], length), :]
        )

    def rim(near, far):
        high = jnp.where(near_is_high, near, far)
        low = jnp.where(near_is_high, far, near)
        return jnp.concatenate(
            [jnp.where(hi_ok, high, 0.0), pad, jnp.where(lo_ok, low, 0.0)], axis=0
        )

    kinds = n.y_kinds
    both = (halo_ref, far_halo_ref)
    for half, (block, halo) in enumerate(((own_ref, halo_ref), (other_ref, far_halo_ref))):
        at_x = xy if half == 0 else 1 - xy
        lanes = pl.ds(pl.multiple_of(at_x * n.x, n.x), n.x)
        for c in range(7):
            for y in range(n.y):
                a_ref[c, y_own + y, 0 : n.z, lanes] = block[pl.ds((c * n.y + y) * n.z, n.z), :]
            for start, use_first, ok in y_slots:
                for r in range(HALO):
                    at = (c * HALO + r) * n.z
                    body = choose(halo, [n.starts[k] + at for k in range(kinds)], use_first, n.z)
                    if ok is not None:
                        body = jnp.where(ok, body, 0.0)
                    a_ref[c, start + r, 0 : n.z, lanes] = body
    for half in range(2):
        lanes = slice(half * n.x, (half + 1) * n.x)
        for c in range(7):
            for y in range(n.y):
                at = n.starts[kinds] + half * n.z_rows + (c * n.y + y) * HALO
                a_ref[c, y_own + y, n.z : deep, lanes] = rim(*(ref[pl.ds(at, HALO), :] for ref in both))
            for start, use_first, ok in y_slots:
                for r in range(HALO):
                    at = half * n.e_rows + (c * HALO + r) * HALO
                    starts = [n.starts[kinds + 1 + k] + at for k in range(kinds)]
                    edge = rim(*(choose(ref, starts, use_first, HALO) for ref in both))
                    if ok is not None:
                        edge = jnp.where(ok, edge, 0.0)
                    a_ref[c, start + r, n.z : deep, lanes] = edge

    shape = (deep, n.nx)
    z_row, x_lane = rows_iota(shape), lanes_iota(shape)
    keep = jnp.where(z_row < n.z + HALO, COURANT, jnp.where(lo_ok & (z_row >= deep - HALO), COURANT, 0.0))
    keep = keep.astype(F32)
    last_x, first_x = x_lane == n.nx - 1, x_lane == 0

    def z_next(v):
        return pltpu.roll(v, deep - 1, 0)

    def z_before(v):
        return pltpu.roll(v, 1, 0)

    def x_next(v):
        return jnp.where(last_x, 0.0, pltpu.roll(v, n.nx - 1, 1))

    def x_before(v):
        return jnp.where(first_x, 0.0, pltpu.roll(v, 1, 1))

    own_lanes = pl.ds(pl.multiple_of(xy * n.x, n.x), n.x)
    for step in range(STEPS):
        for y in range(n.rows):
            ex, ey, ez = (a_ref[c, y] for c in range(3))
            if y + 1 < n.rows:
                ex_y, ez_y = a_ref[0, y + 1] - ex, a_ref[2, y + 1] - ez
            else:
                ex_y, ez_y = -ex, -ez
            rate = keep
            if n.both_y and y < HALO:
                rate = jnp.where(dev == 0, 0.0, keep)
            a_ref[3, y] = a_ref[3, y] - rate * (ez_y - (z_next(ey) - ey))
            a_ref[4, y] = a_ref[4, y] - rate * ((z_next(ex) - ex) - (x_next(ez) - ez))
            a_ref[5, y] = a_ref[5, y] - rate * ((x_next(ey) - ey) - ex_y)
        for y in range(n.rows):
            hx, hy, hz = (a_ref[c, y] for c in range(3, 6))
            rate = a_ref[6, y]
            if y > 0:
                hx_y, hz_y = hx - a_ref[3, y - 1], hz - a_ref[5, y - 1]
            else:
                hx_y, hz_y = hx, hz
            a_ref[0, y] = a_ref[0, y] + rate * (hz_y - (hy - z_before(hy)))
            a_ref[1, y] = a_ref[1, y] + rate * ((hx - z_before(hx)) - (hz - x_before(hz)))
            a_ref[2, y] = a_ref[2, y] + rate * ((hy - x_before(hy)) - hx_y)
        if step == 0:
            spectra_in.wait()
        for c in range(6):
            row = 2 * step + (1 if c < 3 else 0)
            cosine, sine = turn_ref[row : row + 1, :], turn_ref[8 + row : 9 + row, :]
            for y in range(n.y):
                value = a_ref[c, y_own + y, 0 : n.z, own_lanes]
                spectra_out[c, y] = spectra_out[c, y] + value * cosine
                spectra_out[6 + c, y] = spectra_out[6 + c, y] - value * sine
                if step == STEPS - 1:
                    fields_out[c, y] = value

    copies = (
        pltpu.make_async_copy(fields_out, fields_hbm, sems.at[1]),
        pltpu.make_async_copy(spectra_out, spectra_out_hbm, sems.at[2]),
    )
    for copy in copies:
        copy.start()
    facing_x = jnp.where(xy == 0, -1.0, 1.0).astype(F32)
    facing_z = jnp.where(gz == 0, -1.0, 1.0).astype(F32)
    row8, lane = rows_iota((8, LANES)), lanes_iota((8, LANES))
    sign = jnp.where(((row8 & 3) == 0) | ((row8 & 3) == 3), -1.0, 1.0).astype(F32)
    own_block = lane // PATCH == row8
    block_sign = jnp.sum(jnp.where(own_block, sign, 0.0), axis=0, keepdims=True)
    cap_left, cap_right, wall_left = [], [], []
    chunk_out[...] = jnp.zeros_like(chunk_out)
    for y in range(n.y):
        plane = [
            jnp.where(gz == 0, spectra_out[p, y, ZB : ZB + 1, :], spectra_out[p, y, n.z - 1 - ZB : n.z - ZB, :])
            for p in [k + 6 * im for im in range(2) for k in Z_PICKS]
        ]
        current = jnp.concatenate(plane, axis=0) * (sign * facing_z)
        cap_left.append(current)
        cap_right.append(turn(current))
        m_ref[y * 8 : y * 8 + 8, :] = block_transpose(current)
        stack = jnp.concatenate(
            [spectra_out[k + 6 * im, y] for im in range(2) for k in X_PICKS], axis=0
        )
        across = stack.T
        record = jnp.where(xy == 0, across[XB : XB + 1, :], across[n.x - 1 - XB : n.x - XB, :])
        record = record * (block_sign * facing_x)
        for o in range(n.gz):
            mine = place_ref[n.caps + y] == o
            at = o * n.chunk
            chunk_out[at : at + 1, :] += jnp.where(mine, record, 0.0)
            chunk_out[at + 1 : at + 2, :] += jnp.where(mine, 1.0, 0.0).astype(F32)
        spread = jnp.where(own_block, record, 0.0)
        for wide in (16, 32, 64):
            spread = spread + pltpu.roll(spread, wide, 1)
        wall_left.append(jnp.where(lane < n.z, spread, turn(spread))[:, : 2 * n.z])
    for q in range(n.caps):
        chunk_out[pl.ds(place_ref[q], 1), :] = m_ref[q : q + 1, :]
    cap = jnp.concatenate(
        [jnp.concatenate(cap_left, axis=0), jnp.concatenate(cap_right, axis=0)], axis=1
    )
    wall = jnp.concatenate(wall_left, axis=0)
    dot = functools.partial(jnp.dot, preferred_element_type=F32)
    wide = min(512, n.dirs)
    for first in range(0, n.dirs, wide):
        sums = []
        for left, rows in ((cap, slice(0, 2 * n.x)), (wall, slice(2 * n.x, 2 * n.x + 2 * n.z))):
            left_hi, left_lo = split(left)
            high, rest = hi_ref[rows, first : first + wide], lo_ref[rows, first : first + wide]
            sums.append(dot(left_hi, high) + (dot(left_lo, high) + dot(left_hi, rest)))
        for t in range(wide // LANES):
            lanes = slice(first + t * LANES, first + (t + 1) * LANES)
            tile = first // LANES + t
            totals = [None] * 4
            for face in range(2):
                for y in range(n.y):
                    rows = sums[face][y * 8 : y * 8 + 8, t * LANES : (t + 1) * LANES]
                    turned = -turn(rows)
                    for kind in range(4):
                        at = ((face * 2 + kind % 2) * n.y + y) * 8
                        term = v_ref[at : at + 8, lanes] * (rows if kind < 2 else turned)
                        totals[kind] = term if totals[kind] is None else totals[kind] + term
            for kind, total in enumerate(totals):
                at = kind * n.tiles + tile
                far_out[at : at + 1, :] = jnp.sum(total, axis=0, keepdims=True)
    for copy in copies:
        copy.wait()


def adjoint_kernel(
    n, far_ref, target_ref, mask_ref, hi_lo_ref, v_ref, intensity_out, owned_out, adjoint_out, all_ref
):
    hi_ref, lo_ref = halves(n, hi_lo_ref)
    gz, dev, xy = (lax.axis_index(a) for a in ("gz", "dev", "xy"))
    block = n.far_rows + n.chunk
    parts = []
    for kind in range(4):
        total = None
        for k in range(n.gz):
            at = k * block + kind * n.tiles
            term = far_ref[at : at + n.tiles, :]
            total = term if total is None else total + term
        parts.append(total)
    theta_re, phi_re, theta_im, phi_im = parts
    intensity = theta_re * theta_re + theta_im * theta_im + phi_re * phi_re + phi_im * phi_im
    if n.own_dirs % LANES == 0:
        all_ref[...] = intensity
        first = ((gz * n.dev + dev) * n.xy + xy) * (n.own_dirs // LANES)
        intensity_out[...] = all_ref[pl.ds(first, n.own_dirs // LANES), :]
    else:
        intensity_out[...] = intensity
    slope = 2.0 * (mask_ref[...].astype(F32) * (intensity - target_ref[...]))
    slopes = [slope * part for part in parts]

    faces = [[], []]
    for face in range(2):
        for t in range(n.tiles):
            lanes = slice(t * LANES, (t + 1) * LANES)
            rows = []
            for y in range(n.y):
                at = (face * 2 * n.y + y) * 8
                one, two = v_ref[at : at + 8, lanes], v_ref[at + n.y * 8 : at + n.y * 8 + 8, lanes]
                even, odd = (
                    one * slopes[k][t : t + 1, :] + two * slopes[k + 1][t : t + 1, :] for k in (0, 2)
                )
                rows.append(even + turn(odd))
            faces[face].append(jnp.concatenate(rows, axis=0))
    dot = functools.partial(
        lax.dot_general,
        dimension_numbers=(((1,), (1,)), ((), ())),
        preferred_element_type=F32,
    )
    sums = []
    for face, rows in ((0, slice(0, 2 * n.x)), (1, slice(2 * n.x, 2 * n.x + 2 * n.z))):
        left_hi, left_lo = split(jnp.concatenate(faces[face], axis=1))
        high, rest = hi_ref[rows, :], lo_ref[rows, :]
        sums.append(dot(left_hi, high) + (dot(left_lo, high) + dot(left_hi, rest)))
    cap, wall = sums
    row8, lane = rows_iota((8, LANES)), lanes_iota((8, LANES))
    own_block = lane // PATCH == row8
    for y in range(n.y):
        at = slice(y * 8, y * 8 + 8)
        gradient = cap[at, : n.x] - turn(cap[at, n.x :])
        adjoint_out[n.walls + y * 8 : n.walls + y * 8 + 8, 0, :] = block_transpose(gradient)
        gradient = wall[at, : n.z] - turn(wall[at, n.z :])
        spread = jnp.concatenate([gradient] * (LANES // n.z), axis=1)
        adjoint_out[y, :, :] = jnp.sum(
            jnp.where(own_block, spread, 0.0), axis=0, keepdims=True
        )
    walls = [jnp.zeros((1, LANES), F32) for _ in range(n.walls)]
    rank = jnp.zeros((1, LANES), F32)
    for s in range(n.gz):
        at = pl.multiple_of((gz ^ s) * block + n.far_rows, 8)
        rows = far_ref[pl.ds(at, 8), :]
        record, flag = rows[0:1, :], rows[1:2, :] > 0.5
        for r in range(n.walls):
            walls[r] = jnp.where(flag & (rank == float(r)), record, walls[r])
        rank = rank + rows[1:2, :]
    for r in range(n.walls):
        owned_out[r, :, :] = walls[r]
    for cap_at, s in enumerate((0, n.gz - 1)):
        at = pl.multiple_of((gz ^ s) * block + n.far_rows, 8)
        rows = far_ref[pl.ds(at, n.chunk), :]
        owned_out[n.walls + cap_at * n.share : n.walls + (cap_at + 1) * n.share, 0, :] = rows[2 : 2 + n.share, :]


def partner(kind, i, n):
    up = (i % 2 == 0) == (kind == 0)
    return (i + 1) % n if up else (i - 1) % n


def exchange(values, axes, image):
    sizes = [lax.axis_size(a) for a in axes]
    pairs = []
    for source in range(math.prod(sizes)):
        rest, where = source, []
        for size in reversed(sizes):
            where.insert(0, rest % size)
            rest //= size
        target = 0
        for size, at in zip(sizes, image(*where)):
            target = target * size + at
        pairs.append((source, target))
    return lax.ppermute(values, axes if len(axes) > 1 else axes[0], pairs)


def local(
    fields, spectra, permittivity, phase_start, wall_owner, cap_owner, dir_index, target, aim_mask
):
    n = Sizes(permittivity.shape, dir_index.shape[0], cap_owner.shape[1])
    gz = lax.axis_index("gz")

    def out(*shape, dtype=F32):
        return jax.ShapeDtypeStruct(shape, dtype)

    def params(mebibytes):
        return pltpu.CompilerParams(vmem_limit_bytes=mebibytes << 20)

    own, *y_send = pl.pallas_call(
        functools.partial(pack_kernel, n),
        name="pack",
        out_shape=[out(7 * n.y * n.z, n.x)] + [out(n.y_rows, n.x)] * n.y_kinds,
        in_specs=[VMEM] * 2,
        out_specs=[VMEM] * (1 + n.y_kinds),
        compiler_params=params(4),
    )(fields, permittivity)
    y_got = [
        exchange(v, ("dev",), lambda d, k=k: (partner(k, d, n.dev),)) for k, v in enumerate(y_send)
    ]
    other = exchange(own, ("xy",), lambda x: (x ^ 1,))
    z_send, *e_send = pl.pallas_call(
        functools.partial(edge_kernel, n),
        name="edges",
        out_shape=[out(2 * n.z_rows, n.x)] + [out(2 * n.e_rows, n.x)] * n.y_kinds,
        in_specs=[VMEM] * 2,
        out_specs=[VMEM] * (1 + n.y_kinds),
        compiler_params=params(4),
    )(own, other)
    z_got = exchange(z_send, ("gz", "xy"), lambda g, x: (partner(x, g, n.gz), x))
    e_got = [
        exchange(
            v,
            ("gz", "dev", "xy"),
            lambda g, d, x, k=k: (partner(x, g, n.gz), partner(k, d, n.dev), x),
        )
        for k, v in enumerate(e_send)
    ]

    table, v, place, turns = pl.pallas_call(
        functools.partial(table_kernel, n),
        name="tables",
        out_shape=[
            out(2 * n.table_rows, n.dirs, dtype=BF16),
            out(4 * n.y * 8, n.dirs),
            out(n.caps + n.walls, dtype=jnp.int32),
            out(16, LANES),
        ],
        in_specs=[VMEM] + [SMEM] * 3,
        out_specs=[VMEM] * 2 + [SMEM, VMEM],
        scratch_shapes=[pltpu.SMEM((n.gz,), jnp.int32)],
        compiler_params=params(8),
        cost_estimate=pl.CostEstimate(flops=1 << 33, bytes_accessed=16 << 20, transcendentals=0),
    )(dir_index.reshape(n.tiles, LANES), cap_owner, wall_owner, phase_start)
    (*y_got, z_got, turns), e_got = lax.optimization_barrier(((*y_got, z_got, turns), e_got))
    halo = jnp.concatenate([*y_got, z_got, *e_got])
    far_halo = exchange(halo, ("xy",), lambda x: (x ^ 1,))

    block = tuple(permittivity.shape)
    anywhere = pl.BlockSpec(memory_space=pl.ANY)
    fields_out, spectra_out, far, chunk = pl.pallas_call(
        functools.partial(main_kernel, n),
        name="window",
        out_shape=[
            out(6, *block),
            out(12, *block),
            out(n.far_rows, LANES),
            out(n.gz * n.chunk, LANES),
        ],
        in_specs=[VMEM] * 4 + [anywhere, SMEM] + [VMEM] * 3,
        out_specs=[anywhere] * 2 + [VMEM] * 2,
        scratch_shapes=[
            pltpu.VMEM((7, n.rows, n.z + 8, n.nx), F32),
            pltpu.VMEM((n.caps, LANES), F32),
            pltpu.VMEM((6, *block), F32),
            pltpu.VMEM((12, *block), F32),
            pltpu.SemaphoreType.DMA((3,)),
        ],
        compiler_params=params(12),
    )(own, other, halo, far_halo, spectra, place, turns, table, v)

    for axis in ("xy", "dev"):
        size = lax.axis_size(axis)
        got = [exchange(far, (axis,), lambda i, k=k: (i ^ k,)) for k in range(1, size)]
        for term in got:
            far = far + term
    payload = [
        jnp.concatenate([far, lax.dynamic_slice_in_dim(chunk, (gz ^ k) * n.chunk, n.chunk)])
        for k in range(n.gz)
    ]
    got = [exchange(payload[k], ("gz",), lambda g, k=k: (g ^ k,)) for k in range(1, n.gz)]
    gathered = jnp.concatenate([payload[0], *got])

    sliced = n.own_dirs % LANES == 0
    intensity, owned, adjoint = pl.pallas_call(
        functools.partial(adjoint_kernel, n),
        name="adjoint",
        out_shape=[
            out(n.own_dirs // LANES if sliced else n.tiles, LANES),
            out(n.walls + 2 * n.share, 1, LANES),
            out(n.walls + n.caps, 1, LANES),
        ],
        in_specs=[VMEM] * 5,
        out_specs=[VMEM] * 3,
        scratch_shapes=[pltpu.VMEM((n.tiles, LANES), F32)],
        compiler_params=params(8),
    )(gathered, target.reshape(n.tiles, LANES), aim_mask.reshape(n.tiles, LANES), table, v)
    intensity = intensity.reshape(-1)
    if not sliced:
        joined = (gz * n.dev + lax.axis_index("dev")) * n.xy + lax.axis_index("xy")
        intensity = lax.dynamic_slice_in_dim(intensity, joined * n.own_dirs, n.own_dirs)
    shape = (1, 1, 1, -1, LANES)
    return fields_out, spectra_out, owned.reshape(shape), intensity, adjoint.reshape(shape)


def solution(mesh):
    placed = (
        P("groups", "dev", "gz", "xy"),
        P("groups", "dev", "gz", "xy"),
        P(("groups", "dev"), "gz", "xy"),
        P("groups"),
        P("gz", None),
        P(),
        P(),
        P("groups"),
        P("groups"),
    )
    return jax.shard_map(
        local,
        mesh=mesh,
        in_specs=placed,
        out_specs=(
            P("groups", "dev", "gz", "xy"),
            P("groups", "dev", "gz", "xy"),
            P(("groups", "gz"), "dev", "xy", None, None),
            P(("groups", "gz", "dev", "xy")),
            P(("groups", "gz"), "dev", "xy", None, None),
        ),
        check_vma=False,
    )
```

```python
import functools
import math

import jax
import jax.numpy as jnp
from jax import lax
from jax.experimental import pallas as pl
from jax.experimental.pallas import tpu as pltpu
from jax.sharding import PartitionSpec as P

PATCH = 16
XB = 8
ZB = 4
STEPS = 3
THETAS = 64
COURANT = 0.5
ANGULAR_STEP = 0.3
WAVE_NUMBER = 0.6
CURRENT_SIGNS = (-1.0, 1.0, 1.0, -1.0)
X_PICKS = (5, 4, 2, 1)
Z_PICKS = (4, 3, 1, 0)
LANES = 128
HALO = STEPS
F32 = jnp.float32
BF16 = jnp.bfloat16
VMEM = pl.BlockSpec(memory_space=pltpu.VMEM)
SMEM = pl.BlockSpec(memory_space=pltpu.SMEM)
HBM = pl.BlockSpec(memory_space=pltpu.HBM)


def up8(rows):
    return -(-rows // 8) * 8


def sincos(angle):
    turns = jnp.floor(angle * (2.0 / math.pi) + 0.5)
    r = angle - turns * 1.5703125
    r = r - turns * 4.837512969970703125e-4
    r = r - turns * 7.54978995489188e-8
    r2 = r * r
    s = r + r * r2 * (-1.6666654611e-1 + r2 * (8.3321608736e-3 + r2 * -1.9515295891e-4))
    c = 1.0 - 0.5 * r2 + r2 * r2 * (
        4.166664568298827e-2 + r2 * (-1.388731625493765e-3 + r2 * 2.443315711809948e-5)
    )
    quarter = turns.astype(jnp.int32)
    odd = (quarter & 1) == 1
    sine = jnp.where(odd, c, s)
    cosine = jnp.where(odd, s, c)
    sine = jnp.where((quarter & 2) == 2, -sine, sine)
    cosine = jnp.where(((quarter + 1) & 2) == 2, -cosine, cosine)
    return sine, cosine


def split(values):
    high = values.astype(BF16)
    return high, (values - high.astype(F32)).astype(BF16)


def rows_iota(shape):
    return lax.broadcasted_iota(jnp.int32, shape, 0)


def lanes_iota(shape):
    return lax.broadcasted_iota(jnp.int32, shape, len(shape) - 1)


class Sizes:
    def __init__(self, block, directions, caps):
        self.gz, self.dev, self.xy = (lax.axis_size(a) for a in ("gz", "dev", "xy"))
        self.y, self.z, self.x = block
        self.both_y = self.dev > 2
        self.rows = self.y + HALO * (2 if self.both_y else 1)
        self.nx, self.ny, self.nz = self.x * self.xy, self.y * self.dev, self.z * self.gz
        self.dirs = directions
        self.tiles = directions // LANES
        self.table_rows = 2 * self.x + 2 * self.z
        self.walls = self.y * self.z // PATCH
        self.caps = caps
        self.share = caps // self.gz
        self.own_dirs = directions // (self.gz * self.dev * self.xy)
        self.chunk = up8(2 + self.share)
        self.far_rows = 4 * self.tiles
        self.norm = 1.0 / math.sqrt(2.0 * (2 * self.ny * self.nz + 2 * self.ny * self.nx))
        self.y_rows = 7 * HALO * self.z
        self.z_rows = up8(7 * self.y * HALO)
        self.e_rows = up8(7 * HALO * HALO)
        y_kinds = 2 if self.both_y else 1
        sizes = [self.y_rows] * y_kinds + [2 * self.z_rows] + [2 * self.e_rows] * y_kinds
        self.starts = [sum(sizes[:i]) for i in range(len(sizes))]
        self.halo_rows = sum(sizes)
        self.y_kinds = y_kinds


def pack_kernel(n, f_hbm, eps_hbm, own, *rest):
    y_outs, (eps_ref, sems) = rest[: n.y_kinds], rest[n.y_kinds :]
    copies = (
        pltpu.make_async_copy(f_hbm, own.at[0:6], sems.at[0]),
        pltpu.make_async_copy(eps_hbm, eps_ref, sems.at[1]),
    )
    for copy in copies:
        copy.start()
    for copy in copies:
        copy.wait()
    dev_even = lax.axis_index("dev") % 2 == 0
    for y in range(n.y):
        own[6, y] = COURANT / eps_ref[y]
    for c in range(7):
        at = [own[c, y] for y in range(n.y)]
        for kind in range(n.y_kinds):
            top = dev_even if kind == 0 else jnp.logical_not(dev_even)
            for r in range(HALO):
                value = jnp.where(top, at[n.y - HALO + r], at[r])
                y_outs[kind][pl.ds((c * HALO + r) * n.z, n.z), :] = value


def edge_kernel(n, own_ref, other_ref, z_out, *e_outs):
    xy = lax.axis_index("xy")
    dev_even = lax.axis_index("dev") % 2 == 0
    z_top = lax.axis_index("gz") % 2 == xy % 2
    for half in range(2):
        mine = xy == half

        def at(c, y):
            rows = pl.ds((c * n.y + y) * n.z, n.z)
            value = jnp.where(mine, own_ref[rows, :], other_ref[rows, :])
            return jnp.where(z_top, value[n.z - HALO :], value[:HALO])

        for c in range(7):
            edges = [at(c, y) for y in range(n.y)]
            for y in range(n.y):
                z_out[pl.ds(half * n.z_rows + (c * n.y + y) * HALO, HALO), :] = edges[y]
            for kind in range(n.y_kinds):
                top = dev_even if kind == 0 else jnp.logical_not(dev_even)
                for r in range(HALO):
                    edge = jnp.where(top, edges[n.y - HALO + r], edges[r])
                    e_outs[kind][pl.ds(half * n.e_rows + (c * HALO + r) * HALO, HALO), :] = edge


def table_kernel(
    n, dir_hbm, owner_hbm, wall_owner_hbm, phase_hbm, hi_lo_ref, v_ref, place_ref, turn_ref,
    count_ref, dir_ref, owner_ref, wall_owner_ref, phase_ref, sems,
):
    gz, dev, xy = (lax.axis_index(a) for a in ("gz", "dev", "xy"))
    hi_ref, lo_ref = halves(n, hi_lo_ref)
    copies = [
        pltpu.make_async_copy(source, target, sems.at[i])
        for i, (source, target) in enumerate(
            (
                (dir_hbm, dir_ref),
                (owner_hbm, owner_ref),
                (wall_owner_hbm, wall_owner_ref),
                (phase_hbm, phase_ref),
            )
        )
    ]
    for copy in copies:
        copy.start()
    for copy in copies:
        copy.wait()
    index = dir_ref[...]
    bits = THETAS.bit_length() - 1
    polar = (index >> bits).astype(F32)
    azimuth = (index & (THETAS - 1)).astype(F32)
    sin_t, cos_t = sincos(math.pi * (polar + 0.5) / THETAS)
    sin_f, cos_f = sincos(2.0 * math.pi * azimuth / THETAS)
    kx = WAVE_NUMBER * (sin_t * cos_f)
    ky = WAVE_NUMBER * (sin_t * sin_f)
    kz = WAVE_NUMBER * cos_t
    theta = (cos_t * cos_f, cos_t * sin_f, -sin_t)
    phi = (-sin_f, cos_f, jnp.zeros_like(sin_f))
    is_end = jnp.logical_or(gz == 0, gz == n.gz - 1)
    cap_scale = jnp.where(is_end, n.norm, 0.0).astype(F32)
    x_first = (xy * n.x).astype(F32) - (n.nx - 1) / 2.0
    y_first = (dev * n.y).astype(F32) - (n.ny - 1) / 2.0
    z_first = (gz * n.z).astype(F32) - (n.nz - 1) / 2.0
    x_wall = x_first + jnp.where(xy == 0, XB, n.x - 1 - XB).astype(F32)
    z_cap = z_first + jnp.where(gz == 0, ZB, n.z - 1 - ZB).astype(F32)
    row8 = rows_iota((8, LANES))
    row16 = rows_iota((16, LANES))
    fine_x = row8.astype(F32)
    low = row8 < 4
    comp = row8 & 3

    def weights(rows):
        picked = jnp.where(comp == 2, rows[2], rows[3])
        return jnp.where(comp == 0, rows[0], jnp.where(comp == 1, rows[1], picked))

    for t in range(n.tiles):
        lanes = slice(t * LANES, (t + 1) * LANES)
        a, b, c = (v[t : t + 1, :] for v in (kx, ky, kz))
        th = [v[t : t + 1, :] for v in theta]
        ph = [v[t : t + 1, :] for v in phi]
        sf, cf = sincos(a * fine_x)
        for pair in range(n.x // 16):
            if pair % 8 == 0:
                base_x = x_first + 8.0 * 16.0 * (pair // 8)
                coarse_s, coarse_c = sincos(a * (row16.astype(F32) * 8.0 + base_x))
            cosine, sine = [], []
            for h in (2 * (pair % 8), 2 * (pair % 8) + 1):
                cc, cs = coarse_c[h : h + 1, :], coarse_s[h : h + 1, :]
                cosine.append(cc * cf - cs * sf)
                sine.append(cs * cf + cc * sf)
            for part, rows in ((0, cosine), (n.x, sine)):
                high, rest = split(jnp.concatenate(rows, axis=0))
                hi_ref[part + pair * 16 : part + pair * 16 + 16, lanes] = high
                lo_ref[part + pair * 16 : part + pair * 16 + 16, lanes] = rest
        zs, zc = sincos(c * (row16.astype(F32) + z_first))
        for part, rows in ((2 * n.x, zc), (2 * n.x + n.z, zs)):
            high, rest = split(rows)
            hi_ref[part : part + 16, lanes] = high
            lo_ref[part : part + 16, lanes] = rest
        y_of = comp.astype(F32) + y_first
        base_s, base_c = sincos(b * y_of + jnp.where(low, c * z_cap, a * x_wall))
        for face in range(2):
            i, j = ((0, 1), (1, 2))[face]
            scale = cap_scale if face == 0 else n.norm
            w_theta = weights([-th[i], -th[j], -ph[i], -ph[j]]) * scale
            w_phi = weights([-ph[i], -ph[j], th[i], th[j]]) * scale
            for y in range(n.y):
                r = face * 4 + y
                bc, bs = base_c[r : r + 1, :], base_s[r : r + 1, :]
                factor = jnp.where(low, bc, -bs)
                for kind, value in enumerate((factor * w_theta, factor * w_phi)):
                    at = ((face * 2 + kind) * n.y + y) * 8
                    v_ref[at : at + 8, lanes] = value
    for o in range(n.gz):
        count_ref[o] = 0
    which = jnp.where(gz == 0, 0, 1)

    def place(q, carry):
        owner = owner_ref[which, q]
        rank = count_ref[owner]
        count_ref[owner] = rank + 1
        place_ref[q] = owner * n.chunk + 2 + rank
        return carry

    lax.fori_loop(0, n.caps, place, 0)
    for j in range(n.walls):
        place_ref[n.caps + j] = wall_owner_ref[0, j]
    step_of = (row8 // 2).astype(F32)
    part_of = jnp.where((row8 & 1) == 0, 0.5, 1.0)
    sines, cosines = sincos(phase_ref[0] + ANGULAR_STEP * (step_of + part_of))
    turn_ref[0:8, :] = cosines
    turn_ref[8:16, :] = sines


def halves(n, hi_lo_ref):
    return hi_lo_ref.at[0 : n.table_rows], hi_lo_ref.at[n.table_rows : 2 * n.table_rows]


def block_transpose(values):
    row, block = rows_iota((8, LANES)), lanes_iota((8, LANES)) // PATCH
    for bit in (1, 2, 4):
        wide = PATCH * bit
        ahead = pltpu.roll(pltpu.roll(values, 8 - bit, 0), wide, 1)
        behind = pltpu.roll(pltpu.roll(values, bit, 0), LANES - wide, 1)
        row_bit, block_bit = (row & bit) != 0, (block & bit) != 0
        moved = jnp.where(row_bit, behind, ahead)
        values = jnp.where(row_bit == block_bit, values, moved)
    return values


def turn(values):
    swapped = pltpu.roll(values, 4, 0)
    return jnp.where(rows_iota(values.shape) < 4, -swapped, swapped)


def main_kernel(
    n, own_ref, other_ref, halo_ref, far_halo_ref, spectra_hbm, place_ref, turn_ref, hi_lo_ref, v_ref,
    fields_hbm, spectra_out_hbm, far_out, chunk_out, a_ref, m_ref, fields_out, spectra_out, sems,
):
    hi_ref, lo_ref = halves(n, hi_lo_ref)
    spectra_in = pltpu.make_async_copy(spectra_hbm, spectra_out, sems.at[0])
    spectra_in.start()
    gz, dev, xy = (lax.axis_index(a) for a in ("gz", "dev", "xy"))
    gz_even, dev_even = gz % 2 == 0, dev % 2 == 0
    deep = n.z + 8
    lo_ok, hi_ok = gz > 0, gz < n.gz - 1
    if n.both_y:
        y_own = HALO
        y_slots = (
            (0, jnp.logical_not(dev_even), dev > 0),
            (HALO + n.y, dev_even, dev < n.dev - 1),
        )
    else:
        y_own = jnp.where(dev_even, 0, HALO)
        y_slots = ((jnp.where(dev_even, n.y, 0), None, None),)
    pad = jnp.zeros((8 - 2 * HALO, LANES), F32)
    near_is_high = gz % 2 == xy % 2

    def choose(ref, starts, use_first, length):
        if use_first is None:
            return ref[pl.ds(starts[0], length), :]
        return jnp.where(
            use_first, ref[pl.ds(starts[0], length), :], ref[pl.ds(starts[1], length), :]
        )

    def rim(near, far):
        high = jnp.where(near_is_high, near, far)
        low = jnp.where(near_is_high, far, near)
        return jnp.concatenate(
            [jnp.where(hi_ok, high, 0.0), pad, jnp.where(lo_ok, low, 0.0)], axis=0
        )

    kinds = n.y_kinds
    both = (halo_ref, far_halo_ref)
    for half, (block, halo) in enumerate(((own_ref, halo_ref), (other_ref, far_halo_ref))):
        at_x = xy if half == 0 else 1 - xy
        lanes = pl.ds(pl.multiple_of(at_x * n.x, n.x), n.x)
        for c in range(7):
            for y in range(n.y):
                a_ref[c, y_own + y, 0 : n.z, lanes] = block[pl.ds((c * n.y + y) * n.z, n.z), :]
            for start, use_first, ok in y_slots:
                for r in range(HALO):
                    at = (c * HALO + r) * n.z
                    body = choose(halo, [n.starts[k] + at for k in range(kinds)], use_first, n.z)
                    if ok is not None:
                        body = jnp.where(ok, body, 0.0)
                    a_ref[c, start + r, 0 : n.z, lanes] = body
    for half in range(2):
        lanes = slice(half * n.x, (half + 1) * n.x)
        for c in range(7):
            for y in range(n.y):
                at = n.starts[kinds] + half * n.z_rows + (c * n.y + y) * HALO
                a_ref[c, y_own + y, n.z : deep, lanes] = rim(*(ref[pl.ds(at, HALO), :] for ref in both))
            for start, use_first, ok in y_slots:
                for r in range(HALO):
                    at = half * n.e_rows + (c * HALO + r) * HALO
                    starts = [n.starts[kinds + 1 + k] + at for k in range(kinds)]
                    edge = rim(*(choose(ref, starts, use_first, HALO) for ref in both))
                    if ok is not None:
                        edge = jnp.where(ok, edge, 0.0)
                    a_ref[c, start + r, n.z : deep, lanes] = edge

    shape = (deep, n.nx)
    z_row, x_lane = rows_iota(shape), lanes_iota(shape)
    keep = jnp.where(z_row < n.z + HALO, COURANT, jnp.where(lo_ok & (z_row >= deep - HALO), COURANT, 0.0))
    keep = keep.astype(F32)
    last_x, first_x = x_lane == n.nx - 1, x_lane == 0

    def z_next(v):
        return pltpu.roll(v, deep - 1, 0)

    def z_before(v):
        return pltpu.roll(v, 1, 0)

    def x_next(v):
        return jnp.where(last_x, 0.0, pltpu.roll(v, n.nx - 1, 1))

    def x_before(v):
        return jnp.where(first_x, 0.0, pltpu.roll(v, 1, 1))

    own_lanes = pl.ds(pl.multiple_of(xy * n.x, n.x), n.x)
    for step in range(STEPS):
        for y in range(n.rows):
            ex, ey, ez = (a_ref[c, y] for c in range(3))
            if y + 1 < n.rows:
                ex_y, ez_y = a_ref[0, y + 1] - ex, a_ref[2, y + 1] - ez
            else:
                ex_y, ez_y = -ex, -ez
            rate = keep
            if n.both_y and y < HALO:
                rate = jnp.where(dev == 0, 0.0, keep)
            a_ref[3, y] = a_ref[3, y] - rate * (ez_y - (z_next(ey) - ey))
            a_ref[4, y] = a_ref[4, y] - rate * ((z_next(ex) - ex) - (x_next(ez) - ez))
            a_ref[5, y] = a_ref[5, y] - rate * ((x_next(ey) - ey) - ex_y)
        for y in range(n.rows):
            hx, hy, hz = (a_ref[c, y] for c in range(3, 6))
            rate = a_ref[6, y]
            if y > 0:
                hx_y, hz_y = hx - a_ref[3, y - 1], hz - a_ref[5, y - 1]
            else:
                hx_y, hz_y = hx, hz
            a_ref[0, y] = a_ref[0, y] + rate * (hz_y - (hy - z_before(hy)))
            a_ref[1, y] = a_ref[1, y] + rate * ((hx - z_before(hx)) - (hz - x_before(hz)))
            a_ref[2, y] = a_ref[2, y] + rate * ((hy - x_before(hy)) - hx_y)
        if step == 0:
            spectra_in.wait()
        for c in range(6):
            row = 2 * step + (1 if c < 3 else 0)
            cosine, sine = turn_ref[row : row + 1, :], turn_ref[8 + row : 9 + row, :]
            for y in range(n.y):
                value = a_ref[c, y_own + y, 0 : n.z, own_lanes]
                spectra_out[c, y] = spectra_out[c, y] + value * cosine
                spectra_out[6 + c, y] = spectra_out[6 + c, y] - value * sine
                if step == STEPS - 1:
                    fields_out[c, y] = value

    copies = (
        pltpu.make_async_copy(fields_out, fields_hbm, sems.at[1]),
        pltpu.make_async_copy(spectra_out, spectra_out_hbm, sems.at[2]),
    )
    for copy in copies:
        copy.start()
    facing_x = jnp.where(xy == 0, -1.0, 1.0).astype(F32)
    facing_z = jnp.where(gz == 0, -1.0, 1.0).astype(F32)
    row8, lane = rows_iota((8, LANES)), lanes_iota((8, LANES))
    sign = jnp.where(((row8 & 3) == 0) | ((row8 & 3) == 3), -1.0, 1.0).astype(F32)
    own_block = lane // PATCH == row8
    block_sign = jnp.sum(jnp.where(own_block, sign, 0.0), axis=0, keepdims=True)
    cap_left, cap_right, wall_left = [], [], []
    chunk_out[...] = jnp.zeros_like(chunk_out)
    for y in range(n.y):
        plane = [
            jnp.where(gz == 0, spectra_out[p, y, ZB : ZB + 1, :], spectra_out[p, y, n.z - 1 - ZB : n.z - ZB, :])
            for p in [k + 6 * im for im in range(2) for k in Z_PICKS]
        ]
        current = jnp.concatenate(plane, axis=0) * (sign * facing_z)
        cap_left.append(current)
        cap_right.append(turn(current))
        m_ref[y * 8 : y * 8 + 8, :] = block_transpose(current)
        stack = jnp.concatenate(
            [spectra_out[k + 6 * im, y] for im in range(2) for k in X_PICKS], axis=0
        )
        across = stack.T
        record = jnp.where(xy == 0, across[XB : XB + 1, :], across[n.x - 1 - XB : n.x - XB, :])
        record = record * (block_sign * facing_x)
        for o in range(n.gz):
            mine = place_ref[n.caps + y] == o
            at = o * n.chunk
            chunk_out[at : at + 1, :] += jnp.where(mine, record, 0.0)
            chunk_out[at + 1 : at + 2, :] += jnp.where(mine, 1.0, 0.0).astype(F32)
        spread = jnp.where(own_block, record, 0.0)
        for wide in (16, 32, 64):
            spread = spread + pltpu.roll(spread, wide, 1)
        wall_left.append(jnp.where(lane < n.z, spread, turn(spread))[:, : 2 * n.z])
    for q in range(n.caps):
        chunk_out[pl.ds(place_ref[q], 1), :] = m_ref[q : q + 1, :]
    cap = jnp.concatenate(
        [jnp.concatenate(cap_left, axis=0), jnp.concatenate(cap_right, axis=0)], axis=1
    )
    wall = jnp.concatenate(wall_left, axis=0)
    dot = functools.partial(jnp.dot, preferred_element_type=F32)
    wide = min(512, n.dirs)
    for first in range(0, n.dirs, wide):
        sums = []
        for left, rows in ((cap, slice(0, 2 * n.x)), (wall, slice(2 * n.x, 2 * n.x + 2 * n.z))):
            left_hi, left_lo = split(left)
            high, rest = hi_ref[rows, first : first + wide], lo_ref[rows, first : first + wide]
            sums.append(dot(left_hi, high) + (dot(left_lo, high) + dot(left_hi, rest)))
        for t in range(wide // LANES):
            lanes = slice(first + t * LANES, first + (t + 1) * LANES)
            tile = first // LANES + t
            totals = [None] * 4
            for face in range(2):
                for y in range(n.y):
                    rows = sums[face][y * 8 : y * 8 + 8, t * LANES : (t + 1) * LANES]
                    turned = -turn(rows)
                    for kind in range(4):
                        at = ((face * 2 + kind % 2) * n.y + y) * 8
                        term = v_ref[at : at + 8, lanes] * (rows if kind < 2 else turned)
                        totals[kind] = term if totals[kind] is None else totals[kind] + term
            for kind, total in enumerate(totals):
                at = kind * n.tiles + tile
                far_out[at : at + 1, :] = jnp.sum(total, axis=0, keepdims=True)
    for copy in copies:
        copy.wait()


def adjoint_kernel(
    n, far_ref, target_ref, mask_ref, hi_lo_ref, v_ref, intensity_out, owned_out, adjoint_out, all_ref
):
    hi_ref, lo_ref = halves(n, hi_lo_ref)
    gz, dev, xy = (lax.axis_index(a) for a in ("gz", "dev", "xy"))
    block = n.far_rows + n.chunk
    parts = []
    for kind in range(4):
        total = None
        for k in range(n.gz):
            at = k * block + kind * n.tiles
            term = far_ref[at : at + n.tiles, :]
            total = term if total is None else total + term
        parts.append(total)
    theta_re, phi_re, theta_im, phi_im = parts
    intensity = theta_re * theta_re + theta_im * theta_im + phi_re * phi_re + phi_im * phi_im
    if n.own_dirs % LANES == 0:
        all_ref[...] = intensity
        first = ((gz * n.dev + dev) * n.xy + xy) * (n.own_dirs // LANES)
        intensity_out[...] = all_ref[pl.ds(first, n.own_dirs // LANES), :]
    else:
        intensity_out[...] = intensity
    slope = 2.0 * (mask_ref[...].astype(F32) * (intensity - target_ref[...]))
    slopes = [slope * part for part in parts]

    faces = [[], []]
    for face in range(2):
        for t in range(n.tiles):
            lanes = slice(t * LANES, (t + 1) * LANES)
            rows = []
            for y in range(n.y):
                at = (face * 2 * n.y + y) * 8
                one, two = v_ref[at : at + 8, lanes], v_ref[at + n.y * 8 : at + n.y * 8 + 8, lanes]
                even, odd = (
                    one * slopes[k][t : t + 1, :] + two * slopes[k + 1][t : t + 1, :] for k in (0, 2)
                )
                rows.append(even + turn(odd))
            faces[face].append(jnp.concatenate(rows, axis=0))
    dot = functools.partial(
        lax.dot_general,
        dimension_numbers=(((1,), (1,)), ((), ())),
        preferred_element_type=F32,
    )
    sums = []
    for face, rows in ((0, slice(0, 2 * n.x)), (1, slice(2 * n.x, 2 * n.x + 2 * n.z))):
        left_hi, left_lo = split(jnp.concatenate(faces[face], axis=1))
        high, rest = hi_ref[rows, :], lo_ref[rows, :]
        sums.append(dot(left_hi, high) + (dot(left_lo, high) + dot(left_hi, rest)))
    cap, wall = sums
    row8, lane = rows_iota((8, LANES)), lanes_iota((8, LANES))
    own_block = lane // PATCH == row8
    for y in range(n.y):
        at = slice(y * 8, y * 8 + 8)
        gradient = cap[at, : n.x] - turn(cap[at, n.x :])
        adjoint_out[n.walls + y * 8 : n.walls + y * 8 + 8, 0, :] = block_transpose(gradient)
        gradient = wall[at, : n.z] - turn(wall[at, n.z :])
        spread = jnp.concatenate([gradient] * (LANES // n.z), axis=1)
        adjoint_out[y, :, :] = jnp.sum(
            jnp.where(own_block, spread, 0.0), axis=0, keepdims=True
        )
    walls = [jnp.zeros((1, LANES), F32) for _ in range(n.walls)]
    rank = jnp.zeros((1, LANES), F32)
    for s in range(n.gz):
        at = pl.multiple_of((gz ^ s) * block + n.far_rows, 8)
        rows = far_ref[pl.ds(at, 8), :]
        record, flag = rows[0:1, :], rows[1:2, :] > 0.5
        for r in range(n.walls):
            walls[r] = jnp.where(flag & (rank == float(r)), record, walls[r])
        rank = rank + rows[1:2, :]
    for r in range(n.walls):
        owned_out[r, :, :] = walls[r]
    for cap_at, s in enumerate((0, n.gz - 1)):
        at = pl.multiple_of((gz ^ s) * block + n.far_rows, 8)
        rows = far_ref[pl.ds(at, n.chunk), :]
        owned_out[n.walls + cap_at * n.share : n.walls + (cap_at + 1) * n.share, 0, :] = rows[2 : 2 + n.share, :]


def partner(kind, i, n):
    up = (i % 2 == 0) == (kind == 0)
    return (i + 1) % n if up else (i - 1) % n


def exchange(values, axes, image):
    sizes = [lax.axis_size(a) for a in axes]
    pairs = []
    for source in range(math.prod(sizes)):
        rest, where = source, []
        for size in reversed(sizes):
            where.insert(0, rest % size)
            rest //= size
        target = 0
        for size, at in zip(sizes, image(*where)):
            target = target * size + at
        pairs.append((source, target))
    return lax.ppermute(values, axes if len(axes) > 1 else axes[0], pairs)


def local(
    fields, spectra, permittivity, phase_start, wall_owner, cap_owner, dir_index, target, aim_mask
):
    n = Sizes(permittivity.shape, dir_index.shape[0], cap_owner.shape[1])
    gz = lax.axis_index("gz")

    def out(*shape, dtype=F32):
        return jax.ShapeDtypeStruct(shape, dtype)

    def params(mebibytes):
        return pltpu.CompilerParams(vmem_limit_bytes=mebibytes << 20)

    block = tuple(permittivity.shape)
    own, *y_send = pl.pallas_call(
        functools.partial(pack_kernel, n),
        name="pack",
        out_shape=[out(7, *block)] + [out(n.y_rows, n.x)] * n.y_kinds,
        in_specs=[HBM] * 2,
        out_specs=[VMEM] * (1 + n.y_kinds),
        scratch_shapes=[pltpu.VMEM(block, F32), pltpu.SemaphoreType.DMA((2,))],
        compiler_params=params(4),
    )(fields, permittivity)
    own = own.reshape(7 * n.y * n.z, n.x)
    y_got = [
        exchange(v, ("dev",), lambda d, k=k: (partner(k, d, n.dev),)) for k, v in enumerate(y_send)
    ]
    other = exchange(own, ("xy",), lambda x: (x ^ 1,))
    z_send, *e_send = pl.pallas_call(
        functools.partial(edge_kernel, n),
        name="edges",
        out_shape=[out(2 * n.z_rows, n.x)] + [out(2 * n.e_rows, n.x)] * n.y_kinds,
        in_specs=[VMEM] * 2,
        out_specs=[VMEM] * (1 + n.y_kinds),
        compiler_params=params(4),
    )(own, other)
    z_got = exchange(z_send, ("gz", "xy"), lambda g, x: (partner(x, g, n.gz), x))
    e_got = [
        exchange(
            v,
            ("gz", "dev", "xy"),
            lambda g, d, x, k=k: (partner(x, g, n.gz), partner(k, d, n.dev), x),
        )
        for k, v in enumerate(e_send)
    ]

    table, v, place, turns = pl.pallas_call(
        functools.partial(table_kernel, n),
        name="tables",
        out_shape=[
            out(2 * n.table_rows, n.dirs, dtype=BF16),
            out(4 * n.y * 8, n.dirs),
            out(n.caps + n.walls, dtype=jnp.int32),
            out(16, LANES),
        ],
        in_specs=[HBM] * 4,
        out_specs=[VMEM] * 2 + [SMEM, VMEM],
        scratch_shapes=[
            pltpu.SMEM((n.gz,), jnp.int32),
            pltpu.VMEM((n.tiles, LANES), jnp.int32),
            pltpu.SMEM(cap_owner.shape, jnp.int32),
            pltpu.SMEM(wall_owner.shape, jnp.int32),
            pltpu.SMEM(phase_start.shape, F32),
            pltpu.SemaphoreType.DMA((4,)),
        ],
        compiler_params=params(8),
        cost_estimate=pl.CostEstimate(flops=1 << 33, bytes_accessed=16 << 20, transcendentals=0),
    )(dir_index.reshape(n.tiles, LANES), cap_owner, wall_owner, phase_start)
    (*y_got, z_got, turns), e_got = lax.optimization_barrier(((*y_got, z_got, turns), e_got))
    halo = jnp.concatenate([*y_got, z_got, *e_got])
    far_halo = exchange(halo, ("xy",), lambda x: (x ^ 1,))

    anywhere = pl.BlockSpec(memory_space=pl.ANY)
    fields_out, spectra_out, far, chunk = pl.pallas_call(
        functools.partial(main_kernel, n),
        name="window",
        out_shape=[
            out(6, *block),
            out(12, *block),
            out(n.far_rows, LANES),
            out(n.gz * n.chunk, LANES),
        ],
        in_specs=[VMEM] * 4 + [anywhere, SMEM] + [VMEM] * 3,
        out_specs=[anywhere] * 2 + [VMEM] * 2,
        scratch_shapes=[
            pltpu.VMEM((7, n.rows, n.z + 8, n.nx), F32),
            pltpu.VMEM((n.caps, LANES), F32),
            pltpu.VMEM((6, *block), F32),
            pltpu.VMEM((12, *block), F32),
            pltpu.SemaphoreType.DMA((3,)),
        ],
        compiler_params=params(12),
    )(own, other, halo, far_halo, spectra, place, turns, table, v)

    for axis in ("xy", "dev"):
        size = lax.axis_size(axis)
        got = [exchange(far, (axis,), lambda i, k=k: (i ^ k,)) for k in range(1, size)]
        for term in got:
            far = far + term
    payload = [
        jnp.concatenate([far, lax.dynamic_slice_in_dim(chunk, (gz ^ k) * n.chunk, n.chunk)])
        for k in range(n.gz)
    ]
    got = [
        exchange(payload[k], ("gz",), lambda g, k=k: (g ^ k,)) for k in range(n.gz - 1, 0, -1)
    ]
    gathered = jnp.concatenate([payload[0], *reversed(got)])

    sliced = n.own_dirs % LANES == 0
    intensity, owned, adjoint = pl.pallas_call(
        functools.partial(adjoint_kernel, n),
        name="adjoint",
        out_shape=[
            out(n.own_dirs // LANES if sliced else n.tiles, LANES),
            out(n.walls + 2 * n.share, 1, LANES),
            out(n.walls + n.caps, 1, LANES),
        ],
        in_specs=[VMEM] * 5,
        out_specs=[VMEM] * 3,
        scratch_shapes=[pltpu.VMEM((n.tiles, LANES), F32)],
        compiler_params=params(8),
    )(gathered, target.reshape(n.tiles, LANES), aim_mask.reshape(n.tiles, LANES), table, v)
    intensity = intensity.reshape(-1)
    if not sliced:
        joined = (gz * n.dev + lax.axis_index("dev")) * n.xy + lax.axis_index("xy")
        intensity = lax.dynamic_slice_in_dim(intensity, joined * n.own_dirs, n.own_dirs)
    shape = (1, 1, 1, -1, LANES)
    return fields_out, spectra_out, owned.reshape(shape), intensity, adjoint.reshape(shape)


def solution(mesh):
    placed = (
        P("groups", "dev", "gz", "xy"),
        P("groups", "dev", "gz", "xy"),
        P(("groups", "dev"), "gz", "xy"),
        P("groups"),
        P("gz", None),
        P(),
        P(),
        P("groups"),
        P("groups"),
    )
    return jax.shard_map(
        local,
        mesh=mesh,
        in_specs=placed,
        out_specs=(
            P("groups", "dev", "gz", "xy"),
            P("groups", "dev", "gz", "xy"),
            P(("groups", "gz"), "dev", "xy", None, None),
            P(("groups", "gz", "dev", "xy")),
            P(("groups", "gz"), "dev", "xy", None, None),
        ),
        check_vma=False,
    )
```

```python
import functools
import math

import jax
import jax.numpy as jnp
from jax import lax
from jax.experimental import pallas as pl
from jax.experimental.pallas import tpu as pltpu
from jax.sharding import PartitionSpec as P

PATCH = 16
XB = 8
ZB = 4
STEPS = 3
THETAS = 64
COURANT = 0.5
ANGULAR_STEP = 0.3
WAVE_NUMBER = 0.6
CURRENT_SIGNS = (-1.0, 1.0, 1.0, -1.0)
X_PICKS = (5, 4, 2, 1)
Z_PICKS = (4, 3, 1, 0)
LANES = 128
HALO = STEPS
F32 = jnp.float32
BF16 = jnp.bfloat16
VMEM = pl.BlockSpec(memory_space=pltpu.VMEM)
SMEM = pl.BlockSpec(memory_space=pltpu.SMEM)
HBM = pl.BlockSpec(memory_space=pltpu.HBM)


def up8(rows):
    return -(-rows // 8) * 8


def sincos(angle):
    turns = jnp.floor(angle * (2.0 / math.pi) + 0.5)
    r = angle - turns * 1.5703125
    r = r - turns * 4.837512969970703125e-4
    r = r - turns * 7.54978995489188e-8
    r2 = r * r
    s = r + r * r2 * (-1.6666654611e-1 + r2 * (8.3321608736e-3 + r2 * -1.9515295891e-4))
    c = 1.0 - 0.5 * r2 + r2 * r2 * (
        4.166664568298827e-2 + r2 * (-1.388731625493765e-3 + r2 * 2.443315711809948e-5)
    )
    quarter = turns.astype(jnp.int32)
    odd = (quarter & 1) == 1
    sine = jnp.where(odd, c, s)
    cosine = jnp.where(odd, s, c)
    sine = jnp.where((quarter & 2) == 2, -sine, sine)
    cosine = jnp.where(((quarter + 1) & 2) == 2, -cosine, cosine)
    return sine, cosine


def split(values):
    high = values.astype(BF16)
    return high, (values - high.astype(F32)).astype(BF16)


def rows_iota(shape):
    return lax.broadcasted_iota(jnp.int32, shape, 0)


def lanes_iota(shape):
    return lax.broadcasted_iota(jnp.int32, shape, len(shape) - 1)


class Sizes:
    def __init__(self, block, directions, caps):
        self.gz, self.dev, self.xy = (lax.axis_size(a) for a in ("gz", "dev", "xy"))
        self.y, self.z, self.x = block
        self.both_y = self.dev > 2
        self.rows = self.y + HALO * (2 if self.both_y else 1)
        self.nx, self.ny, self.nz = self.x * self.xy, self.y * self.dev, self.z * self.gz
        self.dirs = directions
        self.tiles = directions // LANES
        self.table_rows = 2 * self.x + 2 * self.z
        self.walls = self.y * self.z // PATCH
        self.caps = caps
        self.share = caps // self.gz
        self.own_dirs = directions // (self.gz * self.dev * self.xy)
        self.chunk = up8(2 + self.share)
        self.far_rows = 4 * self.tiles
        self.norm = 1.0 / math.sqrt(2.0 * (2 * self.ny * self.nz + 2 * self.ny * self.nx))
        self.y_rows = 7 * HALO * self.z
        self.z_rows = up8(7 * self.y * HALO)
        self.e_rows = up8(7 * HALO * HALO)
        y_kinds = 2 if self.both_y else 1
        sizes = [self.y_rows] * y_kinds + [2 * self.z_rows] + [2 * self.e_rows] * y_kinds
        self.starts = [sum(sizes[:i]) for i in range(len(sizes))]
        self.halo_rows = sum(sizes)
        self.y_kinds = y_kinds


def pack_kernel(n, f_hbm, eps_hbm, own, *rest):
    y_outs, (eps_ref, sems) = rest[: n.y_kinds], rest[n.y_kinds :]
    copies = (
        pltpu.make_async_copy(f_hbm, own.at[0:6], sems.at[0]),
        pltpu.make_async_copy(eps_hbm, eps_ref, sems.at[1]),
    )
    for copy in copies:
        copy.start()
    for copy in copies:
        copy.wait()
    dev_even = lax.axis_index("dev") % 2 == 0
    for y in range(n.y):
        own[6, y] = COURANT / eps_ref[y]
    for c in range(7):
        at = [own[c, y] for y in range(n.y)]
        for kind in range(n.y_kinds):
            top = dev_even if kind == 0 else jnp.logical_not(dev_even)
            for r in range(HALO):
                value = jnp.where(top, at[n.y - HALO + r], at[r])
                y_outs[kind][pl.ds((c * HALO + r) * n.z, n.z), :] = value


def edge_kernel(n, own_ref, other_ref, z_out, *e_outs):
    xy = lax.axis_index("xy")
    dev_even = lax.axis_index("dev") % 2 == 0
    z_top = lax.axis_index("gz") % 2 == xy % 2
    for half in range(2):
        mine = xy == half

        def at(c, y):
            rows = pl.ds((c * n.y + y) * n.z, n.z)
            value = jnp.where(mine, own_ref[rows, :], other_ref[rows, :])
            return jnp.where(z_top, value[n.z - HALO :], value[:HALO])

        for c in range(7):
            edges = [at(c, y) for y in range(n.y)]
            for y in range(n.y):
                z_out[pl.ds(half * n.z_rows + (c * n.y + y) * HALO, HALO), :] = edges[y]
            for kind in range(n.y_kinds):
                top = dev_even if kind == 0 else jnp.logical_not(dev_even)
                for r in range(HALO):
                    edge = jnp.where(top, edges[n.y - HALO + r], edges[r])
                    e_outs[kind][pl.ds(half * n.e_rows + (c * HALO + r) * HALO, HALO), :] = edge


def table_kernel(
    n, dir_hbm, owner_hbm, wall_owner_hbm, phase_hbm, hi_lo_ref, v_ref, place_ref, turn_ref,
    count_ref, dir_ref, owner_ref, wall_owner_ref, phase_ref, sems,
):
    gz, dev, xy = (lax.axis_index(a) for a in ("gz", "dev", "xy"))
    hi_ref, lo_ref = halves(n, hi_lo_ref)
    copies = [
        pltpu.make_async_copy(source, target, sems.at[i])
        for i, (source, target) in enumerate(
            (
                (dir_hbm, dir_ref),
                (owner_hbm, owner_ref),
                (wall_owner_hbm, wall_owner_ref),
                (phase_hbm, phase_ref),
            )
        )
    ]
    for copy in copies:
        copy.start()
    for copy in copies:
        copy.wait()
    index = dir_ref[...]
    bits = THETAS.bit_length() - 1
    polar = (index >> bits).astype(F32)
    azimuth = (index & (THETAS - 1)).astype(F32)
    sin_t, cos_t = sincos(math.pi * (polar + 0.5) / THETAS)
    sin_f, cos_f = sincos(2.0 * math.pi * azimuth / THETAS)
    kx = WAVE_NUMBER * (sin_t * cos_f)
    ky = WAVE_NUMBER * (sin_t * sin_f)
    kz = WAVE_NUMBER * cos_t
    theta = (cos_t * cos_f, cos_t * sin_f, -sin_t)
    phi = (-sin_f, cos_f, jnp.zeros_like(sin_f))
    is_end = jnp.logical_or(gz == 0, gz == n.gz - 1)
    cap_scale = jnp.where(is_end, n.norm, 0.0).astype(F32)
    x_first = (xy * n.x).astype(F32) - (n.nx - 1) / 2.0
    y_first = (dev * n.y).astype(F32) - (n.ny - 1) / 2.0
    z_first = (gz * n.z).astype(F32) - (n.nz - 1) / 2.0
    x_wall = x_first + jnp.where(xy == 0, XB, n.x - 1 - XB).astype(F32)
    z_cap = z_first + jnp.where(gz == 0, ZB, n.z - 1 - ZB).astype(F32)
    row8 = rows_iota((8, LANES))
    row16 = rows_iota((16, LANES))
    fine_x = row8.astype(F32)
    low = row8 < 4
    comp = row8 & 3

    def weights(rows):
        picked = jnp.where(comp == 2, rows[2], rows[3])
        return jnp.where(comp == 0, rows[0], jnp.where(comp == 1, rows[1], picked))

    for t in range(n.tiles):
        lanes = slice(t * LANES, (t + 1) * LANES)
        a, b, c = (v[t : t + 1, :] for v in (kx, ky, kz))
        th = [v[t : t + 1, :] for v in theta]
        ph = [v[t : t + 1, :] for v in phi]
        sf, cf = sincos(a * fine_x)
        for pair in range(n.x // 16):
            if pair % 8 == 0:
                base_x = x_first + 8.0 * 16.0 * (pair // 8)
                coarse_s, coarse_c = sincos(a * (row16.astype(F32) * 8.0 + base_x))
            cosine, sine = [], []
            for h in (2 * (pair % 8), 2 * (pair % 8) + 1):
                cc, cs = coarse_c[h : h + 1, :], coarse_s[h : h + 1, :]
                cosine.append(cc * cf - cs * sf)
                sine.append(cs * cf + cc * sf)
            for part, rows in ((0, cosine), (n.x, sine)):
                high, rest = split(jnp.concatenate(rows, axis=0))
                hi_ref[part + pair * 16 : part + pair * 16 + 16, lanes] = high
                lo_ref[part + pair * 16 : part + pair * 16 + 16, lanes] = rest
        zs, zc = sincos(c * (row16.astype(F32) + z_first))
        for part, rows in ((2 * n.x, zc), (2 * n.x + n.z, zs)):
            high, rest = split(rows)
            hi_ref[part : part + 16, lanes] = high
            lo_ref[part : part + 16, lanes] = rest
        y_of = comp.astype(F32) + y_first
        base_s, base_c = sincos(b * y_of + jnp.where(low, c * z_cap, a * x_wall))
        for face in range(2):
            i, j = ((0, 1), (1, 2))[face]
            scale = cap_scale if face == 0 else n.norm
            w_theta = weights([-th[i], -th[j], -ph[i], -ph[j]]) * scale
            w_phi = weights([-ph[i], -ph[j], th[i], th[j]]) * scale
            for y in range(n.y):
                r = face * 4 + y
                bc, bs = base_c[r : r + 1, :], base_s[r : r + 1, :]
                factor = jnp.where(low, bc, -bs)
                for kind, value in enumerate((factor * w_theta, factor * w_phi)):
                    at = ((face * 2 + kind) * n.y + y) * 8
                    v_ref[at : at + 8, lanes] = value
    for o in range(n.gz):
        count_ref[o] = 0
    which = jnp.where(gz == 0, 0, 1)

    def place(q, carry):
        owner = owner_ref[which, q]
        rank = count_ref[owner]
        count_ref[owner] = rank + 1
        place_ref[q] = owner * n.chunk + 2 + rank
        return carry

    lax.fori_loop(0, n.caps, place, 0)
    for j in range(n.walls):
        place_ref[n.caps + j] = wall_owner_ref[0, j]
    step_of = (row8 // 2).astype(F32)
    part_of = jnp.where((row8 & 1) == 0, 0.5, 1.0)
    sines, cosines = sincos(phase_ref[0] + ANGULAR_STEP * (step_of + part_of))
    turn_ref[0:8, :] = cosines
    turn_ref[8:16, :] = sines


def halves(n, hi_lo_ref):
    return hi_lo_ref.at[0 : n.table_rows], hi_lo_ref.at[n.table_rows : 2 * n.table_rows]


def block_transpose(values):
    row, block = rows_iota((8, LANES)), lanes_iota((8, LANES)) // PATCH
    for bit in (1, 2, 4):
        wide = PATCH * bit
        ahead = pltpu.roll(pltpu.roll(values, 8 - bit, 0), wide, 1)
        behind = pltpu.roll(pltpu.roll(values, bit, 0), LANES - wide, 1)
        row_bit, block_bit = (row & bit) != 0, (block & bit) != 0
        moved = jnp.where(row_bit, behind, ahead)
        values = jnp.where(row_bit == block_bit, values, moved)
    return values


def turn(values):
    swapped = pltpu.roll(values, 4, 0)
    return jnp.where(rows_iota(values.shape) < 4, -swapped, swapped)


def main_kernel(
    n, own_ref, other_ref, halo_ref, far_halo_ref, spectra_hbm, place_ref, turn_ref, hi_lo_ref, v_ref,
    fields_hbm, spectra_out_hbm, far_out, chunk_out, a_ref, m_ref, fields_out, spectra_out, sems,
):
    hi_ref, lo_ref = halves(n, hi_lo_ref)
    spectra_in = pltpu.make_async_copy(spectra_hbm, spectra_out, sems.at[0])
    spectra_in.start()
    gz, dev, xy = (lax.axis_index(a) for a in ("gz", "dev", "xy"))
    gz_even, dev_even = gz % 2 == 0, dev % 2 == 0
    deep = n.z + 8
    lo_ok, hi_ok = gz > 0, gz < n.gz - 1
    if n.both_y:
        y_own = HALO
        y_slots = (
            (0, jnp.logical_not(dev_even), dev > 0),
            (HALO + n.y, dev_even, dev < n.dev - 1),
        )
    else:
        y_own = jnp.where(dev_even, 0, HALO)
        y_slots = ((jnp.where(dev_even, n.y, 0), None, None),)
    pad = jnp.zeros((8 - 2 * HALO, LANES), F32)
    near_is_high = gz % 2 == xy % 2

    def choose(ref, starts, use_first, length):
        if use_first is None:
            return ref[pl.ds(starts[0], length), :]
        return jnp.where(
            use_first, ref[pl.ds(starts[0], length), :], ref[pl.ds(starts[1], length), :]
        )

    def rim(near, far):
        high = jnp.where(near_is_high, near, far)
        low = jnp.where(near_is_high, far, near)
        return jnp.concatenate(
            [jnp.where(hi_ok, high, 0.0), pad, jnp.where(lo_ok, low, 0.0)], axis=0
        )

    kinds = n.y_kinds
    both = (halo_ref, far_halo_ref)
    for half, (block, halo) in enumerate(((own_ref, halo_ref), (other_ref, far_halo_ref))):
        at_x = xy if half == 0 else 1 - xy
        lanes = pl.ds(pl.multiple_of(at_x * n.x, n.x), n.x)
        for c in range(7):
            for y in range(n.y):
                a_ref[c, y_own + y, 0 : n.z, lanes] = block[pl.ds((c * n.y + y) * n.z, n.z), :]
            for start, use_first, ok in y_slots:
                for r in range(HALO):
                    at = (c * HALO + r) * n.z
                    body = choose(halo, [n.starts[k] + at for k in range(kinds)], use_first, n.z)
                    if ok is not None:
                        body = jnp.where(ok, body, 0.0)
                    a_ref[c, start + r, 0 : n.z, lanes] = body
    for half in range(2):
        lanes = slice(half * n.x, (half + 1) * n.x)
        for c in range(7):
            for y in range(n.y):
                at = n.starts[kinds] + half * n.z_rows + (c * n.y + y) * HALO
                a_ref[c, y_own + y, n.z : deep, lanes] = rim(*(ref[pl.ds(at, HALO), :] for ref in both))
            for start, use_first, ok in y_slots:
                for r in range(HALO):
                    at = half * n.e_rows + (c * HALO + r) * HALO
                    starts = [n.starts[kinds + 1 + k] + at for k in range(kinds)]
                    edge = rim(*(choose(ref, starts, use_first, HALO) for ref in both))
                    if ok is not None:
                        edge = jnp.where(ok, edge, 0.0)
                    a_ref[c, start + r, n.z : deep, lanes] = edge

    shape = (deep, n.nx)
    z_row, x_lane = rows_iota(shape), lanes_iota(shape)
    keep = jnp.where(z_row < n.z + HALO, COURANT, jnp.where(lo_ok & (z_row >= deep - HALO), COURANT, 0.0))
    keep = keep.astype(F32)
    last_x, first_x = x_lane == n.nx - 1, x_lane == 0

    def z_next(v):
        return pltpu.roll(v, deep - 1, 0)

    def z_before(v):
        return pltpu.roll(v, 1, 0)

    def x_next(v):
        return jnp.where(last_x, 0.0, pltpu.roll(v, n.nx - 1, 1))

    def x_before(v):
        return jnp.where(first_x, 0.0, pltpu.roll(v, 1, 1))

    own_lanes = pl.ds(pl.multiple_of(xy * n.x, n.x), n.x)
    for step in range(STEPS):
        for y in range(n.rows):
            ex, ey, ez = (a_ref[c, y] for c in range(3))
            if y + 1 < n.rows:
                ex_y, ez_y = a_ref[0, y + 1] - ex, a_ref[2, y + 1] - ez
            else:
                ex_y, ez_y = -ex, -ez
            rate = keep
            if n.both_y and y < HALO:
                rate = jnp.where(dev == 0, 0.0, keep)
            a_ref[3, y] = a_ref[3, y] - rate * (ez_y - (z_next(ey) - ey))
            a_ref[4, y] = a_ref[4, y] - rate * ((z_next(ex) - ex) - (x_next(ez) - ez))
            a_ref[5, y] = a_ref[5, y] - rate * ((x_next(ey) - ey) - ex_y)
        for y in range(n.rows):
            hx, hy, hz = (a_ref[c, y] for c in range(3, 6))
            rate = a_ref[6, y]
            if y > 0:
                hx_y, hz_y = hx - a_ref[3, y - 1], hz - a_ref[5, y - 1]
            else:
                hx_y, hz_y = hx, hz
            a_ref[0, y] = a_ref[0, y] + rate * (hz_y - (hy - z_before(hy)))
            a_ref[1, y] = a_ref[1, y] + rate * ((hx - z_before(hx)) - (hz - x_before(hz)))
            a_ref[2, y] = a_ref[2, y] + rate * ((hy - x_before(hy)) - hx_y)
        if step == 0:
            spectra_in.wait()
        for c in range(6):
            row = 2 * step + (1 if c < 3 else 0)
            cosine, sine = turn_ref[row : row + 1, :], turn_ref[8 + row : 9 + row, :]
            for y in range(n.y):
                value = a_ref[c, y_own + y, 0 : n.z, own_lanes]
                spectra_out[c, y] = spectra_out[c, y] + value * cosine
                spectra_out[6 + c, y] = spectra_out[6 + c, y] - value * sine
                if step == STEPS - 1:
                    fields_out[c, y] = value

    copies = (
        pltpu.make_async_copy(fields_out, fields_hbm, sems.at[1]),
        pltpu.make_async_copy(spectra_out, spectra_out_hbm, sems.at[2]),
    )
    for copy in copies:
        copy.start()
    facing_x = jnp.where(xy == 0, -1.0, 1.0).astype(F32)
    facing_z = jnp.where(gz == 0, -1.0, 1.0).astype(F32)
    row8, lane = rows_iota((8, LANES)), lanes_iota((8, LANES))
    sign = jnp.where(((row8 & 3) == 0) | ((row8 & 3) == 3), -1.0, 1.0).astype(F32)
    own_block = lane // PATCH == row8
    block_sign = jnp.sum(jnp.where(own_block, sign, 0.0), axis=0, keepdims=True)
    cap_left, cap_right, wall_left = [], [], []
    chunk_out[...] = jnp.zeros_like(chunk_out)
    for y in range(n.y):
        plane = [
            jnp.where(gz == 0, spectra_out[p, y, ZB : ZB + 1, :], spectra_out[p, y, n.z - 1 - ZB : n.z - ZB, :])
            for p in [k + 6 * im for im in range(2) for k in Z_PICKS]
        ]
        current = jnp.concatenate(plane, axis=0) * (sign * facing_z)
        cap_left.append(current)
        cap_right.append(turn(current))
        m_ref[y * 8 : y * 8 + 8, :] = block_transpose(current)
        stack = jnp.concatenate(
            [spectra_out[k + 6 * im, y] for im in range(2) for k in X_PICKS], axis=0
        )
        across = stack.T
        record = jnp.where(xy == 0, across[XB : XB + 1, :], across[n.x - 1 - XB : n.x - XB, :])
        record = record * (block_sign * facing_x)
        for o in range(n.gz):
            mine = place_ref[n.caps + y] == o
            at = o * n.chunk
            chunk_out[at : at + 1, :] += jnp.where(mine, record, 0.0)
            chunk_out[at + 1 : at + 2, :] += jnp.where(mine, 1.0, 0.0).astype(F32)
        spread = jnp.where(own_block, record, 0.0)
        for wide in (16, 32, 64):
            spread = spread + pltpu.roll(spread, wide, 1)
        wall_left.append(jnp.where(lane < n.z, spread, turn(spread))[:, : 2 * n.z])
    for q in range(n.caps):
        chunk_out[pl.ds(place_ref[q], 1), :] = m_ref[q : q + 1, :]
    cap = jnp.concatenate(
        [jnp.concatenate(cap_left, axis=0), jnp.concatenate(cap_right, axis=0)], axis=1
    )
    wall = jnp.concatenate(wall_left, axis=0)
    dot = functools.partial(jnp.dot, preferred_element_type=F32)
    wide = min(512, n.dirs)
    for first in range(0, n.dirs, wide):
        sums = []
        for left, rows in ((cap, slice(0, 2 * n.x)), (wall, slice(2 * n.x, 2 * n.x + 2 * n.z))):
            left_hi, left_lo = split(left)
            high, rest = hi_ref[rows, first : first + wide], lo_ref[rows, first : first + wide]
            sums.append(dot(left_hi, high) + (dot(left_lo, high) + dot(left_hi, rest)))
        for t in range(wide // LANES):
            lanes = slice(first + t * LANES, first + (t + 1) * LANES)
            tile = first // LANES + t
            totals = [None] * 4
            for face in range(2):
                for y in range(n.y):
                    rows = sums[face][y * 8 : y * 8 + 8, t * LANES : (t + 1) * LANES]
                    turned = -turn(rows)
                    for kind in range(4):
                        at = ((face * 2 + kind % 2) * n.y + y) * 8
                        term = v_ref[at : at + 8, lanes] * (rows if kind < 2 else turned)
                        totals[kind] = term if totals[kind] is None else totals[kind] + term
            for kind, total in enumerate(totals):
                at = kind * n.tiles + tile
                far_out[at : at + 1, :] = jnp.sum(total, axis=0, keepdims=True)
    for copy in copies:
        copy.wait()


def adjoint_kernel(
    n, far_ref, target_ref, mask_ref, hi_lo_ref, v_ref, intensity_out, owned_out, adjoint_out, all_ref
):
    hi_ref, lo_ref = halves(n, hi_lo_ref)
    gz, dev, xy = (lax.axis_index(a) for a in ("gz", "dev", "xy"))
    block = n.far_rows + n.chunk
    parts = []
    for kind in range(4):
        total = None
        for k in range(n.gz):
            at = (n.gz - 1 - k) * block + kind * n.tiles
            term = far_ref[at : at + n.tiles, :]
            total = term if total is None else total + term
        parts.append(total)
    theta_re, phi_re, theta_im, phi_im = parts
    intensity = theta_re * theta_re + theta_im * theta_im + phi_re * phi_re + phi_im * phi_im
    if n.own_dirs % LANES == 0:
        all_ref[...] = intensity
        first = ((gz * n.dev + dev) * n.xy + xy) * (n.own_dirs // LANES)
        intensity_out[...] = all_ref[pl.ds(first, n.own_dirs // LANES), :]
    else:
        intensity_out[...] = intensity
    slope = 2.0 * (mask_ref[...].astype(F32) * (intensity - target_ref[...]))
    slopes = [slope * part for part in parts]

    faces = [[], []]
    for face in range(2):
        for t in range(n.tiles):
            lanes = slice(t * LANES, (t + 1) * LANES)
            rows = []
            for y in range(n.y):
                at = (face * 2 * n.y + y) * 8
                one, two = v_ref[at : at + 8, lanes], v_ref[at + n.y * 8 : at + n.y * 8 + 8, lanes]
                even, odd = (
                    one * slopes[k][t : t + 1, :] + two * slopes[k + 1][t : t + 1, :] for k in (0, 2)
                )
                rows.append(even + turn(odd))
            faces[face].append(jnp.concatenate(rows, axis=0))
    dot = functools.partial(
        lax.dot_general,
        dimension_numbers=(((1,), (1,)), ((), ())),
        preferred_element_type=F32,
    )
    sums = []
    for face, rows in ((0, slice(0, 2 * n.x)), (1, slice(2 * n.x, 2 * n.x + 2 * n.z))):
        left_hi, left_lo = split(jnp.concatenate(faces[face], axis=1))
        high, rest = hi_ref[rows, :], lo_ref[rows, :]
        sums.append(dot(left_hi, high) + (dot(left_lo, high) + dot(left_hi, rest)))
    cap, wall = sums
    row8, lane = rows_iota((8, LANES)), lanes_iota((8, LANES))
    own_block = lane // PATCH == row8
    for y in range(n.y):
        at = slice(y * 8, y * 8 + 8)
        gradient = cap[at, : n.x] - turn(cap[at, n.x :])
        adjoint_out[n.walls + y * 8 : n.walls + y * 8 + 8, 0, :] = block_transpose(gradient)
        gradient = wall[at, : n.z] - turn(wall[at, n.z :])
        spread = jnp.concatenate([gradient] * (LANES // n.z), axis=1)
        adjoint_out[y, :, :] = jnp.sum(
            jnp.where(own_block, spread, 0.0), axis=0, keepdims=True
        )
    walls = [jnp.zeros((1, LANES), F32) for _ in range(n.walls)]
    rank = jnp.zeros((1, LANES), F32)
    for s in range(n.gz):
        at = pl.multiple_of((n.gz - 1 - (gz ^ s)) * block + n.far_rows, 8)
        rows = far_ref[pl.ds(at, 8), :]
        record, flag = rows[0:1, :], rows[1:2, :] > 0.5
        for r in range(n.walls):
            walls[r] = jnp.where(flag & (rank == float(r)), record, walls[r])
        rank = rank + rows[1:2, :]
    for r in range(n.walls):
        owned_out[r, :, :] = walls[r]
    for cap_at, s in enumerate((0, n.gz - 1)):
        at = pl.multiple_of((n.gz - 1 - (gz ^ s)) * block + n.far_rows, 8)
        rows = far_ref[pl.ds(at, n.chunk), :]
        owned_out[n.walls + cap_at * n.share : n.walls + (cap_at + 1) * n.share, 0, :] = rows[2 : 2 + n.share, :]


def partner(kind, i, n):
    up = (i % 2 == 0) == (kind == 0)
    return (i + 1) % n if up else (i - 1) % n


def exchange(values, axes, image):
    sizes = [lax.axis_size(a) for a in axes]
    pairs = []
    for source in range(math.prod(sizes)):
        rest, where = source, []
        for size in reversed(sizes):
            where.insert(0, rest % size)
            rest //= size
        target = 0
        for size, at in zip(sizes, image(*where)):
            target = target * size + at
        pairs.append((source, target))
    return lax.ppermute(values, axes if len(axes) > 1 else axes[0], pairs)


def local(
    fields, spectra, permittivity, phase_start, wall_owner, cap_owner, dir_index, target, aim_mask
):
    n = Sizes(permittivity.shape, dir_index.shape[0], cap_owner.shape[1])
    gz = lax.axis_index("gz")

    def out(*shape, dtype=F32):
        return jax.ShapeDtypeStruct(shape, dtype)

    def far_memory(values):
        return pltpu.with_memory_space_constraint(values, pltpu.HBM)

    def params(mebibytes):
        return pltpu.CompilerParams(vmem_limit_bytes=mebibytes << 20)

    block = tuple(permittivity.shape)
    own, *y_send = pl.pallas_call(
        functools.partial(pack_kernel, n),
        name="pack",
        out_shape=[out(7, *block)] + [out(n.y_rows, n.x)] * n.y_kinds,
        in_specs=[HBM] * 2,
        out_specs=[VMEM] * (1 + n.y_kinds),
        scratch_shapes=[pltpu.VMEM(block, F32), pltpu.SemaphoreType.DMA((2,))],
        compiler_params=params(4),
    )(far_memory(fields), far_memory(permittivity))
    own = own.reshape(7 * n.y * n.z, n.x)
    y_got = [
        exchange(v, ("dev",), lambda d, k=k: (partner(k, d, n.dev),)) for k, v in enumerate(y_send)
    ]
    other = exchange(own, ("xy",), lambda x: (x ^ 1,))
    z_send, *e_send = pl.pallas_call(
        functools.partial(edge_kernel, n),
        name="edges",
        out_shape=[out(2 * n.z_rows, n.x)] + [out(2 * n.e_rows, n.x)] * n.y_kinds,
        in_specs=[VMEM] * 2,
        out_specs=[VMEM] * (1 + n.y_kinds),
        compiler_params=params(4),
    )(own, other)
    z_got = exchange(z_send, ("gz", "xy"), lambda g, x: (partner(x, g, n.gz), x))
    e_got = [
        exchange(
            v,
            ("gz", "dev", "xy"),
            lambda g, d, x, k=k: (partner(x, g, n.gz), partner(k, d, n.dev), x),
        )
        for k, v in enumerate(e_send)
    ]

    table, v, place, turns = pl.pallas_call(
        functools.partial(table_kernel, n),
        name="tables",
        out_shape=[
            out(2 * n.table_rows, n.dirs, dtype=BF16),
            out(4 * n.y * 8, n.dirs),
            out(n.caps + n.walls, dtype=jnp.int32),
            out(16, LANES),
        ],
        in_specs=[HBM] * 4,
        out_specs=[VMEM] * 2 + [SMEM, VMEM],
        scratch_shapes=[
            pltpu.SMEM((n.gz,), jnp.int32),
            pltpu.VMEM((n.tiles, LANES), jnp.int32),
            pltpu.SMEM(cap_owner.shape, jnp.int32),
            pltpu.SMEM(wall_owner.shape, jnp.int32),
            pltpu.SMEM(phase_start.shape, F32),
            pltpu.SemaphoreType.DMA((4,)),
        ],
        compiler_params=params(8),
        cost_estimate=pl.CostEstimate(flops=1 << 33, bytes_accessed=16 << 20, transcendentals=0),
    )(*map(far_memory, (dir_index.reshape(n.tiles, LANES), cap_owner, wall_owner)), phase_start)
    (*y_got, z_got, turns), e_got = lax.optimization_barrier(((*y_got, z_got, turns), e_got))
    halo = jnp.concatenate([*y_got, z_got, *e_got])
    far_halo = exchange(halo, ("xy",), lambda x: (x ^ 1,))

    anywhere = pl.BlockSpec(memory_space=pl.ANY)
    fields_out, spectra_out, far, chunk = pl.pallas_call(
        functools.partial(main_kernel, n),
        name="window",
        out_shape=[
            out(6, *block),
            out(12, *block),
            out(n.far_rows, LANES),
            out(n.gz * n.chunk, LANES),
        ],
        in_specs=[VMEM] * 4 + [anywhere, SMEM] + [VMEM] * 3,
        out_specs=[anywhere] * 2 + [VMEM] * 2,
        scratch_shapes=[
            pltpu.VMEM((7, n.rows, n.z + 8, n.nx), F32),
            pltpu.VMEM((n.caps, LANES), F32),
            pltpu.VMEM((6, *block), F32),
            pltpu.VMEM((12, *block), F32),
            pltpu.SemaphoreType.DMA((3,)),
        ],
        compiler_params=params(12),
    )(own, other, halo, far_halo, spectra, place, turns, table, v)

    for axis in ("xy", "dev"):
        size = lax.axis_size(axis)
        got = [exchange(far, (axis,), lambda i, k=k: (i ^ k,)) for k in range(1, size)]
        for term in got:
            far = far + term
    payload = [
        jnp.concatenate([far, lax.dynamic_slice_in_dim(chunk, (gz ^ k) * n.chunk, n.chunk)])
        for k in range(n.gz)
    ]
    got = [
        exchange(payload[k], ("gz",), lambda g, k=k: (g ^ k,)) for k in range(n.gz - 1, 0, -1)
    ]
    gathered = jnp.concatenate([*got, payload[0]])

    sliced = n.own_dirs % LANES == 0
    intensity, owned, adjoint = pl.pallas_call(
        functools.partial(adjoint_kernel, n),
        name="adjoint",
        out_shape=[
            out(n.own_dirs // LANES if sliced else n.tiles, LANES),
            out(n.walls + 2 * n.share, 1, LANES),
            out(n.walls + n.caps, 1, LANES),
        ],
        in_specs=[VMEM] * 5,
        out_specs=[VMEM] * 3,
        scratch_shapes=[pltpu.VMEM((n.tiles, LANES), F32)],
        compiler_params=params(8),
    )(gathered, target.reshape(n.tiles, LANES), aim_mask.reshape(n.tiles, LANES), table, v)
    intensity = intensity.reshape(-1)
    if not sliced:
        joined = (gz * n.dev + lax.axis_index("dev")) * n.xy + lax.axis_index("xy")
        intensity = lax.dynamic_slice_in_dim(intensity, joined * n.own_dirs, n.own_dirs)
    shape = (1, 1, 1, -1, LANES)
    return fields_out, spectra_out, owned.reshape(shape), intensity, adjoint.reshape(shape)


def solution(mesh):
    placed = (
        P("groups", "dev", "gz", "xy"),
        P("groups", "dev", "gz", "xy"),
        P(("groups", "dev"), "gz", "xy"),
        P("groups"),
        P("gz", None),
        P(),
        P(),
        P("groups"),
        P("groups"),
    )
    return jax.shard_map(
        local,
        mesh=mesh,
        in_specs=placed,
        out_specs=(
            P("groups", "dev", "gz", "xy"),
            P("groups", "dev", "gz", "xy"),
            P(("groups", "gz"), "dev", "xy", None, None),
            P(("groups", "gz", "dev", "xy")),
            P(("groups", "gz"), "dev", "xy", None, None),
        ),
        check_vma=False,
    )
```

```python
import functools
import math

import jax
import jax.numpy as jnp
from jax import lax
from jax.experimental import pallas as pl
from jax.experimental.pallas import tpu as pltpu
from jax.sharding import PartitionSpec as P

PATCH = 16
XB = 8
ZB = 4
STEPS = 3
THETAS = 64
COURANT = 0.5
ANGULAR_STEP = 0.3
WAVE_NUMBER = 0.6
CURRENT_SIGNS = (-1.0, 1.0, 1.0, -1.0)
X_PICKS = (5, 4, 2, 1)
Z_PICKS = (4, 3, 1, 0)
LANES = 128
HALO = STEPS
F32 = jnp.float32
BF16 = jnp.bfloat16
VMEM = pl.BlockSpec(memory_space=pltpu.VMEM)
SMEM = pl.BlockSpec(memory_space=pltpu.SMEM)
HBM = pl.BlockSpec(memory_space=pltpu.HBM)


def up8(rows):
    return -(-rows // 8) * 8


def sincos(angle):
    turns = jnp.floor(angle * (2.0 / math.pi) + 0.5)
    r = angle - turns * 1.5703125
    r = r - turns * 4.837512969970703125e-4
    r = r - turns * 7.54978995489188e-8
    r2 = r * r
    s = r + r * r2 * (-1.6666654611e-1 + r2 * (8.3321608736e-3 + r2 * -1.9515295891e-4))
    c = 1.0 - 0.5 * r2 + r2 * r2 * (
        4.166664568298827e-2 + r2 * (-1.388731625493765e-3 + r2 * 2.443315711809948e-5)
    )
    quarter = turns.astype(jnp.int32)
    odd = (quarter & 1) == 1
    sine = jnp.where(odd, c, s)
    cosine = jnp.where(odd, s, c)
    sine = jnp.where((quarter & 2) == 2, -sine, sine)
    cosine = jnp.where(((quarter + 1) & 2) == 2, -cosine, cosine)
    return sine, cosine


def split(values):
    high = values.astype(BF16)
    return high, (values - high.astype(F32)).astype(BF16)


def rows_iota(shape):
    return lax.broadcasted_iota(jnp.int32, shape, 0)


def lanes_iota(shape):
    return lax.broadcasted_iota(jnp.int32, shape, len(shape) - 1)


class Sizes:
    def __init__(self, block, directions, caps):
        self.gz, self.dev, self.xy = (lax.axis_size(a) for a in ("gz", "dev", "xy"))
        self.y, self.z, self.x = block
        self.both_y = self.dev > 2
        self.rows = self.y + HALO * (2 if self.both_y else 1)
        self.nx, self.ny, self.nz = self.x * self.xy, self.y * self.dev, self.z * self.gz
        self.dirs = directions
        self.tiles = directions // LANES
        self.table_rows = 2 * self.x + 2 * self.z
        self.walls = self.y * self.z // PATCH
        self.caps = caps
        self.share = caps // self.gz
        self.own_dirs = directions // (self.gz * self.dev * self.xy)
        self.chunk = up8(2 + self.share)
        self.far_rows = 4 * self.tiles
        self.norm = 1.0 / math.sqrt(2.0 * (2 * self.ny * self.nz + 2 * self.ny * self.nx))
        self.y_rows = 7 * HALO * self.z
        self.z_rows = up8(7 * self.y * HALO)
        self.e_rows = up8(7 * HALO * HALO)
        y_kinds = 2 if self.both_y else 1
        sizes = [self.y_rows] * y_kinds + [2 * self.z_rows] + [2 * self.e_rows] * y_kinds
        self.starts = [sum(sizes[:i]) for i in range(len(sizes))]
        self.halo_rows = sum(sizes)
        self.y_kinds = y_kinds


def pack_kernel(n, f_hbm, eps_hbm, own, *rest):
    y_outs, (eps_ref, sems) = rest[: n.y_kinds], rest[n.y_kinds :]
    copies = (
        pltpu.make_async_copy(f_hbm, own.at[0:6], sems.at[0]),
        pltpu.make_async_copy(eps_hbm, eps_ref, sems.at[1]),
    )
    for copy in copies:
        copy.start()
    for copy in copies:
        copy.wait()
    dev_even = lax.axis_index("dev") % 2 == 0
    for y in range(n.y):
        own[6, y] = COURANT / eps_ref[y]
    for c in range(7):
        at = [own[c, y] for y in range(n.y)]
        for kind in range(n.y_kinds):
            top = dev_even if kind == 0 else jnp.logical_not(dev_even)
            for r in range(HALO):
                value = jnp.where(top, at[n.y - HALO + r], at[r])
                y_outs[kind][pl.ds((c * HALO + r) * n.z, n.z), :] = value


def edge_kernel(n, own_ref, other_ref, z_out, *e_outs):
    xy = lax.axis_index("xy")
    dev_even = lax.axis_index("dev") % 2 == 0
    z_top = lax.axis_index("gz") % 2 == xy % 2
    for half in range(2):
        mine = xy == half

        def at(c, y):
            rows = pl.ds((c * n.y + y) * n.z, n.z)
            value = jnp.where(mine, own_ref[rows, :], other_ref[rows, :])
            return jnp.where(z_top, value[n.z - HALO :], value[:HALO])

        for c in range(7):
            edges = [at(c, y) for y in range(n.y)]
            for y in range(n.y):
                z_out[pl.ds(half * n.z_rows + (c * n.y + y) * HALO, HALO), :] = edges[y]
            for kind in range(n.y_kinds):
                top = dev_even if kind == 0 else jnp.logical_not(dev_even)
                for r in range(HALO):
                    edge = jnp.where(top, edges[n.y - HALO + r], edges[r])
                    e_outs[kind][pl.ds(half * n.e_rows + (c * HALO + r) * HALO, HALO), :] = edge


def table_kernel(
    n, dir_hbm, owner_hbm, wall_owner_hbm, phase_hbm, hi_lo_ref, v_ref, place_ref, turn_ref,
    count_ref, dir_ref, owner_ref, wall_owner_ref, phase_ref, sems,
):
    gz, dev, xy = (lax.axis_index(a) for a in ("gz", "dev", "xy"))
    hi_ref, lo_ref = halves(n, hi_lo_ref)
    copies = [
        pltpu.make_async_copy(source, target, sems.at[i])
        for i, (source, target) in enumerate(
            (
                (dir_hbm, dir_ref),
                (owner_hbm, owner_ref),
                (wall_owner_hbm, wall_owner_ref),
                (phase_hbm, phase_ref),
            )
        )
    ]
    for copy in copies:
        copy.start()
    for copy in copies:
        copy.wait()
    index = dir_ref[...]
    bits = THETAS.bit_length() - 1
    polar = (index >> bits).astype(F32)
    azimuth = (index & (THETAS - 1)).astype(F32)
    sin_t, cos_t = sincos(math.pi * (polar + 0.5) / THETAS)
    sin_f, cos_f = sincos(2.0 * math.pi * azimuth / THETAS)
    kx = WAVE_NUMBER * (sin_t * cos_f)
    ky = WAVE_NUMBER * (sin_t * sin_f)
    kz = WAVE_NUMBER * cos_t
    theta = (cos_t * cos_f, cos_t * sin_f, -sin_t)
    phi = (-sin_f, cos_f, jnp.zeros_like(sin_f))
    is_end = jnp.logical_or(gz == 0, gz == n.gz - 1)
    cap_scale = jnp.where(is_end, n.norm, 0.0).astype(F32)
    x_first = (xy * n.x).astype(F32) - (n.nx - 1) / 2.0
    y_first = (dev * n.y).astype(F32) - (n.ny - 1) / 2.0
    z_first = (gz * n.z).astype(F32) - (n.nz - 1) / 2.0
    x_wall = x_first + jnp.where(xy == 0, XB, n.x - 1 - XB).astype(F32)
    z_cap = z_first + jnp.where(gz == 0, ZB, n.z - 1 - ZB).astype(F32)
    row8 = rows_iota((8, LANES))
    row16 = rows_iota((16, LANES))
    fine_x = row8.astype(F32)
    low = row8 < 4
    comp = row8 & 3

    def weights(rows):
        picked = jnp.where(comp == 2, rows[2], rows[3])
        return jnp.where(comp == 0, rows[0], jnp.where(comp == 1, rows[1], picked))

    for t in range(n.tiles):
        lanes = slice(t * LANES, (t + 1) * LANES)
        a, b, c = (v[t : t + 1, :] for v in (kx, ky, kz))
        th = [v[t : t + 1, :] for v in theta]
        ph = [v[t : t + 1, :] for v in phi]
        sf, cf = sincos(a * fine_x)
        for pair in range(n.x // 16):
            if pair % 8 == 0:
                base_x = x_first + 8.0 * 16.0 * (pair // 8)
                coarse_s, coarse_c = sincos(a * (row16.astype(F32) * 8.0 + base_x))
            cosine, sine = [], []
            for h in (2 * (pair % 8), 2 * (pair % 8) + 1):
                cc, cs = coarse_c[h : h + 1, :], coarse_s[h : h + 1, :]
                cosine.append(cc * cf - cs * sf)
                sine.append(cs * cf + cc * sf)
            for part, rows in ((0, cosine), (n.x, sine)):
                high, rest = split(jnp.concatenate(rows, axis=0))
                hi_ref[part + pair * 16 : part + pair * 16 + 16, lanes] = high
                lo_ref[part + pair * 16 : part + pair * 16 + 16, lanes] = rest
        zs, zc = sincos(c * (row16.astype(F32) + z_first))
        for part, rows in ((2 * n.x, zc), (2 * n.x + n.z, zs)):
            high, rest = split(rows)
            hi_ref[part : part + 16, lanes] = high
            lo_ref[part : part + 16, lanes] = rest
        y_of = comp.astype(F32) + y_first
        base_s, base_c = sincos(b * y_of + jnp.where(low, c * z_cap, a * x_wall))
        for face in range(2):
            i, j = ((0, 1), (1, 2))[face]
            scale = cap_scale if face == 0 else n.norm
            w_theta = weights([-th[i], -th[j], -ph[i], -ph[j]]) * scale
            w_phi = weights([-ph[i], -ph[j], th[i], th[j]]) * scale
            for kind, value in enumerate((w_theta, w_phi)):
                at = 16 + (face * 2 + kind) * 8
                v_ref[at : at + 8, lanes] = value
        v_ref[0:8, lanes] = base_c
        v_ref[8:16, lanes] = base_s
    for o in range(n.gz):
        count_ref[o] = 0
    which = jnp.where(gz == 0, 0, 1)

    def place(q, carry):
        owner = owner_ref[which, q]
        rank = count_ref[owner]
        count_ref[owner] = rank + 1
        place_ref[q] = owner * n.chunk + 2 + rank
        return carry

    lax.fori_loop(0, n.caps, place, 0)
    for j in range(n.walls):
        place_ref[n.caps + j] = wall_owner_ref[0, j]
    step_of = (row8 // 2).astype(F32)
    part_of = jnp.where((row8 & 1) == 0, 0.5, 1.0)
    sines, cosines = sincos(phase_ref[0] + ANGULAR_STEP * (step_of + part_of))
    turn_ref[0:8, :] = cosines
    turn_ref[8:16, :] = sines


def halves(n, hi_lo_ref):
    return hi_lo_ref.at[0 : n.table_rows], hi_lo_ref.at[n.table_rows : 2 * n.table_rows]


def block_transpose(values):
    row, block = rows_iota((8, LANES)), lanes_iota((8, LANES)) // PATCH
    for bit in (1, 2, 4):
        wide = PATCH * bit
        ahead = pltpu.roll(pltpu.roll(values, 8 - bit, 0), wide, 1)
        behind = pltpu.roll(pltpu.roll(values, bit, 0), LANES - wide, 1)
        row_bit, block_bit = (row & bit) != 0, (block & bit) != 0
        moved = jnp.where(row_bit, behind, ahead)
        values = jnp.where(row_bit == block_bit, values, moved)
    return values


def patch_factors(n, v_ref, face, lanes):
    low = rows_iota((8, LANES)) < 4
    base_c, base_s = v_ref[0:8, lanes], v_ref[8:16, lanes]
    at = [face * 4 + y for y in range(n.y)]
    return [jnp.where(low, base_c[r : r + 1, :], -base_s[r : r + 1, :]) for r in at]


def face_weights(v_ref, face, lanes):
    return (v_ref[16 + face * 16 + 8 * kind : 24 + face * 16 + 8 * kind, lanes] for kind in range(2))


def turn(values):
    swapped = pltpu.roll(values, 4, 0)
    return jnp.where(rows_iota(values.shape) < 4, -swapped, swapped)


def main_kernel(
    n, own_ref, other_ref, halo_ref, far_halo_ref, spectra_hbm, place_ref, turn_ref, hi_lo_ref, v_ref,
    fields_hbm, spectra_out_hbm, far_out, chunk_out, a_ref, m_ref, fields_out, spectra_out, sems,
):
    hi_ref, lo_ref = halves(n, hi_lo_ref)
    spectra_in = pltpu.make_async_copy(spectra_hbm, spectra_out, sems.at[0])
    spectra_in.start()
    gz, dev, xy = (lax.axis_index(a) for a in ("gz", "dev", "xy"))
    gz_even, dev_even = gz % 2 == 0, dev % 2 == 0
    deep = n.z + 8
    lo_ok, hi_ok = gz > 0, gz < n.gz - 1
    if n.both_y:
        y_own = HALO
        y_slots = (
            (0, jnp.logical_not(dev_even), dev > 0),
            (HALO + n.y, dev_even, dev < n.dev - 1),
        )
    else:
        y_own = jnp.where(dev_even, 0, HALO)
        y_slots = ((jnp.where(dev_even, n.y, 0), None, None),)
    pad = jnp.zeros((8 - 2 * HALO, LANES), F32)
    near_is_high = gz % 2 == xy % 2

    def choose(ref, starts, use_first, length):
        if use_first is None:
            return ref[pl.ds(starts[0], length), :]
        return jnp.where(
            use_first, ref[pl.ds(starts[0], length), :], ref[pl.ds(starts[1], length), :]
        )

    def rim(near, far):
        high = jnp.where(near_is_high, near, far)
        low = jnp.where(near_is_high, far, near)
        return jnp.concatenate(
            [jnp.where(hi_ok, high, 0.0), pad, jnp.where(lo_ok, low, 0.0)], axis=0
        )

    kinds = n.y_kinds
    both = (halo_ref, far_halo_ref)
    for half, (block, halo) in enumerate(((own_ref, halo_ref), (other_ref, far_halo_ref))):
        at_x = xy if half == 0 else 1 - xy
        lanes = pl.ds(pl.multiple_of(at_x * n.x, n.x), n.x)
        for c in range(7):
            for y in range(n.y):
                a_ref[c, y_own + y, 0 : n.z, lanes] = block[pl.ds((c * n.y + y) * n.z, n.z), :]
            for start, use_first, ok in y_slots:
                for r in range(HALO):
                    at = (c * HALO + r) * n.z
                    body = choose(halo, [n.starts[k] + at for k in range(kinds)], use_first, n.z)
                    if ok is not None:
                        body = jnp.where(ok, body, 0.0)
                    a_ref[c, start + r, 0 : n.z, lanes] = body
    for half in range(2):
        lanes = slice(half * n.x, (half + 1) * n.x)
        for c in range(7):
            for y in range(n.y):
                at = n.starts[kinds] + half * n.z_rows + (c * n.y + y) * HALO
                a_ref[c, y_own + y, n.z : deep, lanes] = rim(*(ref[pl.ds(at, HALO), :] for ref in both))
            for start, use_first, ok in y_slots:
                for r in range(HALO):
                    at = half * n.e_rows + (c * HALO + r) * HALO
                    starts = [n.starts[kinds + 1 + k] + at for k in range(kinds)]
                    edge = rim(*(choose(ref, starts, use_first, HALO) for ref in both))
                    if ok is not None:
                        edge = jnp.where(ok, edge, 0.0)
                    a_ref[c, start + r, n.z : deep, lanes] = edge

    shape = (deep, n.nx)
    z_row, x_lane = rows_iota(shape), lanes_iota(shape)
    keep = jnp.where(z_row < n.z + HALO, COURANT, jnp.where(lo_ok & (z_row >= deep - HALO), COURANT, 0.0))
    keep = keep.astype(F32)
    last_x, first_x = x_lane == n.nx - 1, x_lane == 0

    def z_next(v):
        return pltpu.roll(v, deep - 1, 0)

    def z_before(v):
        return pltpu.roll(v, 1, 0)

    def x_next(v):
        return jnp.where(last_x, 0.0, pltpu.roll(v, n.nx - 1, 1))

    def x_before(v):
        return jnp.where(first_x, 0.0, pltpu.roll(v, 1, 1))

    own_lanes = pl.ds(pl.multiple_of(xy * n.x, n.x), n.x)
    for step in range(STEPS):
        for y in range(n.rows):
            ex, ey, ez = (a_ref[c, y] for c in range(3))
            if y + 1 < n.rows:
                ex_y, ez_y = a_ref[0, y + 1] - ex, a_ref[2, y + 1] - ez
            else:
                ex_y, ez_y = -ex, -ez
            rate = keep
            if n.both_y and y < HALO:
                rate = jnp.where(dev == 0, 0.0, keep)
            a_ref[3, y] = a_ref[3, y] - rate * (ez_y - (z_next(ey) - ey))
            a_ref[4, y] = a_ref[4, y] - rate * ((z_next(ex) - ex) - (x_next(ez) - ez))
            a_ref[5, y] = a_ref[5, y] - rate * ((x_next(ey) - ey) - ex_y)
        for y in range(n.rows):
            hx, hy, hz = (a_ref[c, y] for c in range(3, 6))
            rate = a_ref[6, y]
            if y > 0:
                hx_y, hz_y = hx - a_ref[3, y - 1], hz - a_ref[5, y - 1]
            else:
                hx_y, hz_y = hx, hz
            a_ref[0, y] = a_ref[0, y] + rate * (hz_y - (hy - z_before(hy)))
            a_ref[1, y] = a_ref[1, y] + rate * ((hx - z_before(hx)) - (hz - x_before(hz)))
            a_ref[2, y] = a_ref[2, y] + rate * ((hy - x_before(hy)) - hx_y)
        if step == 0:
            spectra_in.wait()
        for c in range(6):
            row = 2 * step + (1 if c < 3 else 0)
            cosine, sine = turn_ref[row : row + 1, :], turn_ref[8 + row : 9 + row, :]
            for y in range(n.y):
                value = a_ref[c, y_own + y, 0 : n.z, own_lanes]
                spectra_out[c, y] = spectra_out[c, y] + value * cosine
                spectra_out[6 + c, y] = spectra_out[6 + c, y] - value * sine
                if step == STEPS - 1:
                    fields_out[c, y] = value

    copies = (
        pltpu.make_async_copy(fields_out, fields_hbm, sems.at[1]),
        pltpu.make_async_copy(spectra_out, spectra_out_hbm, sems.at[2]),
    )
    for copy in copies:
        copy.start()
    facing_x = jnp.where(xy == 0, -1.0, 1.0).astype(F32)
    facing_z = jnp.where(gz == 0, -1.0, 1.0).astype(F32)
    row8, lane = rows_iota((8, LANES)), lanes_iota((8, LANES))
    sign = jnp.where(((row8 & 3) == 0) | ((row8 & 3) == 3), -1.0, 1.0).astype(F32)
    own_block = lane // PATCH == row8
    block_sign = jnp.sum(jnp.where(own_block, sign, 0.0), axis=0, keepdims=True)
    cap_left, cap_right, wall_left = [], [], []
    chunk_out[...] = jnp.zeros_like(chunk_out)
    for y in range(n.y):
        plane = [
            jnp.where(gz == 0, spectra_out[p, y, ZB : ZB + 1, :], spectra_out[p, y, n.z - 1 - ZB : n.z - ZB, :])
            for p in [k + 6 * im for im in range(2) for k in Z_PICKS]
        ]
        current = jnp.concatenate(plane, axis=0) * (sign * facing_z)
        cap_left.append(current)
        cap_right.append(turn(current))
        m_ref[y * 8 : y * 8 + 8, :] = block_transpose(current)
        stack = jnp.concatenate(
            [spectra_out[k + 6 * im, y] for im in range(2) for k in X_PICKS], axis=0
        )
        across = stack.T
        record = jnp.where(xy == 0, across[XB : XB + 1, :], across[n.x - 1 - XB : n.x - XB, :])
        record = record * (block_sign * facing_x)
        for o in range(n.gz):
            mine = place_ref[n.caps + y] == o
            at = o * n.chunk
            chunk_out[at : at + 1, :] += jnp.where(mine, record, 0.0)
            chunk_out[at + 1 : at + 2, :] += jnp.where(mine, 1.0, 0.0).astype(F32)
        spread = jnp.where(own_block, record, 0.0)
        for wide in (16, 32, 64):
            spread = spread + pltpu.roll(spread, wide, 1)
        wall_left.append(jnp.where(lane < n.z, spread, turn(spread))[:, : 2 * n.z])
    for q in range(n.caps):
        chunk_out[pl.ds(place_ref[q], 1), :] = m_ref[q : q + 1, :]
    cap = jnp.concatenate(
        [jnp.concatenate(cap_left, axis=0), jnp.concatenate(cap_right, axis=0)], axis=1
    )
    wall = jnp.concatenate(wall_left, axis=0)
    dot = functools.partial(jnp.dot, preferred_element_type=F32)
    wide = min(512, n.dirs)
    for first in range(0, n.dirs, wide):
        sums = []
        for left, rows in ((cap, slice(0, 2 * n.x)), (wall, slice(2 * n.x, 2 * n.x + 2 * n.z))):
            left_hi, left_lo = split(left)
            high, rest = hi_ref[rows, first : first + wide], lo_ref[rows, first : first + wide]
            sums.append(dot(left_hi, high) + (dot(left_lo, high) + dot(left_hi, rest)))
        for t in range(wide // LANES):
            lanes = slice(first + t * LANES, first + (t + 1) * LANES)
            tile = first // LANES + t
            totals = [0.0] * 4
            for face in range(2):
                even, odd = 0.0, 0.0
                for y, factor in enumerate(patch_factors(n, v_ref, face, lanes)):
                    rows = sums[face][y * 8 : y * 8 + 8, t * LANES : (t + 1) * LANES]
                    even = even + factor * rows
                    odd = odd - factor * turn(rows)
                w_theta, w_phi = face_weights(v_ref, face, lanes)
                for kind, term in enumerate((w_theta * even, w_phi * even, w_theta * odd, w_phi * odd)):
                    totals[kind] = totals[kind] + term
            for kind, total in enumerate(totals):
                at = kind * n.tiles + tile
                far_out[at : at + 1, :] = jnp.sum(total, axis=0, keepdims=True)
    for copy in copies:
        copy.wait()


def adjoint_kernel(
    n, far_ref, target_ref, mask_ref, hi_lo_ref, v_ref, intensity_out, owned_out, adjoint_out, all_ref
):
    hi_ref, lo_ref = halves(n, hi_lo_ref)
    gz, dev, xy = (lax.axis_index(a) for a in ("gz", "dev", "xy"))
    block = n.far_rows + n.chunk
    parts = []
    for kind in range(4):
        total = None
        for k in range(n.gz):
            at = (n.gz - 1 - k) * block + kind * n.tiles
            term = far_ref[at : at + n.tiles, :]
            total = term if total is None else total + term
        parts.append(total)
    theta_re, phi_re, theta_im, phi_im = parts
    intensity = theta_re * theta_re + theta_im * theta_im + phi_re * phi_re + phi_im * phi_im
    if n.own_dirs % LANES == 0:
        all_ref[...] = intensity
        first = ((gz * n.dev + dev) * n.xy + xy) * (n.own_dirs // LANES)
        intensity_out[...] = all_ref[pl.ds(first, n.own_dirs // LANES), :]
    else:
        intensity_out[...] = intensity
    slope = 2.0 * (mask_ref[...].astype(F32) * (intensity - target_ref[...]))
    slopes = [slope * part for part in parts]

    faces = [[], []]
    for face in range(2):
        for t in range(n.tiles):
            lanes = slice(t * LANES, (t + 1) * LANES)
            w_theta, w_phi = face_weights(v_ref, face, lanes)
            even, odd = (
                w_theta * slopes[k][t : t + 1, :] + w_phi * slopes[k + 1][t : t + 1, :] for k in (0, 2)
            )
            rows = [
                factor * even + turn(factor * odd) for factor in patch_factors(n, v_ref, face, lanes)
            ]
            faces[face].append(jnp.concatenate(rows, axis=0))
    dot = functools.partial(
        lax.dot_general,
        dimension_numbers=(((1,), (1,)), ((), ())),
        preferred_element_type=F32,
    )
    sums = []
    for face, rows in ((0, slice(0, 2 * n.x)), (1, slice(2 * n.x, 2 * n.x + 2 * n.z))):
        left_hi, left_lo = split(jnp.concatenate(faces[face], axis=1))
        high, rest = hi_ref[rows, :], lo_ref[rows, :]
        sums.append(dot(left_hi, high) + (dot(left_lo, high) + dot(left_hi, rest)))
    cap, wall = sums
    row8, lane = rows_iota((8, LANES)), lanes_iota((8, LANES))
    own_block = lane // PATCH == row8
    for y in range(n.y):
        at = slice(y * 8, y * 8 + 8)
        gradient = cap[at, : n.x] - turn(cap[at, n.x :])
        adjoint_out[n.walls + y * 8 : n.walls + y * 8 + 8, 0, :] = block_transpose(gradient)
        gradient = wall[at, : n.z] - turn(wall[at, n.z :])
        spread = jnp.concatenate([gradient] * (LANES // n.z), axis=1)
        adjoint_out[y, :, :] = jnp.sum(
            jnp.where(own_block, spread, 0.0), axis=0, keepdims=True
        )
    walls = [jnp.zeros((1, LANES), F32) for _ in range(n.walls)]
    rank = jnp.zeros((1, LANES), F32)
    for s in range(n.gz):
        at = pl.multiple_of((n.gz - 1 - (gz ^ s)) * block + n.far_rows, 8)
        rows = far_ref[pl.ds(at, 8), :]
        record, flag = rows[0:1, :], rows[1:2, :] > 0.5
        for r in range(n.walls):
            walls[r] = jnp.where(flag & (rank == float(r)), record, walls[r])
        rank = rank + rows[1:2, :]
    for r in range(n.walls):
        owned_out[r, :, :] = walls[r]
    for cap_at, s in enumerate((0, n.gz - 1)):
        at = pl.multiple_of((n.gz - 1 - (gz ^ s)) * block + n.far_rows, 8)
        rows = far_ref[pl.ds(at, n.chunk), :]
        owned_out[n.walls + cap_at * n.share : n.walls + (cap_at + 1) * n.share, 0, :] = rows[2 : 2 + n.share, :]


def partner(kind, i, n):
    up = (i % 2 == 0) == (kind == 0)
    return (i + 1) % n if up else (i - 1) % n


def exchange(values, axes, image):
    sizes = [lax.axis_size(a) for a in axes]
    pairs = []
    for source in range(math.prod(sizes)):
        rest, where = source, []
        for size in reversed(sizes):
            where.insert(0, rest % size)
            rest //= size
        target = 0
        for size, at in zip(sizes, image(*where)):
            target = target * size + at
        pairs.append((source, target))
    return lax.ppermute(values, axes if len(axes) > 1 else axes[0], pairs)


def local(
    fields, spectra, permittivity, phase_start, wall_owner, cap_owner, dir_index, target, aim_mask
):
    n = Sizes(permittivity.shape, dir_index.shape[0], cap_owner.shape[1])
    gz = lax.axis_index("gz")

    def out(*shape, dtype=F32):
        return jax.ShapeDtypeStruct(shape, dtype)

    def far_memory(values):
        return pltpu.with_memory_space_constraint(values, pltpu.HBM)

    def params(mebibytes):
        return pltpu.CompilerParams(vmem_limit_bytes=mebibytes << 20)

    block = tuple(permittivity.shape)
    own, *y_send = pl.pallas_call(
        functools.partial(pack_kernel, n),
        name="pack",
        out_shape=[out(7, *block)] + [out(n.y_rows, n.x)] * n.y_kinds,
        in_specs=[HBM] * 2,
        out_specs=[VMEM] * (1 + n.y_kinds),
        scratch_shapes=[pltpu.VMEM(block, F32), pltpu.SemaphoreType.DMA((2,))],
        compiler_params=params(4),
    )(far_memory(fields), far_memory(permittivity))
    own = own.reshape(7 * n.y * n.z, n.x)
    y_got = [
        exchange(v, ("dev",), lambda d, k=k: (partner(k, d, n.dev),)) for k, v in enumerate(y_send)
    ]
    other = exchange(own, ("xy",), lambda x: (x ^ 1,))
    z_send, *e_send = pl.pallas_call(
        functools.partial(edge_kernel, n),
        name="edges",
        out_shape=[out(2 * n.z_rows, n.x)] + [out(2 * n.e_rows, n.x)] * n.y_kinds,
        in_specs=[VMEM] * 2,
        out_specs=[VMEM] * (1 + n.y_kinds),
        compiler_params=params(4),
    )(own, other)
    z_got = exchange(z_send, ("gz", "xy"), lambda g, x: (partner(x, g, n.gz), x))
    e_got = [
        exchange(
            v,
            ("gz", "dev", "xy"),
            lambda g, d, x, k=k: (partner(x, g, n.gz), partner(k, d, n.dev), x),
        )
        for k, v in enumerate(e_send)
    ]

    table, v, place, turns = pl.pallas_call(
        functools.partial(table_kernel, n),
        name="tables",
        out_shape=[
            out(2 * n.table_rows, n.dirs, dtype=BF16),
            out(48, n.dirs),
            out(n.caps + n.walls, dtype=jnp.int32),
            out(16, LANES),
        ],
        in_specs=[HBM] * 4,
        out_specs=[VMEM] * 2 + [SMEM, VMEM],
        scratch_shapes=[
            pltpu.SMEM((n.gz,), jnp.int32),
            pltpu.VMEM((n.tiles, LANES), jnp.int32),
            pltpu.SMEM(cap_owner.shape, jnp.int32),
            pltpu.SMEM(wall_owner.shape, jnp.int32),
            pltpu.SMEM(phase_start.shape, F32),
            pltpu.SemaphoreType.DMA((4,)),
        ],
        compiler_params=params(8),
        cost_estimate=pl.CostEstimate(flops=1 << 33, bytes_accessed=16 << 20, transcendentals=0),
    )(*map(far_memory, (dir_index.reshape(n.tiles, LANES), cap_owner, wall_owner)), phase_start)
    (*y_got, z_got, turns), e_got = lax.optimization_barrier(((*y_got, z_got, turns), e_got))
    halo = jnp.concatenate([*y_got, z_got, *e_got])
    far_halo = exchange(halo, ("xy",), lambda x: (x ^ 1,))

    anywhere = pl.BlockSpec(memory_space=pl.ANY)
    fields_out, spectra_out, far, chunk = pl.pallas_call(
        functools.partial(main_kernel, n),
        name="window",
        out_shape=[
            out(6, *block),
            out(12, *block),
            out(n.far_rows, LANES),
            out(n.gz * n.chunk, LANES),
        ],
        in_specs=[VMEM] * 4 + [anywhere, SMEM] + [VMEM] * 3,
        out_specs=[anywhere] * 2 + [VMEM] * 2,
        scratch_shapes=[
            pltpu.VMEM((7, n.rows, n.z + 8, n.nx), F32),
            pltpu.VMEM((n.caps, LANES), F32),
            pltpu.VMEM((6, *block), F32),
            pltpu.VMEM((12, *block), F32),
            pltpu.SemaphoreType.DMA((3,)),
        ],
        compiler_params=params(12),
    )(own, other, halo, far_halo, spectra, place, turns, table, v)

    for axis in ("xy", "dev"):
        size = lax.axis_size(axis)
        got = [exchange(far, (axis,), lambda i, k=k: (i ^ k,)) for k in range(1, size)]
        for term in got:
            far = far + term
    payload = [
        jnp.concatenate([far, lax.dynamic_slice_in_dim(chunk, (gz ^ k) * n.chunk, n.chunk)])
        for k in range(n.gz)
    ]
    got = [
        exchange(payload[k], ("gz",), lambda g, k=k: (g ^ k,)) for k in range(n.gz - 1, 0, -1)
    ]
    gathered = jnp.concatenate([*got, payload[0]])

    sliced = n.own_dirs % LANES == 0
    intensity, owned, adjoint = pl.pallas_call(
        functools.partial(adjoint_kernel, n),
        name="adjoint",
        out_shape=[
            out(n.own_dirs // LANES if sliced else n.tiles, LANES),
            out(n.walls + 2 * n.share, 1, LANES),
            out(n.walls + n.caps, 1, LANES),
        ],
        in_specs=[VMEM] * 5,
        out_specs=[VMEM] * 3,
        scratch_shapes=[pltpu.VMEM((n.tiles, LANES), F32)],
        compiler_params=params(8),
    )(gathered, target.reshape(n.tiles, LANES), aim_mask.reshape(n.tiles, LANES), table, v)
    intensity = intensity.reshape(-1)
    if not sliced:
        joined = (gz * n.dev + lax.axis_index("dev")) * n.xy + lax.axis_index("xy")
        intensity = lax.dynamic_slice_in_dim(intensity, joined * n.own_dirs, n.own_dirs)
    shape = (1, 1, 1, -1, LANES)
    return fields_out, spectra_out, owned.reshape(shape), intensity, adjoint.reshape(shape)


def solution(mesh):
    placed = (
        P("groups", "dev", "gz", "xy"),
        P("groups", "dev", "gz", "xy"),
        P(("groups", "dev"), "gz", "xy"),
        P("groups"),
        P("gz", None),
        P(),
        P(),
        P("groups"),
        P("groups"),
    )
    return jax.shard_map(
        local,
        mesh=mesh,
        in_specs=placed,
        out_specs=(
            P("groups", "dev", "gz", "xy"),
            P("groups", "dev", "gz", "xy"),
            P(("groups", "gz"), "dev", "xy", None, None),
            P(("groups", "gz", "dev", "xy")),
            P(("groups", "gz"), "dev", "xy", None, None),
        ),
        check_vma=False,
    )
```

```python
import functools
import math

import jax
import jax.numpy as jnp
from jax import lax
from jax.experimental import pallas as pl
from jax.experimental.pallas import tpu as pltpu
from jax.sharding import PartitionSpec as P

PATCH = 16
XB = 8
ZB = 4
STEPS = 3
THETAS = 64
COURANT = 0.5
ANGULAR_STEP = 0.3
WAVE_NUMBER = 0.6
CURRENT_SIGNS = (-1.0, 1.0, 1.0, -1.0)
X_PICKS = (5, 4, 2, 1)
Z_PICKS = (4, 3, 1, 0)
LANES = 128
HALO = STEPS
F32 = jnp.float32
BF16 = jnp.bfloat16
VMEM = pl.BlockSpec(memory_space=pltpu.VMEM)
SMEM = pl.BlockSpec(memory_space=pltpu.SMEM)
HBM = pl.BlockSpec(memory_space=pltpu.HBM)


def up8(rows):
    return -(-rows // 8) * 8


def sincos(angle):
    turns = jnp.floor(angle * (2.0 / math.pi) + 0.5)
    r = angle - turns * 1.5703125
    r = r - turns * 4.837512969970703125e-4
    r = r - turns * 7.54978995489188e-8
    r2 = r * r
    s = r + r * r2 * (-1.6666654611e-1 + r2 * (8.3321608736e-3 + r2 * -1.9515295891e-4))
    c = 1.0 - 0.5 * r2 + r2 * r2 * (
        4.166664568298827e-2 + r2 * (-1.388731625493765e-3 + r2 * 2.443315711809948e-5)
    )
    quarter = turns.astype(jnp.int32)
    odd = (quarter & 1) == 1
    sine = jnp.where(odd, c, s)
    cosine = jnp.where(odd, s, c)
    sine = jnp.where((quarter & 2) == 2, -sine, sine)
    cosine = jnp.where(((quarter + 1) & 2) == 2, -cosine, cosine)
    return sine, cosine


def split(values):
    high = values.astype(BF16)
    return high, (values - high.astype(F32)).astype(BF16)


def rows_iota(shape):
    return lax.broadcasted_iota(jnp.int32, shape, 0)


def lanes_iota(shape):
    return lax.broadcasted_iota(jnp.int32, shape, len(shape) - 1)


class Sizes:
    def __init__(self, block, directions, caps):
        self.gz, self.dev, self.xy = (lax.axis_size(a) for a in ("gz", "dev", "xy"))
        self.y, self.z, self.x = block
        self.both_y = self.dev > 2
        self.rows = self.y + HALO * (2 if self.both_y else 1)
        self.nx, self.ny, self.nz = self.x * self.xy, self.y * self.dev, self.z * self.gz
        self.dirs = directions
        self.tiles = directions // LANES
        self.table_rows = 2 * self.x + 2 * self.z
        self.walls = self.y * self.z // PATCH
        self.caps = caps
        self.share = caps // self.gz
        self.own_dirs = directions // (self.gz * self.dev * self.xy)
        self.chunk = up8(2 + self.share)
        self.far_rows = 4 * self.tiles
        self.norm = 1.0 / math.sqrt(2.0 * (2 * self.ny * self.nz + 2 * self.ny * self.nx))
        self.y_rows = 7 * HALO * self.z
        self.z_rows = up8(7 * self.y * HALO)
        self.e_rows = up8(7 * HALO * HALO)
        y_kinds = 2 if self.both_y else 1
        sizes = [self.y_rows] * y_kinds + [2 * self.z_rows] + [2 * self.e_rows] * y_kinds
        self.starts = [sum(sizes[:i]) for i in range(len(sizes))]
        self.halo_rows = sum(sizes)
        self.y_kinds = y_kinds


def pack_kernel(n, f_hbm, eps_hbm, own, *rest):
    y_outs, (eps_ref, sems) = rest[: n.y_kinds], rest[n.y_kinds :]
    copies = (
        pltpu.make_async_copy(f_hbm, own.at[0:6], sems.at[0]),
        pltpu.make_async_copy(eps_hbm, eps_ref, sems.at[1]),
    )
    for copy in copies:
        copy.start()
    for copy in copies:
        copy.wait()
    dev_even = lax.axis_index("dev") % 2 == 0
    for y in range(n.y):
        own[6, y] = COURANT / eps_ref[y]
    for c in range(7):
        at = [own[c, y] for y in range(n.y)]
        for kind in range(n.y_kinds):
            top = dev_even if kind == 0 else jnp.logical_not(dev_even)
            for r in range(HALO):
                value = jnp.where(top, at[n.y - HALO + r], at[r])
                y_outs[kind][pl.ds((c * HALO + r) * n.z, n.z), :] = value


def edge_kernel(n, own_ref, other_ref, z_out, *e_outs):
    xy = lax.axis_index("xy")
    dev_even = lax.axis_index("dev") % 2 == 0
    z_top = lax.axis_index("gz") % 2 == xy % 2
    for half in range(2):
        mine = xy == half

        def at(c, y):
            rows = pl.ds((c * n.y + y) * n.z, n.z)
            value = jnp.where(mine, own_ref[rows, :], other_ref[rows, :])
            return jnp.where(z_top, value[n.z - HALO :], value[:HALO])

        for c in range(7):
            edges = [at(c, y) for y in range(n.y)]
            for y in range(n.y):
                z_out[pl.ds(half * n.z_rows + (c * n.y + y) * HALO, HALO), :] = edges[y]
            for kind in range(n.y_kinds):
                top = dev_even if kind == 0 else jnp.logical_not(dev_even)
                for r in range(HALO):
                    edge = jnp.where(top, edges[n.y - HALO + r], edges[r])
                    e_outs[kind][pl.ds(half * n.e_rows + (c * HALO + r) * HALO, HALO), :] = edge


def table_kernel(
    n, dir_hbm, owner_hbm, wall_owner_hbm, phase_ref, hi_lo_ref, v_ref, place_ref, turn_ref,
    count_ref, dir_ref, owner_ref, wall_owner_ref, sems,
):
    gz, dev, xy = (lax.axis_index(a) for a in ("gz", "dev", "xy"))
    hi_ref, lo_ref = halves(n, hi_lo_ref)
    copies = [
        pltpu.make_async_copy(source, target, sems.at[i])
        for i, (source, target) in enumerate(
            (
                (dir_hbm, dir_ref),
                (owner_hbm, owner_ref),
                (wall_owner_hbm, wall_owner_ref),
            )
        )
    ]
    for copy in copies:
        copy.start()
    for copy in copies:
        copy.wait()
    index = dir_ref[...]
    bits = THETAS.bit_length() - 1
    polar = (index >> bits).astype(F32)
    azimuth = (index & (THETAS - 1)).astype(F32)
    sin_t, cos_t = sincos(math.pi * (polar + 0.5) / THETAS)
    sin_f, cos_f = sincos(2.0 * math.pi * azimuth / THETAS)
    kx = WAVE_NUMBER * (sin_t * cos_f)
    ky = WAVE_NUMBER * (sin_t * sin_f)
    kz = WAVE_NUMBER * cos_t
    theta = (cos_t * cos_f, cos_t * sin_f, -sin_t)
    phi = (-sin_f, cos_f, jnp.zeros_like(sin_f))
    is_end = jnp.logical_or(gz == 0, gz == n.gz - 1)
    cap_scale = jnp.where(is_end, n.norm, 0.0).astype(F32)
    x_first = (xy * n.x).astype(F32) - (n.nx - 1) / 2.0
    y_first = (dev * n.y).astype(F32) - (n.ny - 1) / 2.0
    z_first = (gz * n.z).astype(F32) - (n.nz - 1) / 2.0
    x_wall = x_first + jnp.where(xy == 0, XB, n.x - 1 - XB).astype(F32)
    z_cap = z_first + jnp.where(gz == 0, ZB, n.z - 1 - ZB).astype(F32)
    row8 = rows_iota((8, LANES))
    row16 = rows_iota((16, LANES))
    fine_x = row8.astype(F32)
    low = row8 < 4
    comp = row8 & 3

    def weights(rows):
        picked = jnp.where(comp == 2, rows[2], rows[3])
        return jnp.where(comp == 0, rows[0], jnp.where(comp == 1, rows[1], picked))

    for t in range(n.tiles):
        lanes = slice(t * LANES, (t + 1) * LANES)
        a, b, c = (v[t : t + 1, :] for v in (kx, ky, kz))
        th = [v[t : t + 1, :] for v in theta]
        ph = [v[t : t + 1, :] for v in phi]
        sf, cf = sincos(a * fine_x)
        for pair in range(n.x // 16):
            if pair % 8 == 0:
                base_x = x_first + 8.0 * 16.0 * (pair // 8)
                coarse_s, coarse_c = sincos(a * (row16.astype(F32) * 8.0 + base_x))
            cosine, sine = [], []
            for h in (2 * (pair % 8), 2 * (pair % 8) + 1):
                cc, cs = coarse_c[h : h + 1, :], coarse_s[h : h + 1, :]
                cosine.append(cc * cf - cs * sf)
                sine.append(cs * cf + cc * sf)
            for part, rows in ((0, cosine), (n.x, sine)):
                high, rest = split(jnp.concatenate(rows, axis=0))
                hi_ref[part + pair * 16 : part + pair * 16 + 16, lanes] = high
                lo_ref[part + pair * 16 : part + pair * 16 + 16, lanes] = rest
        zs, zc = sincos(c * (row16.astype(F32) + z_first))
        for part, rows in ((2 * n.x, zc), (2 * n.x + n.z, zs)):
            high, rest = split(rows)
            hi_ref[part : part + 16, lanes] = high
            lo_ref[part : part + 16, lanes] = rest
        y_of = comp.astype(F32) + y_first
        base_s, base_c = sincos(b * y_of + jnp.where(low, c * z_cap, a * x_wall))
        for face in range(2):
            i, j = ((0, 1), (1, 2))[face]
            scale = cap_scale if face == 0 else n.norm
            w_theta = weights([-th[i], -th[j], -ph[i], -ph[j]]) * scale
            w_phi = weights([-ph[i], -ph[j], th[i], th[j]]) * scale
            for kind, value in enumerate((w_theta, w_phi)):
                at = 16 * n.y + (face * 2 + kind) * 8
                v_ref[at : at + 8, lanes] = value
        for r in range(2 * n.y):
            factor = jnp.where(low, base_c[r : r + 1, :], -base_s[r : r + 1, :])
            v_ref[8 * r : 8 * r + 8, lanes] = factor
    for o in range(n.gz):
        count_ref[o] = 0
    which = jnp.where(gz == 0, 0, 1)

    def place(q, carry):
        owner = owner_ref[which, q]
        rank = count_ref[owner]
        count_ref[owner] = rank + 1
        place_ref[q] = owner * n.chunk + 2 + rank
        return carry

    lax.fori_loop(0, n.caps, place, 0)
    for j in range(n.walls):
        place_ref[n.caps + j] = wall_owner_ref[0, j]
    step_of = (row8 // 2).astype(F32)
    part_of = jnp.where((row8 & 1) == 0, 0.5, 1.0)
    sines, cosines = sincos(phase_ref[0] + ANGULAR_STEP * (step_of + part_of))
    turn_ref[0:8, :] = cosines
    turn_ref[8:16, :] = sines


def halves(n, hi_lo_ref):
    return hi_lo_ref.at[0 : n.table_rows], hi_lo_ref.at[n.table_rows : 2 * n.table_rows]


def block_transpose(values):
    row, block = rows_iota((8, LANES)), lanes_iota((8, LANES)) // PATCH
    for bit in (1, 2, 4):
        wide = PATCH * bit
        ahead = pltpu.roll(pltpu.roll(values, 8 - bit, 0), wide, 1)
        behind = pltpu.roll(pltpu.roll(values, bit, 0), LANES - wide, 1)
        row_bit, block_bit = (row & bit) != 0, (block & bit) != 0
        moved = jnp.where(row_bit, behind, ahead)
        values = jnp.where(row_bit == block_bit, values, moved)
    return values


def patch_factors(n, v_ref, face, lanes):
    at = [(face * n.y + y) * 8 for y in range(n.y)]
    return [v_ref[r : r + 8, lanes] for r in at]


def face_weights(n, v_ref, face, lanes):
    at = [16 * n.y + (face * 2 + kind) * 8 for kind in range(2)]
    return [v_ref[r : r + 8, lanes] for r in at]


def turn(values):
    swapped = pltpu.roll(values, 4, 0)
    return jnp.where(rows_iota(values.shape) < 4, -swapped, swapped)


def main_kernel(
    n, own_ref, other_ref, halo_ref, far_halo_ref, spectra_hbm, place_ref, turn_ref, hi_lo_ref, v_ref,
    fields_hbm, spectra_out_hbm, far_out, chunk_out, a_ref, m_ref, fields_out, spectra_out, sems,
):
    hi_ref, lo_ref = halves(n, hi_lo_ref)
    spectra_in = pltpu.make_async_copy(spectra_hbm, spectra_out, sems.at[0])
    spectra_in.start()
    gz, dev, xy = (lax.axis_index(a) for a in ("gz", "dev", "xy"))
    gz_even, dev_even = gz % 2 == 0, dev % 2 == 0
    deep = n.z + 8
    lo_ok, hi_ok = gz > 0, gz < n.gz - 1
    if n.both_y:
        y_own = HALO
        y_slots = (
            (0, jnp.logical_not(dev_even), dev > 0),
            (HALO + n.y, dev_even, dev < n.dev - 1),
        )
    else:
        y_own = jnp.where(dev_even, 0, HALO)
        y_slots = ((jnp.where(dev_even, n.y, 0), None, None),)
    pad = jnp.zeros((8 - 2 * HALO, LANES), F32)
    near_is_high = gz % 2 == xy % 2

    def choose(ref, starts, use_first, length):
        if use_first is None:
            return ref[pl.ds(starts[0], length), :]
        return jnp.where(
            use_first, ref[pl.ds(starts[0], length), :], ref[pl.ds(starts[1], length), :]
        )

    def rim(near, far):
        high = jnp.where(near_is_high, near, far)
        low = jnp.where(near_is_high, far, near)
        return jnp.concatenate(
            [jnp.where(hi_ok, high, 0.0), pad, jnp.where(lo_ok, low, 0.0)], axis=0
        )

    kinds = n.y_kinds
    both = (halo_ref, far_halo_ref)
    for half, (block, halo) in enumerate(((own_ref, halo_ref), (other_ref, far_halo_ref))):
        at_x = xy if half == 0 else 1 - xy
        lanes = pl.ds(pl.multiple_of(at_x * n.x, n.x), n.x)
        for c in range(7):
            for y in range(n.y):
                a_ref[c, y_own + y, 0 : n.z, lanes] = block[pl.ds((c * n.y + y) * n.z, n.z), :]
            for start, use_first, ok in y_slots:
                for r in range(HALO):
                    at = (c * HALO + r) * n.z
                    body = choose(halo, [n.starts[k] + at for k in range(kinds)], use_first, n.z)
                    if ok is not None:
                        body = jnp.where(ok, body, 0.0)
                    a_ref[c, start + r, 0 : n.z, lanes] = body
    for half in range(2):
        lanes = slice(half * n.x, (half + 1) * n.x)
        for c in range(7):
            for y in range(n.y):
                at = n.starts[kinds] + half * n.z_rows + (c * n.y + y) * HALO
                a_ref[c, y_own + y, n.z : deep, lanes] = rim(*(ref[pl.ds(at, HALO), :] for ref in both))
            for start, use_first, ok in y_slots:
                for r in range(HALO):
                    at = half * n.e_rows + (c * HALO + r) * HALO
                    starts = [n.starts[kinds + 1 + k] + at for k in range(kinds)]
                    edge = rim(*(choose(ref, starts, use_first, HALO) for ref in both))
                    if ok is not None:
                        edge = jnp.where(ok, edge, 0.0)
                    a_ref[c, start + r, n.z : deep, lanes] = edge

    shape = (deep, n.nx)
    z_row, x_lane = rows_iota(shape), lanes_iota(shape)
    keep = jnp.where(z_row < n.z + HALO, COURANT, jnp.where(lo_ok & (z_row >= deep - HALO), COURANT, 0.0))
    keep = keep.astype(F32)
    last_x, first_x = x_lane == n.nx - 1, x_lane == 0

    def z_next(v):
        return pltpu.roll(v, deep - 1, 0)

    def z_before(v):
        return pltpu.roll(v, 1, 0)

    def x_next(v):
        return jnp.where(last_x, 0.0, pltpu.roll(v, n.nx - 1, 1))

    def x_before(v):
        return jnp.where(first_x, 0.0, pltpu.roll(v, 1, 1))

    own_lanes = pl.ds(pl.multiple_of(xy * n.x, n.x), n.x)
    for step in range(STEPS):
        for y in range(n.rows):
            ex, ey, ez = (a_ref[c, y] for c in range(3))
            if y + 1 < n.rows:
                ex_y, ez_y = a_ref[0, y + 1] - ex, a_ref[2, y + 1] - ez
            else:
                ex_y, ez_y = -ex, -ez
            rate = keep
            if n.both_y and y < HALO:
                rate = jnp.where(dev == 0, 0.0, keep)
            a_ref[3, y] = a_ref[3, y] - rate * (ez_y - (z_next(ey) - ey))
            a_ref[4, y] = a_ref[4, y] - rate * ((z_next(ex) - ex) - (x_next(ez) - ez))
            a_ref[5, y] = a_ref[5, y] - rate * ((x_next(ey) - ey) - ex_y)
        for y in range(n.rows):
            hx, hy, hz = (a_ref[c, y] for c in range(3, 6))
            rate = a_ref[6, y]
            if y > 0:
                hx_y, hz_y = hx - a_ref[3, y - 1], hz - a_ref[5, y - 1]
            else:
                hx_y, hz_y = hx, hz
            a_ref[0, y] = a_ref[0, y] + rate * (hz_y - (hy - z_before(hy)))
            a_ref[1, y] = a_ref[1, y] + rate * ((hx - z_before(hx)) - (hz - x_before(hz)))
            a_ref[2, y] = a_ref[2, y] + rate * ((hy - x_before(hy)) - hx_y)
        if step == 0:
            spectra_in.wait()
        for c in range(6):
            row = 2 * step + (1 if c < 3 else 0)
            cosine, sine = turn_ref[row : row + 1, :], turn_ref[8 + row : 9 + row, :]
            for y in range(n.y):
                value = a_ref[c, y_own + y, 0 : n.z, own_lanes]
                spectra_out[c, y] = spectra_out[c, y] + value * cosine
                spectra_out[6 + c, y] = spectra_out[6 + c, y] - value * sine
                if step == STEPS - 1:
                    fields_out[c, y] = value

    copies = (
        pltpu.make_async_copy(fields_out, fields_hbm, sems.at[1]),
        pltpu.make_async_copy(spectra_out, spectra_out_hbm, sems.at[2]),
    )
    for copy in copies:
        copy.start()
    facing_x = jnp.where(xy == 0, -1.0, 1.0).astype(F32)
    facing_z = jnp.where(gz == 0, -1.0, 1.0).astype(F32)
    row8, lane = rows_iota((8, LANES)), lanes_iota((8, LANES))
    sign = jnp.where(((row8 & 3) == 0) | ((row8 & 3) == 3), -1.0, 1.0).astype(F32)
    own_block = lane // PATCH == row8
    block_sign = jnp.sum(jnp.where(own_block, sign, 0.0), axis=0, keepdims=True)
    cap_left, cap_right, wall_left = [], [], []
    chunk_out[...] = jnp.zeros_like(chunk_out)
    for y in range(n.y):
        plane = [
            jnp.where(gz == 0, spectra_out[p, y, ZB : ZB + 1, :], spectra_out[p, y, n.z - 1 - ZB : n.z - ZB, :])
            for p in [k + 6 * im for im in range(2) for k in Z_PICKS]
        ]
        current = jnp.concatenate(plane, axis=0) * (sign * facing_z)
        cap_left.append(current)
        cap_right.append(turn(current))
        m_ref[y * 8 : y * 8 + 8, :] = block_transpose(current)
        stack = jnp.concatenate(
            [spectra_out[k + 6 * im, y] for im in range(2) for k in X_PICKS], axis=0
        )
        across = stack.T
        record = jnp.where(xy == 0, across[XB : XB + 1, :], across[n.x - 1 - XB : n.x - XB, :])
        record = record * (block_sign * facing_x)
        for o in range(n.gz):
            mine = place_ref[n.caps + y] == o
            at = o * n.chunk
            chunk_out[at : at + 1, :] += jnp.where(mine, record, 0.0)
            chunk_out[at + 1 : at + 2, :] += jnp.where(mine, 1.0, 0.0).astype(F32)
        spread = jnp.where(own_block, record, 0.0)
        for wide in (16, 32, 64):
            spread = spread + pltpu.roll(spread, wide, 1)
        wall_left.append(jnp.where(lane < n.z, spread, turn(spread))[:, : 2 * n.z])
    for q in range(n.caps):
        chunk_out[pl.ds(place_ref[q], 1), :] = m_ref[q : q + 1, :]
    cap = jnp.concatenate(
        [jnp.concatenate(cap_left, axis=0), jnp.concatenate(cap_right, axis=0)], axis=1
    )
    wall = jnp.concatenate(wall_left, axis=0)
    dot = functools.partial(jnp.dot, preferred_element_type=F32)
    wide = min(512, n.dirs)
    for first in range(0, n.dirs, wide):
        sums = []
        for left, rows in ((cap, slice(0, 2 * n.x)), (wall, slice(2 * n.x, 2 * n.x + 2 * n.z))):
            left_hi, left_lo = split(left)
            high, rest = hi_ref[rows, first : first + wide], lo_ref[rows, first : first + wide]
            sums.append(dot(left_hi, high) + (dot(left_lo, high) + dot(left_hi, rest)))
        for t in range(wide // LANES):
            lanes = slice(first + t * LANES, first + (t + 1) * LANES)
            tile = first // LANES + t
            totals = [0.0] * 4
            for face in range(2):
                even, odd = 0.0, 0.0
                for y, factor in enumerate(patch_factors(n, v_ref, face, lanes)):
                    rows = sums[face][y * 8 : y * 8 + 8, t * LANES : (t + 1) * LANES]
                    even = even + factor * rows
                    odd = odd - factor * turn(rows)
                w_theta, w_phi = face_weights(n, v_ref, face, lanes)
                for kind, term in enumerate((w_theta * even, w_phi * even, w_theta * odd, w_phi * odd)):
                    totals[kind] = totals[kind] + term
            for kind, total in enumerate(totals):
                at = kind * n.tiles + tile
                far_out[at : at + 1, :] = jnp.sum(total, axis=0, keepdims=True)
    for copy in copies:
        copy.wait()


def adjoint_kernel(
    n, far_ref, target_ref, mask_ref, hi_lo_ref, v_ref, intensity_out, owned_out, adjoint_out, all_ref
):
    hi_ref, lo_ref = halves(n, hi_lo_ref)
    gz, dev, xy = (lax.axis_index(a) for a in ("gz", "dev", "xy"))
    block = n.far_rows + n.chunk
    parts = []
    for kind in range(4):
        total = None
        for k in range(n.gz):
            at = (n.gz - 1 - k) * block + kind * n.tiles
            term = far_ref[at : at + n.tiles, :]
            total = term if total is None else total + term
        parts.append(total)
    theta_re, phi_re, theta_im, phi_im = parts
    intensity = theta_re * theta_re + theta_im * theta_im + phi_re * phi_re + phi_im * phi_im
    if n.own_dirs % LANES == 0:
        all_ref[...] = intensity
        first = ((gz * n.dev + dev) * n.xy + xy) * (n.own_dirs // LANES)
        intensity_out[...] = all_ref[pl.ds(first, n.own_dirs // LANES), :]
    else:
        intensity_out[...] = intensity
    slope = 2.0 * (mask_ref[...].astype(F32) * (intensity - target_ref[...]))
    slopes = [slope * part for part in parts]

    faces = [[], []]
    for face in range(2):
        for t in range(n.tiles):
            lanes = slice(t * LANES, (t + 1) * LANES)
            w_theta, w_phi = face_weights(n, v_ref, face, lanes)
            even, odd = (
                w_theta * slopes[k][t : t + 1, :] + w_phi * slopes[k + 1][t : t + 1, :] for k in (0, 2)
            )
            rows = [
                factor * even + turn(factor * odd) for factor in patch_factors(n, v_ref, face, lanes)
            ]
            faces[face].append(jnp.concatenate(rows, axis=0))
    dot = functools.partial(
        lax.dot_general,
        dimension_numbers=(((1,), (1,)), ((), ())),
        preferred_element_type=F32,
    )
    sums = []
    for face, rows in ((0, slice(0, 2 * n.x)), (1, slice(2 * n.x, 2 * n.x + 2 * n.z))):
        left_hi, left_lo = split(jnp.concatenate(faces[face], axis=1))
        high, rest = hi_ref[rows, :], lo_ref[rows, :]
        sums.append(dot(left_hi, high) + (dot(left_lo, high) + dot(left_hi, rest)))
    cap, wall = sums
    row8, lane = rows_iota((8, LANES)), lanes_iota((8, LANES))
    own_block = lane // PATCH == row8
    for y in range(n.y):
        at = slice(y * 8, y * 8 + 8)
        gradient = cap[at, : n.x] - turn(cap[at, n.x :])
        adjoint_out[n.walls + y * 8 : n.walls + y * 8 + 8, 0, :] = block_transpose(gradient)
        gradient = wall[at, : n.z] - turn(wall[at, n.z :])
        spread = jnp.concatenate([gradient] * (LANES // n.z), axis=1)
        adjoint_out[y, :, :] = jnp.sum(
            jnp.where(own_block, spread, 0.0), axis=0, keepdims=True
        )
    walls = [jnp.zeros((1, LANES), F32) for _ in range(n.walls)]
    rank = jnp.zeros((1, LANES), F32)
    for s in range(n.gz):
        at = pl.multiple_of((n.gz - 1 - (gz ^ s)) * block + n.far_rows, 8)
        rows = far_ref[pl.ds(at, 8), :]
        record, flag = rows[0:1, :], rows[1:2, :] > 0.5
        for r in range(n.walls):
            walls[r] = jnp.where(flag & (rank == float(r)), record, walls[r])
        rank = rank + rows[1:2, :]
    for r in range(n.walls):
        owned_out[r, :, :] = walls[r]
    for cap_at, s in enumerate((0, n.gz - 1)):
        at = pl.multiple_of((n.gz - 1 - (gz ^ s)) * block + n.far_rows, 8)
        rows = far_ref[pl.ds(at, n.chunk), :]
        owned_out[n.walls + cap_at * n.share : n.walls + (cap_at + 1) * n.share, 0, :] = rows[2 : 2 + n.share, :]


def partner(kind, i, n):
    up = (i % 2 == 0) == (kind == 0)
    return (i + 1) % n if up else (i - 1) % n


def exchange(values, axes, image):
    sizes = [lax.axis_size(a) for a in axes]
    pairs = []
    for source in range(math.prod(sizes)):
        rest, where = source, []
        for size in reversed(sizes):
            where.insert(0, rest % size)
            rest //= size
        target = 0
        for size, at in zip(sizes, image(*where)):
            target = target * size + at
        pairs.append((source, target))
    return lax.ppermute(values, axes if len(axes) > 1 else axes[0], pairs)


def local(
    fields, spectra, permittivity, phase_start, wall_owner, cap_owner, dir_index, target, aim_mask
):
    n = Sizes(permittivity.shape, dir_index.shape[0], cap_owner.shape[1])
    gz = lax.axis_index("gz")

    def out(*shape, dtype=F32):
        return jax.ShapeDtypeStruct(shape, dtype)

    def far_memory(values):
        return pltpu.with_memory_space_constraint(values, pltpu.HBM)

    def params(mebibytes):
        return pltpu.CompilerParams(vmem_limit_bytes=mebibytes << 20)

    block = tuple(permittivity.shape)
    own, *y_send = pl.pallas_call(
        functools.partial(pack_kernel, n),
        name="pack",
        out_shape=[out(7, *block)] + [out(n.y_rows, n.x)] * n.y_kinds,
        in_specs=[HBM] * 2,
        out_specs=[VMEM] * (1 + n.y_kinds),
        scratch_shapes=[pltpu.VMEM(block, F32), pltpu.SemaphoreType.DMA((2,))],
        compiler_params=params(4),
    )(far_memory(fields), far_memory(permittivity))
    own = own.reshape(7 * n.y * n.z, n.x)
    y_got = [
        exchange(v, ("dev",), lambda d, k=k: (partner(k, d, n.dev),)) for k, v in enumerate(y_send)
    ]
    other = exchange(own, ("xy",), lambda x: (x ^ 1,))
    z_send, *e_send = pl.pallas_call(
        functools.partial(edge_kernel, n),
        name="edges",
        out_shape=[out(2 * n.z_rows, n.x)] + [out(2 * n.e_rows, n.x)] * n.y_kinds,
        in_specs=[VMEM] * 2,
        out_specs=[VMEM] * (1 + n.y_kinds),
        compiler_params=params(4),
    )(own, other)
    z_got = exchange(z_send, ("gz", "xy"), lambda g, x: (partner(x, g, n.gz), x))
    e_got = [
        exchange(
            v,
            ("gz", "dev", "xy"),
            lambda g, d, x, k=k: (partner(x, g, n.gz), partner(k, d, n.dev), x),
        )
        for k, v in enumerate(e_send)
    ]

    table, v, place, turns = pl.pallas_call(
        functools.partial(table_kernel, n),
        name="tables",
        out_shape=[
            out(2 * n.table_rows, n.dirs, dtype=BF16),
            out(16 * n.y + 32, n.dirs),
            out(n.caps + n.walls, dtype=jnp.int32),
            out(16, LANES),
        ],
        in_specs=[HBM] * 3 + [SMEM],
        out_specs=[VMEM] * 2 + [SMEM, VMEM],
        scratch_shapes=[
            pltpu.SMEM((n.gz,), jnp.int32),
            pltpu.VMEM((n.tiles, LANES), jnp.int32),
            pltpu.SMEM(cap_owner.shape, jnp.int32),
            pltpu.SMEM(wall_owner.shape, jnp.int32),
            pltpu.SemaphoreType.DMA((3,)),
        ],
        compiler_params=params(8),
        cost_estimate=pl.CostEstimate(flops=1 << 33, bytes_accessed=16 << 20, transcendentals=0),
    )(*map(far_memory, (dir_index.reshape(n.tiles, LANES), cap_owner, wall_owner)), phase_start)
    (*y_got, z_got, turns), e_got = lax.optimization_barrier(((*y_got, z_got, turns), e_got))
    halo = jnp.concatenate([*y_got, z_got, *e_got])
    far_halo = exchange(halo, ("xy",), lambda x: (x ^ 1,))

    anywhere = pl.BlockSpec(memory_space=pl.ANY)
    fields_out, spectra_out, far, chunk = pl.pallas_call(
        functools.partial(main_kernel, n),
        name="window",
        out_shape=[
            out(6, *block),
            out(12, *block),
            out(n.far_rows, LANES),
            out(n.gz * n.chunk, LANES),
        ],
        in_specs=[VMEM] * 4 + [anywhere, SMEM] + [VMEM] * 3,
        out_specs=[anywhere] * 2 + [VMEM] * 2,
        scratch_shapes=[
            pltpu.VMEM((7, n.rows, n.z + 8, n.nx), F32),
            pltpu.VMEM((n.caps, LANES), F32),
            pltpu.VMEM((6, *block), F32),
            pltpu.VMEM((12, *block), F32),
            pltpu.SemaphoreType.DMA((3,)),
        ],
        compiler_params=params(12),
    )(own, other, halo, far_halo, spectra, place, turns, table, v)

    for axis in ("xy", "dev"):
        size = lax.axis_size(axis)
        got = [exchange(far, (axis,), lambda i, k=k: (i ^ k,)) for k in range(1, size)]
        for term in got:
            far = far + term
    payload = [
        jnp.concatenate([far, lax.dynamic_slice_in_dim(chunk, (gz ^ k) * n.chunk, n.chunk)])
        for k in range(n.gz)
    ]
    got = [
        exchange(payload[k], ("gz",), lambda g, k=k: (g ^ k,)) for k in range(n.gz - 1, 0, -1)
    ]
    gathered = jnp.concatenate([*got, payload[0]])

    sliced = n.own_dirs % LANES == 0
    intensity, owned, adjoint = pl.pallas_call(
        functools.partial(adjoint_kernel, n),
        name="adjoint",
        out_shape=[
            out(n.own_dirs // LANES if sliced else n.tiles, LANES),
            out(n.walls + 2 * n.share, 1, LANES),
            out(n.walls + n.caps, 1, LANES),
        ],
        in_specs=[VMEM] * 5,
        out_specs=[VMEM] * 3,
        scratch_shapes=[pltpu.VMEM((n.tiles, LANES), F32)],
        compiler_params=params(8),
    )(gathered, target.reshape(n.tiles, LANES), aim_mask.reshape(n.tiles, LANES), table, v)
    intensity = intensity.reshape(-1)
    if not sliced:
        joined = (gz * n.dev + lax.axis_index("dev")) * n.xy + lax.axis_index("xy")
        intensity = lax.dynamic_slice_in_dim(intensity, joined * n.own_dirs, n.own_dirs)
    shape = (1, 1, 1, -1, LANES)
    return fields_out, spectra_out, owned.reshape(shape), intensity, adjoint.reshape(shape)


def solution(mesh):
    placed = (
        P("groups", "dev", "gz", "xy"),
        P("groups", "dev", "gz", "xy"),
        P(("groups", "dev"), "gz", "xy"),
        P("groups"),
        P("gz", None),
        P(),
        P(),
        P("groups"),
        P("groups"),
    )
    return jax.shard_map(
        local,
        mesh=mesh,
        in_specs=placed,
        out_specs=(
            P("groups", "dev", "gz", "xy"),
            P("groups", "dev", "gz", "xy"),
            P(("groups", "gz"), "dev", "xy", None, None),
            P(("groups", "gz", "dev", "xy")),
            P(("groups", "gz"), "dev", "xy", None, None),
        ),
        check_vma=False,
    )
```

```python
import functools
import math

import jax
import jax.numpy as jnp
from jax import lax
from jax.experimental import pallas as pl
from jax.experimental.pallas import tpu as pltpu
from jax.sharding import PartitionSpec as P

PATCH = 16
XB = 8
ZB = 4
STEPS = 3
THETAS = 64
COURANT = 0.5
ANGULAR_STEP = 0.3
WAVE_NUMBER = 0.6
CURRENT_SIGNS = (-1.0, 1.0, 1.0, -1.0)
X_PICKS = (5, 4, 2, 1)
Z_PICKS = (4, 3, 1, 0)
LANES = 128
HALO = STEPS
F32 = jnp.float32
BF16 = jnp.bfloat16
VMEM = pl.BlockSpec(memory_space=pltpu.VMEM)
SMEM = pl.BlockSpec(memory_space=pltpu.SMEM)
HBM = pl.BlockSpec(memory_space=pltpu.HBM)


def up8(rows):
    return -(-rows // 8) * 8


def sincos(angle):
    turns = jnp.floor(angle * (2.0 / math.pi) + 0.5)
    r = angle - turns * 1.5703125
    r = r - turns * 4.837512969970703125e-4
    r = r - turns * 7.54978995489188e-8
    r2 = r * r
    s = r + r * r2 * (-1.6666654611e-1 + r2 * (8.3321608736e-3 + r2 * -1.9515295891e-4))
    c = 1.0 - 0.5 * r2 + r2 * r2 * (
        4.166664568298827e-2 + r2 * (-1.388731625493765e-3 + r2 * 2.443315711809948e-5)
    )
    quarter = turns.astype(jnp.int32)
    odd = (quarter & 1) == 1
    sine = jnp.where(odd, c, s)
    cosine = jnp.where(odd, s, c)
    sine = jnp.where((quarter & 2) == 2, -sine, sine)
    cosine = jnp.where(((quarter + 1) & 2) == 2, -cosine, cosine)
    return sine, cosine


def split(values):
    high = values.astype(BF16)
    return high, (values - high.astype(F32)).astype(BF16)


def rows_iota(shape):
    return lax.broadcasted_iota(jnp.int32, shape, 0)


def lanes_iota(shape):
    return lax.broadcasted_iota(jnp.int32, shape, len(shape) - 1)


class Sizes:
    def __init__(self, block, directions, caps):
        self.gz, self.dev, self.xy = (lax.axis_size(a) for a in ("gz", "dev", "xy"))
        self.y, self.z, self.x = block
        self.both_y = self.dev > 2
        self.rows = self.y + HALO * (2 if self.both_y else 1)
        self.nx, self.ny, self.nz = self.x * self.xy, self.y * self.dev, self.z * self.gz
        self.dirs = directions
        self.tiles = directions // LANES
        self.table_rows = 2 * self.x + 2 * self.z
        self.walls = self.y * self.z // PATCH
        self.caps = caps
        self.share = caps // self.gz
        self.own_dirs = directions // (self.gz * self.dev * self.xy)
        self.chunk = up8(2 + self.share)
        self.far_rows = 4 * self.tiles
        self.norm = 1.0 / math.sqrt(2.0 * (2 * self.ny * self.nz + 2 * self.ny * self.nx))
        self.y_rows = 7 * HALO * self.z
        self.z_rows = up8(7 * self.y * HALO)
        self.e_rows = up8(7 * HALO * HALO)
        y_kinds = 2 if self.both_y else 1
        sizes = [self.y_rows] * y_kinds + [2 * self.z_rows] + [2 * self.e_rows] * y_kinds
        self.starts = [sum(sizes[:i]) for i in range(len(sizes))]
        self.halo_rows = sum(sizes)
        self.y_kinds = y_kinds


def pack_kernel(n, f_hbm, eps_hbm, own, *rest):
    y_outs, (eps_ref, sems) = rest[: n.y_kinds], rest[n.y_kinds :]
    copies = (
        pltpu.make_async_copy(f_hbm, own.at[0:6], sems.at[0]),
        pltpu.make_async_copy(eps_hbm, eps_ref, sems.at[1]),
    )
    for copy in copies:
        copy.start()
    for copy in copies:
        copy.wait()
    dev_even = lax.axis_index("dev") % 2 == 0
    for y in range(n.y):
        own[6, y] = COURANT / eps_ref[y]
    for c in range(7):
        at = [own[c, y] for y in range(n.y)]
        for kind in range(n.y_kinds):
            top = dev_even if kind == 0 else jnp.logical_not(dev_even)
            for r in range(HALO):
                value = jnp.where(top, at[n.y - HALO + r], at[r])
                y_outs[kind][pl.ds((c * HALO + r) * n.z, n.z), :] = value


def edge_kernel(n, own_ref, other_ref, z_out, *e_outs):
    xy = lax.axis_index("xy")
    dev_even = lax.axis_index("dev") % 2 == 0
    z_top = lax.axis_index("gz") % 2 == xy % 2
    for half in range(2):
        mine = xy == half

        def at(c, y):
            rows = pl.ds((c * n.y + y) * n.z, n.z)
            value = jnp.where(mine, own_ref[rows, :], other_ref[rows, :])
            return jnp.where(z_top, value[n.z - HALO :], value[:HALO])

        for c in range(7):
            edges = [at(c, y) for y in range(n.y)]
            for y in range(n.y):
                z_out[pl.ds(half * n.z_rows + (c * n.y + y) * HALO, HALO), :] = edges[y]
            for kind in range(n.y_kinds):
                top = dev_even if kind == 0 else jnp.logical_not(dev_even)
                for r in range(HALO):
                    edge = jnp.where(top, edges[n.y - HALO + r], edges[r])
                    e_outs[kind][pl.ds(half * n.e_rows + (c * HALO + r) * HALO, HALO), :] = edge


def table_kernel(
    n, dir_hbm, owner_hbm, wall_owner_hbm, hi_lo_ref, v_ref, place_ref,
    count_ref, dir_ref, owner_ref, wall_owner_ref, sems,
):
    gz, dev, xy = (lax.axis_index(a) for a in ("gz", "dev", "xy"))
    hi_ref, lo_ref = halves(n, hi_lo_ref)
    copies = [
        pltpu.make_async_copy(source, target, sems.at[i])
        for i, (source, target) in enumerate(
            (
                (dir_hbm, dir_ref),
                (owner_hbm, owner_ref),
                (wall_owner_hbm, wall_owner_ref),
            )
        )
    ]
    for copy in copies:
        copy.start()
    for copy in copies:
        copy.wait()
    index = dir_ref[...]
    bits = THETAS.bit_length() - 1
    polar = (index >> bits).astype(F32)
    azimuth = (index & (THETAS - 1)).astype(F32)
    sin_t, cos_t = sincos(math.pi * (polar + 0.5) / THETAS)
    sin_f, cos_f = sincos(2.0 * math.pi * azimuth / THETAS)
    kx = WAVE_NUMBER * (sin_t * cos_f)
    ky = WAVE_NUMBER * (sin_t * sin_f)
    kz = WAVE_NUMBER * cos_t
    theta = (cos_t * cos_f, cos_t * sin_f, -sin_t)
    phi = (-sin_f, cos_f, jnp.zeros_like(sin_f))
    is_end = jnp.logical_or(gz == 0, gz == n.gz - 1)
    cap_scale = jnp.where(is_end, n.norm, 0.0).astype(F32)
    x_first = (xy * n.x).astype(F32) - (n.nx - 1) / 2.0
    y_first = (dev * n.y).astype(F32) - (n.ny - 1) / 2.0
    z_first = (gz * n.z).astype(F32) - (n.nz - 1) / 2.0
    x_wall = x_first + jnp.where(xy == 0, XB, n.x - 1 - XB).astype(F32)
    z_cap = z_first + jnp.where(gz == 0, ZB, n.z - 1 - ZB).astype(F32)
    row8 = rows_iota((8, LANES))
    row16 = rows_iota((16, LANES))
    fine_x = row8.astype(F32)
    low = row8 < 4
    comp = row8 & 3

    def weights(rows):
        picked = jnp.where(comp == 2, rows[2], rows[3])
        return jnp.where(comp == 0, rows[0], jnp.where(comp == 1, rows[1], picked))

    for t in range(n.tiles):
        lanes = slice(t * LANES, (t + 1) * LANES)
        a, b, c = (v[t : t + 1, :] for v in (kx, ky, kz))
        th = [v[t : t + 1, :] for v in theta]
        ph = [v[t : t + 1, :] for v in phi]
        sf, cf = sincos(a * fine_x)
        for pair in range(n.x // 16):
            if pair % 8 == 0:
                base_x = x_first + 8.0 * 16.0 * (pair // 8)
                coarse_s, coarse_c = sincos(a * (row16.astype(F32) * 8.0 + base_x))
            cosine, sine = [], []
            for h in (2 * (pair % 8), 2 * (pair % 8) + 1):
                cc, cs = coarse_c[h : h + 1, :], coarse_s[h : h + 1, :]
                cosine.append(cc * cf - cs * sf)
                sine.append(cs * cf + cc * sf)
            for part, rows in ((0, cosine), (n.x, sine)):
                high, rest = split(jnp.concatenate(rows, axis=0))
                hi_ref[part + pair * 16 : part + pair * 16 + 16, lanes] = high
                lo_ref[part + pair * 16 : part + pair * 16 + 16, lanes] = rest
        zs, zc = sincos(c * (row16.astype(F32) + z_first))
        for part, rows in ((2 * n.x, zc), (2 * n.x + n.z, zs)):
            high, rest = split(rows)
            hi_ref[part : part + 16, lanes] = high
            lo_ref[part : part + 16, lanes] = rest
        y_of = comp.astype(F32) + y_first
        base_s, base_c = sincos(b * y_of + jnp.where(low, c * z_cap, a * x_wall))
        for face in range(2):
            i, j = ((0, 1), (1, 2))[face]
            scale = cap_scale if face == 0 else n.norm
            w_theta = weights([-th[i], -th[j], -ph[i], -ph[j]]) * scale
            w_phi = weights([-ph[i], -ph[j], th[i], th[j]]) * scale
            for kind, value in enumerate((w_theta, w_phi)):
                at = 16 * n.y + (face * 2 + kind) * 8
                v_ref[at : at + 8, lanes] = value
        for r in range(2 * n.y):
            factor = jnp.where(low, base_c[r : r + 1, :], -base_s[r : r + 1, :])
            v_ref[8 * r : 8 * r + 8, lanes] = factor
    for o in range(n.gz):
        count_ref[o] = 0
    which = jnp.where(gz == 0, 0, 1)

    def place(q, carry):
        owner = owner_ref[which, q]
        rank = count_ref[owner]
        count_ref[owner] = rank + 1
        place_ref[q] = owner * n.chunk + 2 + rank
        return carry

    lax.fori_loop(0, n.caps, place, 0)
    for j in range(n.walls):
        place_ref[n.caps + j] = wall_owner_ref[0, j]


def halves(n, hi_lo_ref):
    return hi_lo_ref.at[0 : n.table_rows], hi_lo_ref.at[n.table_rows : 2 * n.table_rows]


def block_transpose(values):
    row, block = rows_iota((8, LANES)), lanes_iota((8, LANES)) // PATCH
    for bit in (1, 2, 4):
        wide = PATCH * bit
        ahead = pltpu.roll(pltpu.roll(values, 8 - bit, 0), wide, 1)
        behind = pltpu.roll(pltpu.roll(values, bit, 0), LANES - wide, 1)
        row_bit, block_bit = (row & bit) != 0, (block & bit) != 0
        moved = jnp.where(row_bit, behind, ahead)
        values = jnp.where(row_bit == block_bit, values, moved)
    return values


def patch_factors(n, v_ref, face, lanes):
    at = [(face * n.y + y) * 8 for y in range(n.y)]
    return [v_ref[r : r + 8, lanes] for r in at]


def face_weights(n, v_ref, face, lanes):
    at = [16 * n.y + (face * 2 + kind) * 8 for kind in range(2)]
    return [v_ref[r : r + 8, lanes] for r in at]


def turn(values):
    swapped = pltpu.roll(values, 4, 0)
    return jnp.where(rows_iota(values.shape) < 4, -swapped, swapped)


def main_kernel(
    n, own_ref, other_ref, halo_ref, far_halo_ref, spectra_hbm, place_ref, phase_ref, hi_lo_ref, v_ref,
    fields_hbm, spectra_out_hbm, far_out, chunk_out, a_ref, m_ref, fields_out, spectra_out, sems,
):
    hi_ref, lo_ref = halves(n, hi_lo_ref)
    spectra_in = pltpu.make_async_copy(spectra_hbm, spectra_out, sems.at[0])
    spectra_in.start()
    gz, dev, xy = (lax.axis_index(a) for a in ("gz", "dev", "xy"))
    gz_even, dev_even = gz % 2 == 0, dev % 2 == 0
    deep = n.z + 8
    lo_ok, hi_ok = gz > 0, gz < n.gz - 1
    if n.both_y:
        y_own = HALO
        y_slots = (
            (0, jnp.logical_not(dev_even), dev > 0),
            (HALO + n.y, dev_even, dev < n.dev - 1),
        )
    else:
        y_own = jnp.where(dev_even, 0, HALO)
        y_slots = ((jnp.where(dev_even, n.y, 0), None, None),)
    pad = jnp.zeros((8 - 2 * HALO, LANES), F32)
    near_is_high = gz % 2 == xy % 2

    def choose(ref, starts, use_first, length):
        if use_first is None:
            return ref[pl.ds(starts[0], length), :]
        return jnp.where(
            use_first, ref[pl.ds(starts[0], length), :], ref[pl.ds(starts[1], length), :]
        )

    def rim(near, far):
        high = jnp.where(near_is_high, near, far)
        low = jnp.where(near_is_high, far, near)
        return jnp.concatenate(
            [jnp.where(hi_ok, high, 0.0), pad, jnp.where(lo_ok, low, 0.0)], axis=0
        )

    kinds = n.y_kinds
    both = (halo_ref, far_halo_ref)
    for half, (block, halo) in enumerate(((own_ref, halo_ref), (other_ref, far_halo_ref))):
        at_x = xy if half == 0 else 1 - xy
        lanes = pl.ds(pl.multiple_of(at_x * n.x, n.x), n.x)
        for c in range(7):
            for y in range(n.y):
                a_ref[c, y_own + y, 0 : n.z, lanes] = block[pl.ds((c * n.y + y) * n.z, n.z), :]
            for start, use_first, ok in y_slots:
                for r in range(HALO):
                    at = (c * HALO + r) * n.z
                    body = choose(halo, [n.starts[k] + at for k in range(kinds)], use_first, n.z)
                    if ok is not None:
                        body = jnp.where(ok, body, 0.0)
                    a_ref[c, start + r, 0 : n.z, lanes] = body
    for half in range(2):
        lanes = slice(half * n.x, (half + 1) * n.x)
        for c in range(7):
            for y in range(n.y):
                at = n.starts[kinds] + half * n.z_rows + (c * n.y + y) * HALO
                a_ref[c, y_own + y, n.z : deep, lanes] = rim(*(ref[pl.ds(at, HALO), :] for ref in both))
            for start, use_first, ok in y_slots:
                for r in range(HALO):
                    at = half * n.e_rows + (c * HALO + r) * HALO
                    starts = [n.starts[kinds + 1 + k] + at for k in range(kinds)]
                    edge = rim(*(choose(ref, starts, use_first, HALO) for ref in both))
                    if ok is not None:
                        edge = jnp.where(ok, edge, 0.0)
                    a_ref[c, start + r, n.z : deep, lanes] = edge

    shape = (deep, n.nx)
    z_row, x_lane = rows_iota(shape), lanes_iota(shape)
    keep = jnp.where(z_row < n.z + HALO, COURANT, jnp.where(lo_ok & (z_row >= deep - HALO), COURANT, 0.0))
    keep = keep.astype(F32)
    last_x, first_x = x_lane == n.nx - 1, x_lane == 0

    def z_next(v):
        return pltpu.roll(v, deep - 1, 0)

    def z_before(v):
        return pltpu.roll(v, 1, 0)

    def x_next(v):
        return jnp.where(last_x, 0.0, pltpu.roll(v, n.nx - 1, 1))

    def x_before(v):
        return jnp.where(first_x, 0.0, pltpu.roll(v, 1, 1))

    own_lanes = pl.ds(pl.multiple_of(xy * n.x, n.x), n.x)
    angle_row = rows_iota((8, LANES))
    step_of = (angle_row // 2).astype(F32)
    part_of = jnp.where((angle_row & 1) == 0, 0.5, 1.0)
    sines, cosines = sincos(phase_ref[0] + ANGULAR_STEP * (step_of + part_of))
    for step in range(STEPS):
        for y in range(n.rows):
            ex, ey, ez = (a_ref[c, y] for c in range(3))
            if y + 1 < n.rows:
                ex_y, ez_y = a_ref[0, y + 1] - ex, a_ref[2, y + 1] - ez
            else:
                ex_y, ez_y = -ex, -ez
            rate = keep
            if n.both_y and y < HALO:
                rate = jnp.where(dev == 0, 0.0, keep)
            a_ref[3, y] = a_ref[3, y] - rate * (ez_y - (z_next(ey) - ey))
            a_ref[4, y] = a_ref[4, y] - rate * ((z_next(ex) - ex) - (x_next(ez) - ez))
            a_ref[5, y] = a_ref[5, y] - rate * ((x_next(ey) - ey) - ex_y)
        for y in range(n.rows):
            hx, hy, hz = (a_ref[c, y] for c in range(3, 6))
            rate = a_ref[6, y]
            if y > 0:
                hx_y, hz_y = hx - a_ref[3, y - 1], hz - a_ref[5, y - 1]
            else:
                hx_y, hz_y = hx, hz
            a_ref[0, y] = a_ref[0, y] + rate * (hz_y - (hy - z_before(hy)))
            a_ref[1, y] = a_ref[1, y] + rate * ((hx - z_before(hx)) - (hz - x_before(hz)))
            a_ref[2, y] = a_ref[2, y] + rate * ((hy - x_before(hy)) - hx_y)
        if step == 0:
            spectra_in.wait()
        for c in range(6):
            row = 2 * step + (1 if c < 3 else 0)
            cosine, sine = cosines[row : row + 1, :], sines[row : row + 1, :]
            for y in range(n.y):
                value = a_ref[c, y_own + y, 0 : n.z, own_lanes]
                spectra_out[c, y] = spectra_out[c, y] + value * cosine
                spectra_out[6 + c, y] = spectra_out[6 + c, y] - value * sine
                if step == STEPS - 1:
                    fields_out[c, y] = value

    copies = (
        pltpu.make_async_copy(fields_out, fields_hbm, sems.at[1]),
        pltpu.make_async_copy(spectra_out, spectra_out_hbm, sems.at[2]),
    )
    for copy in copies:
        copy.start()
    facing_x = jnp.where(xy == 0, -1.0, 1.0).astype(F32)
    facing_z = jnp.where(gz == 0, -1.0, 1.0).astype(F32)
    row8, lane = rows_iota((8, LANES)), lanes_iota((8, LANES))
    sign = jnp.where(((row8 & 3) == 0) | ((row8 & 3) == 3), -1.0, 1.0).astype(F32)
    own_block = lane // PATCH == row8
    block_sign = jnp.sum(jnp.where(own_block, sign, 0.0), axis=0, keepdims=True)
    cap_left, cap_right, wall_left = [], [], []
    chunk_out[...] = jnp.zeros_like(chunk_out)
    for y in range(n.y):
        plane = [
            jnp.where(gz == 0, spectra_out[p, y, ZB : ZB + 1, :], spectra_out[p, y, n.z - 1 - ZB : n.z - ZB, :])
            for p in [k + 6 * im for im in range(2) for k in Z_PICKS]
        ]
        current = jnp.concatenate(plane, axis=0) * (sign * facing_z)
        cap_left.append(current)
        cap_right.append(turn(current))
        m_ref[y * 8 : y * 8 + 8, :] = block_transpose(current)
        stack = jnp.concatenate(
            [spectra_out[k + 6 * im, y] for im in range(2) for k in X_PICKS], axis=0
        )
        across = stack.T
        record = jnp.where(xy == 0, across[XB : XB + 1, :], across[n.x - 1 - XB : n.x - XB, :])
        record = record * (block_sign * facing_x)
        for o in range(n.gz):
            mine = place_ref[n.caps + y] == o
            at = o * n.chunk
            chunk_out[at : at + 1, :] += jnp.where(mine, record, 0.0)
            chunk_out[at + 1 : at + 2, :] += jnp.where(mine, 1.0, 0.0).astype(F32)
        spread = jnp.where(own_block, record, 0.0)
        for wide in (16, 32, 64):
            spread = spread + pltpu.roll(spread, wide, 1)
        wall_left.append(jnp.where(lane < n.z, spread, turn(spread))[:, : 2 * n.z])
    for q in range(n.caps):
        chunk_out[pl.ds(place_ref[q], 1), :] = m_ref[q : q + 1, :]
    cap = jnp.concatenate(
        [jnp.concatenate(cap_left, axis=0), jnp.concatenate(cap_right, axis=0)], axis=1
    )
    wall = jnp.concatenate(wall_left, axis=0)
    dot = functools.partial(jnp.dot, preferred_element_type=F32)
    wide = min(512, n.dirs)
    for first in range(0, n.dirs, wide):
        sums = []
        for left, rows in ((cap, slice(0, 2 * n.x)), (wall, slice(2 * n.x, 2 * n.x + 2 * n.z))):
            left_hi, left_lo = split(left)
            high, rest = hi_ref[rows, first : first + wide], lo_ref[rows, first : first + wide]
            sums.append(dot(left_hi, high) + (dot(left_lo, high) + dot(left_hi, rest)))
        for t in range(wide // LANES):
            lanes = slice(first + t * LANES, first + (t + 1) * LANES)
            tile = first // LANES + t
            totals = [0.0] * 4
            for face in range(2):
                even, odd = 0.0, 0.0
                for y, factor in enumerate(patch_factors(n, v_ref, face, lanes)):
                    rows = sums[face][y * 8 : y * 8 + 8, t * LANES : (t + 1) * LANES]
                    even = even + factor * rows
                    odd = odd - factor * turn(rows)
                w_theta, w_phi = face_weights(n, v_ref, face, lanes)
                for kind, term in enumerate((w_theta * even, w_phi * even, w_theta * odd, w_phi * odd)):
                    totals[kind] = totals[kind] + term
            for kind, total in enumerate(totals):
                at = kind * n.tiles + tile
                far_out[at : at + 1, :] = jnp.sum(total, axis=0, keepdims=True)
    for copy in copies:
        copy.wait()


def adjoint_kernel(
    n, far_ref, target_ref, mask_ref, hi_lo_ref, v_ref, intensity_out, owned_out, adjoint_out, all_ref
):
    hi_ref, lo_ref = halves(n, hi_lo_ref)
    gz, dev, xy = (lax.axis_index(a) for a in ("gz", "dev", "xy"))
    block = n.far_rows + n.chunk
    parts = []
    for kind in range(4):
        total = None
        for k in range(n.gz):
            at = (n.gz - 1 - k) * block + kind * n.tiles
            term = far_ref[at : at + n.tiles, :]
            total = term if total is None else total + term
        parts.append(total)
    theta_re, phi_re, theta_im, phi_im = parts
    intensity = theta_re * theta_re + theta_im * theta_im + phi_re * phi_re + phi_im * phi_im
    if n.own_dirs % LANES == 0:
        all_ref[...] = intensity
        first = ((gz * n.dev + dev) * n.xy + xy) * (n.own_dirs // LANES)
        intensity_out[...] = all_ref[pl.ds(first, n.own_dirs // LANES), :]
    else:
        intensity_out[...] = intensity
    slope = 2.0 * (mask_ref[...].astype(F32) * (intensity - target_ref[...]))
    slopes = [slope * part for part in parts]

    faces = [[], []]
    for face in range(2):
        for t in range(n.tiles):
            lanes = slice(t * LANES, (t + 1) * LANES)
            w_theta, w_phi = face_weights(n, v_ref, face, lanes)
            even, odd = (
                w_theta * slopes[k][t : t + 1, :] + w_phi * slopes[k + 1][t : t + 1, :] for k in (0, 2)
            )
            rows = [
                factor * even + turn(factor * odd) for factor in patch_factors(n, v_ref, face, lanes)
            ]
            faces[face].append(jnp.concatenate(rows, axis=0))
    dot = functools.partial(
        lax.dot_general,
        dimension_numbers=(((1,), (1,)), ((), ())),
        preferred_element_type=F32,
    )
    sums = []
    for face, rows in ((0, slice(0, 2 * n.x)), (1, slice(2 * n.x, 2 * n.x + 2 * n.z))):
        left_hi, left_lo = split(jnp.concatenate(faces[face], axis=1))
        high, rest = hi_ref[rows, :], lo_ref[rows, :]
        sums.append(dot(left_hi, high) + (dot(left_lo, high) + dot(left_hi, rest)))
    cap, wall = sums
    row8, lane = rows_iota((8, LANES)), lanes_iota((8, LANES))
    own_block = lane // PATCH == row8
    for y in range(n.y):
        at = slice(y * 8, y * 8 + 8)
        gradient = cap[at, : n.x] - turn(cap[at, n.x :])
        adjoint_out[n.walls + y * 8 : n.walls + y * 8 + 8, 0, :] = block_transpose(gradient)
        gradient = wall[at, : n.z] - turn(wall[at, n.z :])
        spread = jnp.concatenate([gradient] * (LANES // n.z), axis=1)
        adjoint_out[y, :, :] = jnp.sum(
            jnp.where(own_block, spread, 0.0), axis=0, keepdims=True
        )
    walls = [jnp.zeros((1, LANES), F32) for _ in range(n.walls)]
    rank = jnp.zeros((1, LANES), F32)
    for s in range(n.gz):
        at = pl.multiple_of((n.gz - 1 - (gz ^ s)) * block + n.far_rows, 8)
        rows = far_ref[pl.ds(at, 8), :]
        record, flag = rows[0:1, :], rows[1:2, :] > 0.5
        for r in range(n.walls):
            walls[r] = jnp.where(flag & (rank == float(r)), record, walls[r])
        rank = rank + rows[1:2, :]
    for r in range(n.walls):
        owned_out[r, :, :] = walls[r]
    for cap_at, s in enumerate((0, n.gz - 1)):
        at = pl.multiple_of((n.gz - 1 - (gz ^ s)) * block + n.far_rows, 8)
        rows = far_ref[pl.ds(at, n.chunk), :]
        owned_out[n.walls + cap_at * n.share : n.walls + (cap_at + 1) * n.share, 0, :] = rows[2 : 2 + n.share, :]


def partner(kind, i, n):
    up = (i % 2 == 0) == (kind == 0)
    return (i + 1) % n if up else (i - 1) % n


def exchange(values, axes, image):
    sizes = [lax.axis_size(a) for a in axes]
    pairs = []
    for source in range(math.prod(sizes)):
        rest, where = source, []
        for size in reversed(sizes):
            where.insert(0, rest % size)
            rest //= size
        target = 0
        for size, at in zip(sizes, image(*where)):
            target = target * size + at
        pairs.append((source, target))
    return lax.ppermute(values, axes if len(axes) > 1 else axes[0], pairs)


def local(
    fields, spectra, permittivity, phase_start, wall_owner, cap_owner, dir_index, target, aim_mask
):
    n = Sizes(permittivity.shape, dir_index.shape[0], cap_owner.shape[1])
    gz = lax.axis_index("gz")

    def out(*shape, dtype=F32):
        return jax.ShapeDtypeStruct(shape, dtype)

    def far_memory(values):
        return pltpu.with_memory_space_constraint(values, pltpu.HBM)

    def params(mebibytes):
        return pltpu.CompilerParams(vmem_limit_bytes=mebibytes << 20)

    block = tuple(permittivity.shape)
    own, *y_send = pl.pallas_call(
        functools.partial(pack_kernel, n),
        name="pack",
        out_shape=[out(7, *block)] + [out(n.y_rows, n.x)] * n.y_kinds,
        in_specs=[HBM] * 2,
        out_specs=[VMEM] * (1 + n.y_kinds),
        scratch_shapes=[pltpu.VMEM(block, F32), pltpu.SemaphoreType.DMA((2,))],
        compiler_params=params(4),
    )(far_memory(fields), far_memory(permittivity))
    own = own.reshape(7 * n.y * n.z, n.x)
    y_got = [
        exchange(v, ("dev",), lambda d, k=k: (partner(k, d, n.dev),)) for k, v in enumerate(y_send)
    ]
    other = exchange(own, ("xy",), lambda x: (x ^ 1,))
    z_send, *e_send = pl.pallas_call(
        functools.partial(edge_kernel, n),
        name="edges",
        out_shape=[out(2 * n.z_rows, n.x)] + [out(2 * n.e_rows, n.x)] * n.y_kinds,
        in_specs=[VMEM] * 2,
        out_specs=[VMEM] * (1 + n.y_kinds),
        compiler_params=params(4),
    )(own, other)
    z_got = exchange(z_send, ("gz", "xy"), lambda g, x: (partner(x, g, n.gz), x))
    e_got = [
        exchange(
            v,
            ("gz", "dev", "xy"),
            lambda g, d, x, k=k: (partner(x, g, n.gz), partner(k, d, n.dev), x),
        )
        for k, v in enumerate(e_send)
    ]

    table, v, place = pl.pallas_call(
        functools.partial(table_kernel, n),
        name="tables",
        out_shape=[
            out(2 * n.table_rows, n.dirs, dtype=BF16),
            out(16 * n.y + 32, n.dirs),
            out(n.caps + n.walls, dtype=jnp.int32),
        ],
        in_specs=[HBM] * 3,
        out_specs=[VMEM] * 2 + [SMEM],
        scratch_shapes=[
            pltpu.SMEM((n.gz,), jnp.int32),
            pltpu.VMEM((n.tiles, LANES), jnp.int32),
            pltpu.SMEM(cap_owner.shape, jnp.int32),
            pltpu.SMEM(wall_owner.shape, jnp.int32),
            pltpu.SemaphoreType.DMA((3,)),
        ],
        compiler_params=params(8),
        cost_estimate=pl.CostEstimate(flops=1 << 33, bytes_accessed=16 << 20, transcendentals=0),
    )(*map(far_memory, (dir_index.reshape(n.tiles, LANES), cap_owner, wall_owner)))
    (*y_got, z_got, place), e_got = lax.optimization_barrier(((*y_got, z_got, place), e_got))
    halo = jnp.concatenate([*y_got, z_got, *e_got])
    far_halo = exchange(halo, ("xy",), lambda x: (x ^ 1,))

    anywhere = pl.BlockSpec(memory_space=pl.ANY)
    fields_out, spectra_out, far, chunk = pl.pallas_call(
        functools.partial(main_kernel, n),
        name="window",
        out_shape=[
            out(6, *block),
            out(12, *block),
            out(n.far_rows, LANES),
            out(n.gz * n.chunk, LANES),
        ],
        in_specs=[VMEM] * 4 + [anywhere, SMEM, SMEM] + [VMEM] * 2,
        out_specs=[anywhere] * 2 + [VMEM] * 2,
        scratch_shapes=[
            pltpu.VMEM((7, n.rows, n.z + 8, n.nx), F32),
            pltpu.VMEM((n.caps, LANES), F32),
            pltpu.VMEM((6, *block), F32),
            pltpu.VMEM((12, *block), F32),
            pltpu.SemaphoreType.DMA((3,)),
        ],
        compiler_params=params(12),
    )(own, other, halo, far_halo, spectra, place, phase_start, table, v)

    for axis in ("xy", "dev"):
        size = lax.axis_size(axis)
        got = [exchange(far, (axis,), lambda i, k=k: (i ^ k,)) for k in range(1, size)]
        for term in got:
            far = far + term
    payload = [
        jnp.concatenate([far, lax.dynamic_slice_in_dim(chunk, (gz ^ k) * n.chunk, n.chunk)])
        for k in range(n.gz)
    ]
    got = [
        exchange(payload[k], ("gz",), lambda g, k=k: (g ^ k,)) for k in range(n.gz - 1, 0, -1)
    ]
    gathered = jnp.concatenate([*got, payload[0]])

    sliced = n.own_dirs % LANES == 0
    intensity, owned, adjoint = pl.pallas_call(
        functools.partial(adjoint_kernel, n),
        name="adjoint",
        out_shape=[
            out(n.own_dirs // LANES if sliced else n.tiles, LANES),
            out(n.walls + 2 * n.share, 1, LANES),
            out(n.walls + n.caps, 1, LANES),
        ],
        in_specs=[VMEM] * 5,
        out_specs=[VMEM] * 3,
        scratch_shapes=[pltpu.VMEM((n.tiles, LANES), F32)],
        compiler_params=params(8),
    )(gathered, target.reshape(n.tiles, LANES), aim_mask.reshape(n.tiles, LANES), table, v)
    intensity = intensity.reshape(-1)
    if not sliced:
        joined = (gz * n.dev + lax.axis_index("dev")) * n.xy + lax.axis_index("xy")
        intensity = lax.dynamic_slice_in_dim(intensity, joined * n.own_dirs, n.own_dirs)
    shape = (1, 1, 1, -1, LANES)
    return fields_out, spectra_out, owned.reshape(shape), intensity, adjoint.reshape(shape)


def solution(mesh):
    placed = (
        P("groups", "dev", "gz", "xy"),
        P("groups", "dev", "gz", "xy"),
        P(("groups", "dev"), "gz", "xy"),
        P("groups"),
        P("gz", None),
        P(),
        P(),
        P("groups"),
        P("groups"),
    )
    return jax.shard_map(
        local,
        mesh=mesh,
        in_specs=placed,
        out_specs=(
            P("groups", "dev", "gz", "xy"),
            P("groups", "dev", "gz", "xy"),
            P(("groups", "gz"), "dev", "xy", None, None),
            P(("groups", "gz", "dev", "xy")),
            P(("groups", "gz"), "dev", "xy", None, None),
        ),
        check_vma=False,
    )
```

```python
import functools
import math

import jax
import jax.numpy as jnp
from jax import lax
from jax.experimental import pallas as pl
from jax.experimental.pallas import tpu as pltpu
from jax.sharding import PartitionSpec as P

PATCH = 16
XB = 8
ZB = 4
STEPS = 3
THETAS = 64
COURANT = 0.5
ANGULAR_STEP = 0.3
WAVE_NUMBER = 0.6
CURRENT_SIGNS = (-1.0, 1.0, 1.0, -1.0)
X_PICKS = (5, 4, 2, 1)
Z_PICKS = (4, 3, 1, 0)
LANES = 128
HALO = STEPS
F32 = jnp.float32
BF16 = jnp.bfloat16
VMEM = pl.BlockSpec(memory_space=pltpu.VMEM)
SMEM = pl.BlockSpec(memory_space=pltpu.SMEM)
HBM = pl.BlockSpec(memory_space=pltpu.HBM)


def up8(rows):
    return -(-rows // 8) * 8


def sincos(angle):
    turns = jnp.floor(angle * (2.0 / math.pi) + 0.5)
    r = angle - turns * 1.5703125
    r = r - turns * 4.837512969970703125e-4
    r = r - turns * 7.54978995489188e-8
    r2 = r * r
    s = r + r * r2 * (-1.6666654611e-1 + r2 * (8.3321608736e-3 + r2 * -1.9515295891e-4))
    c = 1.0 - 0.5 * r2 + r2 * r2 * (
        4.166664568298827e-2 + r2 * (-1.388731625493765e-3 + r2 * 2.443315711809948e-5)
    )
    quarter = turns.astype(jnp.int32)
    odd = (quarter & 1) == 1
    sine = jnp.where(odd, c, s)
    cosine = jnp.where(odd, s, c)
    sine = jnp.where((quarter & 2) == 2, -sine, sine)
    cosine = jnp.where(((quarter + 1) & 2) == 2, -cosine, cosine)
    return sine, cosine


def split(values):
    high = values.astype(BF16)
    return high, (values - high.astype(F32)).astype(BF16)


def three_products(dot, left, high, rest):
    left_hi, left_lo = split(left)
    both = dot(jnp.concatenate([left_hi, left_lo], axis=0), high)
    rows = left.shape[0]
    return both[:rows] + (both[rows:] + dot(left_hi, rest))


def rows_iota(shape):
    return lax.broadcasted_iota(jnp.int32, shape, 0)


def lanes_iota(shape):
    return lax.broadcasted_iota(jnp.int32, shape, len(shape) - 1)


class Sizes:
    def __init__(self, block, directions, caps):
        self.gz, self.dev, self.xy = (lax.axis_size(a) for a in ("gz", "dev", "xy"))
        self.y, self.z, self.x = block
        self.both_y = self.dev > 2
        self.rows = self.y + HALO * (2 if self.both_y else 1)
        self.nx, self.ny, self.nz = self.x * self.xy, self.y * self.dev, self.z * self.gz
        self.dirs = directions
        self.tiles = directions // LANES
        self.table_rows = 2 * self.x + 2 * self.z
        self.walls = self.y * self.z // PATCH
        self.caps = caps
        self.share = caps // self.gz
        self.own_dirs = directions // (self.gz * self.dev * self.xy)
        self.chunk = up8(2 + self.share)
        self.far_rows = 4 * self.tiles
        self.norm = 1.0 / math.sqrt(2.0 * (2 * self.ny * self.nz + 2 * self.ny * self.nx))
        self.y_rows = 7 * HALO * self.z
        self.z_rows = up8(7 * self.y * HALO)
        self.e_rows = up8(7 * HALO * HALO)
        y_kinds = 2 if self.both_y else 1
        sizes = [self.y_rows] * y_kinds + [2 * self.z_rows] + [2 * self.e_rows] * y_kinds
        self.starts = [sum(sizes[:i]) for i in range(len(sizes))]
        self.halo_rows = sum(sizes)
        self.y_kinds = y_kinds


def pack_kernel(n, f_hbm, eps_hbm, own, *rest):
    y_outs, (eps_ref, sems) = rest[: n.y_kinds], rest[n.y_kinds :]
    copies = (
        pltpu.make_async_copy(f_hbm, own.at[0:6], sems.at[0]),
        pltpu.make_async_copy(eps_hbm, eps_ref, sems.at[1]),
    )
    for copy in copies:
        copy.start()
    for copy in copies:
        copy.wait()
    dev_even = lax.axis_index("dev") % 2 == 0
    for y in range(n.y):
        own[6, y] = COURANT / eps_ref[y]
    for c in range(7):
        at = [own[c, y] for y in range(n.y)]
        for kind in range(n.y_kinds):
            top = dev_even if kind == 0 else jnp.logical_not(dev_even)
            for r in range(HALO):
                value = jnp.where(top, at[n.y - HALO + r], at[r])
                y_outs[kind][pl.ds((c * HALO + r) * n.z, n.z), :] = value


def edge_kernel(n, own_ref, other_ref, z_out, *e_outs):
    xy = lax.axis_index("xy")
    dev_even = lax.axis_index("dev") % 2 == 0
    z_top = lax.axis_index("gz") % 2 == xy % 2
    for half in range(2):
        mine = xy == half

        def at(c, y):
            rows = pl.ds((c * n.y + y) * n.z, n.z)
            value = jnp.where(mine, own_ref[rows, :], other_ref[rows, :])
            return jnp.where(z_top, value[n.z - HALO :], value[:HALO])

        for c in range(7):
            edges = [at(c, y) for y in range(n.y)]
            for y in range(n.y):
                z_out[pl.ds(half * n.z_rows + (c * n.y + y) * HALO, HALO), :] = edges[y]
            for kind in range(n.y_kinds):
                top = dev_even if kind == 0 else jnp.logical_not(dev_even)
                for r in range(HALO):
                    edge = jnp.where(top, edges[n.y - HALO + r], edges[r])
                    e_outs[kind][pl.ds(half * n.e_rows + (c * HALO + r) * HALO, HALO), :] = edge


def table_kernel(
    n, dir_hbm, owner_hbm, wall_owner_hbm, hi_lo_ref, v_ref, place_ref,
    count_ref, dir_ref, owner_ref, wall_owner_ref, sems,
):
    gz, dev, xy = (lax.axis_index(a) for a in ("gz", "dev", "xy"))
    hi_ref, lo_ref = halves(n, hi_lo_ref)
    copies = [
        pltpu.make_async_copy(source, target, sems.at[i])
        for i, (source, target) in enumerate(
            (
                (dir_hbm, dir_ref),
                (owner_hbm, owner_ref),
                (wall_owner_hbm, wall_owner_ref),
            )
        )
    ]
    for copy in copies:
        copy.start()
    for copy in copies:
        copy.wait()
    index = dir_ref[...]
    bits = THETAS.bit_length() - 1
    polar = (index >> bits).astype(F32)
    azimuth = (index & (THETAS - 1)).astype(F32)
    sin_t, cos_t = sincos(math.pi * (polar + 0.5) / THETAS)
    sin_f, cos_f = sincos(2.0 * math.pi * azimuth / THETAS)
    kx = WAVE_NUMBER * (sin_t * cos_f)
    ky = WAVE_NUMBER * (sin_t * sin_f)
    kz = WAVE_NUMBER * cos_t
    theta = (cos_t * cos_f, cos_t * sin_f, -sin_t)
    phi = (-sin_f, cos_f, jnp.zeros_like(sin_f))
    is_end = jnp.logical_or(gz == 0, gz == n.gz - 1)
    cap_scale = jnp.where(is_end, n.norm, 0.0).astype(F32)
    x_first = (xy * n.x).astype(F32) - (n.nx - 1) / 2.0
    y_first = (dev * n.y).astype(F32) - (n.ny - 1) / 2.0
    z_first = (gz * n.z).astype(F32) - (n.nz - 1) / 2.0
    x_wall = x_first + jnp.where(xy == 0, XB, n.x - 1 - XB).astype(F32)
    z_cap = z_first + jnp.where(gz == 0, ZB, n.z - 1 - ZB).astype(F32)
    row8 = rows_iota((8, LANES))
    row16 = rows_iota((16, LANES))
    fine_x = row8.astype(F32)
    low = row8 < 4
    comp = row8 & 3

    def weights(rows):
        picked = jnp.where(comp == 2, rows[2], rows[3])
        return jnp.where(comp == 0, rows[0], jnp.where(comp == 1, rows[1], picked))

    for t in range(n.tiles):
        lanes = slice(t * LANES, (t + 1) * LANES)
        a, b, c = (v[t : t + 1, :] for v in (kx, ky, kz))
        th = [v[t : t + 1, :] for v in theta]
        ph = [v[t : t + 1, :] for v in phi]
        sf, cf = sincos(a * fine_x)
        for pair in range(n.x // 16):
            if pair % 8 == 0:
                base_x = x_first + 8.0 * 16.0 * (pair // 8)
                coarse_s, coarse_c = sincos(a * (row16.astype(F32) * 8.0 + base_x))
            cosine, sine = [], []
            for h in (2 * (pair % 8), 2 * (pair % 8) + 1):
                cc, cs = coarse_c[h : h + 1, :], coarse_s[h : h + 1, :]
                cosine.append(cc * cf - cs * sf)
                sine.append(cs * cf + cc * sf)
            for part, rows in ((0, cosine), (n.x, sine)):
                high, rest = split(jnp.concatenate(rows, axis=0))
                hi_ref[part + pair * 16 : part + pair * 16 + 16, lanes] = high
                lo_ref[part + pair * 16 : part + pair * 16 + 16, lanes] = rest
        zs, zc = sincos(c * (row16.astype(F32) + z_first))
        for part, rows in ((2 * n.x, zc), (2 * n.x + n.z, zs)):
            high, rest = split(rows)
            hi_ref[part : part + 16, lanes] = high
            lo_ref[part : part + 16, lanes] = rest
        y_of = comp.astype(F32) + y_first
        base_s, base_c = sincos(b * y_of + jnp.where(low, c * z_cap, a * x_wall))
        for face in range(2):
            i, j = ((0, 1), (1, 2))[face]
            scale = cap_scale if face == 0 else n.norm
            w_theta = weights([-th[i], -th[j], -ph[i], -ph[j]]) * scale
            w_phi = weights([-ph[i], -ph[j], th[i], th[j]]) * scale
            for kind, value in enumerate((w_theta, w_phi)):
                at = 16 * n.y + (face * 2 + kind) * 8
                v_ref[at : at + 8, lanes] = value
        for r in range(2 * n.y):
            factor = jnp.where(low, base_c[r : r + 1, :], -base_s[r : r + 1, :])
            v_ref[8 * r : 8 * r + 8, lanes] = factor
    for o in range(n.gz):
        count_ref[o] = 0
    which = jnp.where(gz == 0, 0, 1)

    def place(q, carry):
        owner = owner_ref[which, q]
        rank = count_ref[owner]
        count_ref[owner] = rank + 1
        place_ref[q] = owner * n.chunk + 2 + rank
        return carry

    lax.fori_loop(0, n.caps, place, 0)
    for j in range(n.walls):
        place_ref[n.caps + j] = wall_owner_ref[0, j]


def halves(n, hi_lo_ref):
    return hi_lo_ref.at[0 : n.table_rows], hi_lo_ref.at[n.table_rows : 2 * n.table_rows]


def block_transpose(values):
    row, block = rows_iota((8, LANES)), lanes_iota((8, LANES)) // PATCH
    for bit in (1, 2, 4):
        wide = PATCH * bit
        ahead = pltpu.roll(pltpu.roll(values, 8 - bit, 0), wide, 1)
        behind = pltpu.roll(pltpu.roll(values, bit, 0), LANES - wide, 1)
        row_bit, block_bit = (row & bit) != 0, (block & bit) != 0
        moved = jnp.where(row_bit, behind, ahead)
        values = jnp.where(row_bit == block_bit, values, moved)
    return values


def patch_factors(n, v_ref, face, lanes):
    at = [(face * n.y + y) * 8 for y in range(n.y)]
    return [v_ref[r : r + 8, lanes] for r in at]


def face_weights(n, v_ref, face, lanes):
    at = [16 * n.y + (face * 2 + kind) * 8 for kind in range(2)]
    return [v_ref[r : r + 8, lanes] for r in at]


def turn(values):
    swapped = pltpu.roll(values, 4, 0)
    return jnp.where(rows_iota(values.shape) < 4, -swapped, swapped)


def main_kernel(
    n, own_ref, other_ref, halo_ref, far_halo_ref, spectra_hbm, place_ref, phase_ref, hi_lo_ref, v_ref,
    fields_hbm, spectra_out_hbm, far_out, chunk_out, a_ref, m_ref, fields_out, spectra_out, sems,
):
    hi_ref, lo_ref = halves(n, hi_lo_ref)
    spectra_in = pltpu.make_async_copy(spectra_hbm, spectra_out, sems.at[0])
    spectra_in.start()
    gz, dev, xy = (lax.axis_index(a) for a in ("gz", "dev", "xy"))
    gz_even, dev_even = gz % 2 == 0, dev % 2 == 0
    deep = n.z + 8
    lo_ok, hi_ok = gz > 0, gz < n.gz - 1
    if n.both_y:
        y_own = HALO
        y_slots = (
            (0, jnp.logical_not(dev_even), dev > 0),
            (HALO + n.y, dev_even, dev < n.dev - 1),
        )
    else:
        y_own = jnp.where(dev_even, 0, HALO)
        y_slots = ((jnp.where(dev_even, n.y, 0), None, None),)
    pad = jnp.zeros((8 - 2 * HALO, LANES), F32)
    near_is_high = gz % 2 == xy % 2

    def choose(ref, starts, use_first, length):
        if use_first is None:
            return ref[pl.ds(starts[0], length), :]
        return jnp.where(
            use_first, ref[pl.ds(starts[0], length), :], ref[pl.ds(starts[1], length), :]
        )

    def rim(near, far):
        high = jnp.where(near_is_high, near, far)
        low = jnp.where(near_is_high, far, near)
        return jnp.concatenate(
            [jnp.where(hi_ok, high, 0.0), pad, jnp.where(lo_ok, low, 0.0)], axis=0
        )

    kinds = n.y_kinds
    both = (halo_ref, far_halo_ref)
    for half, (block, halo) in enumerate(((own_ref, halo_ref), (other_ref, far_halo_ref))):
        at_x = xy if half == 0 else 1 - xy
        lanes = pl.ds(pl.multiple_of(at_x * n.x, n.x), n.x)
        for c in range(7):
            for y in range(n.y):
                a_ref[c, y_own + y, 0 : n.z, lanes] = block[pl.ds((c * n.y + y) * n.z, n.z), :]
            for start, use_first, ok in y_slots:
                for r in range(HALO):
                    at = (c * HALO + r) * n.z
                    body = choose(halo, [n.starts[k] + at for k in range(kinds)], use_first, n.z)
                    if ok is not None:
                        body = jnp.where(ok, body, 0.0)
                    a_ref[c, start + r, 0 : n.z, lanes] = body
    for half in range(2):
        lanes = slice(half * n.x, (half + 1) * n.x)
        for c in range(7):
            for y in range(n.y):
                at = n.starts[kinds] + half * n.z_rows + (c * n.y + y) * HALO
                a_ref[c, y_own + y, n.z : deep, lanes] = rim(*(ref[pl.ds(at, HALO), :] for ref in both))
            for start, use_first, ok in y_slots:
                for r in range(HALO):
                    at = half * n.e_rows + (c * HALO + r) * HALO
                    starts = [n.starts[kinds + 1 + k] + at for k in range(kinds)]
                    edge = rim(*(choose(ref, starts, use_first, HALO) for ref in both))
                    if ok is not None:
                        edge = jnp.where(ok, edge, 0.0)
                    a_ref[c, start + r, n.z : deep, lanes] = edge

    shape = (deep, n.nx)
    z_row, x_lane = rows_iota(shape), lanes_iota(shape)
    keep = jnp.where(z_row < n.z + HALO, COURANT, jnp.where(lo_ok & (z_row >= deep - HALO), COURANT, 0.0))
    keep = keep.astype(F32)
    last_x, first_x = x_lane == n.nx - 1, x_lane == 0

    def z_next(v):
        return pltpu.roll(v, deep - 1, 0)

    def z_before(v):
        return pltpu.roll(v, 1, 0)

    def x_next(v):
        return jnp.where(last_x, 0.0, pltpu.roll(v, n.nx - 1, 1))

    def x_before(v):
        return jnp.where(first_x, 0.0, pltpu.roll(v, 1, 1))

    own_lanes = pl.ds(pl.multiple_of(xy * n.x, n.x), n.x)
    angle_row = rows_iota((8, LANES))
    step_of = (angle_row // 2).astype(F32)
    part_of = jnp.where((angle_row & 1) == 0, 0.5, 1.0)
    sines, cosines = sincos(phase_ref[0] + ANGULAR_STEP * (step_of + part_of))
    for step in range(STEPS):
        for y in range(n.rows):
            ex, ey, ez = (a_ref[c, y] for c in range(3))
            if y + 1 < n.rows:
                ex_y, ez_y = a_ref[0, y + 1] - ex, a_ref[2, y + 1] - ez
            else:
                ex_y, ez_y = -ex, -ez
            rate = keep
            if n.both_y and y < HALO:
                rate = jnp.where(dev == 0, 0.0, keep)
            a_ref[3, y] = a_ref[3, y] - rate * (ez_y - (z_next(ey) - ey))
            a_ref[4, y] = a_ref[4, y] - rate * ((z_next(ex) - ex) - (x_next(ez) - ez))
            a_ref[5, y] = a_ref[5, y] - rate * ((x_next(ey) - ey) - ex_y)
        for y in range(n.rows):
            hx, hy, hz = (a_ref[c, y] for c in range(3, 6))
            rate = a_ref[6, y]
            if y > 0:
                hx_y, hz_y = hx - a_ref[3, y - 1], hz - a_ref[5, y - 1]
            else:
                hx_y, hz_y = hx, hz
            a_ref[0, y] = a_ref[0, y] + rate * (hz_y - (hy - z_before(hy)))
            a_ref[1, y] = a_ref[1, y] + rate * ((hx - z_before(hx)) - (hz - x_before(hz)))
            a_ref[2, y] = a_ref[2, y] + rate * ((hy - x_before(hy)) - hx_y)
        if step == 0:
            spectra_in.wait()
        for c in range(6):
            row = 2 * step + (1 if c < 3 else 0)
            cosine, sine = cosines[row : row + 1, :], sines[row : row + 1, :]
            for y in range(n.y):
                value = a_ref[c, y_own + y, 0 : n.z, own_lanes]
                spectra_out[c, y] = spectra_out[c, y] + value * cosine
                spectra_out[6 + c, y] = spectra_out[6 + c, y] - value * sine
                if step == STEPS - 1:
                    fields_out[c, y] = value

    copies = (
        pltpu.make_async_copy(fields_out, fields_hbm, sems.at[1]),
        pltpu.make_async_copy(spectra_out, spectra_out_hbm, sems.at[2]),
    )
    for copy in copies:
        copy.start()
    facing_x = jnp.where(xy == 0, -1.0, 1.0).astype(F32)
    facing_z = jnp.where(gz == 0, -1.0, 1.0).astype(F32)
    row8, lane = rows_iota((8, LANES)), lanes_iota((8, LANES))
    sign = jnp.where(((row8 & 3) == 0) | ((row8 & 3) == 3), -1.0, 1.0).astype(F32)
    own_block = lane // PATCH == row8
    block_sign = jnp.sum(jnp.where(own_block, sign, 0.0), axis=0, keepdims=True)
    cap_left, cap_right, wall_left = [], [], []
    chunk_out[...] = jnp.zeros_like(chunk_out)
    for y in range(n.y):
        plane = [
            jnp.where(gz == 0, spectra_out[p, y, ZB : ZB + 1, :], spectra_out[p, y, n.z - 1 - ZB : n.z - ZB, :])
            for p in [k + 6 * im for im in range(2) for k in Z_PICKS]
        ]
        current = jnp.concatenate(plane, axis=0) * (sign * facing_z)
        cap_left.append(current)
        cap_right.append(turn(current))
        m_ref[y * 8 : y * 8 + 8, :] = block_transpose(current)
        stack = jnp.concatenate(
            [spectra_out[k + 6 * im, y] for im in range(2) for k in X_PICKS], axis=0
        )
        across = stack.T
        record = jnp.where(xy == 0, across[XB : XB + 1, :], across[n.x - 1 - XB : n.x - XB, :])
        record = record * (block_sign * facing_x)
        for o in range(n.gz):
            mine = place_ref[n.caps + y] == o
            at = o * n.chunk
            chunk_out[at : at + 1, :] += jnp.where(mine, record, 0.0)
            chunk_out[at + 1 : at + 2, :] += jnp.where(mine, 1.0, 0.0).astype(F32)
        spread = jnp.where(own_block, record, 0.0)
        for wide in (16, 32, 64):
            spread = spread + pltpu.roll(spread, wide, 1)
        wall_left.append(jnp.where(lane < n.z, spread, turn(spread))[:, : 2 * n.z])
    for q in range(n.caps):
        chunk_out[pl.ds(place_ref[q], 1), :] = m_ref[q : q + 1, :]
    cap = jnp.concatenate(
        [jnp.concatenate(cap_left, axis=0), jnp.concatenate(cap_right, axis=0)], axis=1
    )
    wall = jnp.concatenate(wall_left, axis=0)
    dot = functools.partial(jnp.dot, preferred_element_type=F32)
    wide = min(512, n.dirs)
    for first in range(0, n.dirs, wide):
        sums = []
        for left, rows in ((cap, slice(0, 2 * n.x)), (wall, slice(2 * n.x, 2 * n.x + 2 * n.z))):
            high, rest = hi_ref[rows, first : first + wide], lo_ref[rows, first : first + wide]
            sums.append(three_products(dot, left, high, rest))
        for t in range(wide // LANES):
            lanes = slice(first + t * LANES, first + (t + 1) * LANES)
            tile = first // LANES + t
            totals = [0.0] * 4
            for face in range(2):
                even, odd = 0.0, 0.0
                for y, factor in enumerate(patch_factors(n, v_ref, face, lanes)):
                    rows = sums[face][y * 8 : y * 8 + 8, t * LANES : (t + 1) * LANES]
                    even = even + factor * rows
                    odd = odd - factor * turn(rows)
                w_theta, w_phi = face_weights(n, v_ref, face, lanes)
                for kind, term in enumerate((w_theta * even, w_phi * even, w_theta * odd, w_phi * odd)):
                    totals[kind] = totals[kind] + term
            for kind, total in enumerate(totals):
                at = kind * n.tiles + tile
                far_out[at : at + 1, :] = jnp.sum(total, axis=0, keepdims=True)
    for copy in copies:
        copy.wait()


def adjoint_kernel(
    n, far_ref, target_ref, mask_ref, hi_lo_ref, v_ref, intensity_out, owned_out, adjoint_out, all_ref
):
    hi_ref, lo_ref = halves(n, hi_lo_ref)
    gz, dev, xy = (lax.axis_index(a) for a in ("gz", "dev", "xy"))
    block = n.far_rows + n.chunk
    parts = []
    for kind in range(4):
        total = None
        for k in range(n.gz):
            at = (n.gz - 1 - k) * block + kind * n.tiles
            term = far_ref[at : at + n.tiles, :]
            total = term if total is None else total + term
        parts.append(total)
    theta_re, phi_re, theta_im, phi_im = parts
    intensity = theta_re * theta_re + theta_im * theta_im + phi_re * phi_re + phi_im * phi_im
    if n.own_dirs % LANES == 0:
        all_ref[...] = intensity
        first = ((gz * n.dev + dev) * n.xy + xy) * (n.own_dirs // LANES)
        intensity_out[...] = all_ref[pl.ds(first, n.own_dirs // LANES), :]
    else:
        intensity_out[...] = intensity
    slope = 2.0 * (mask_ref[...].astype(F32) * (intensity - target_ref[...]))
    slopes = [slope * part for part in parts]

    faces = [[], []]
    for face in range(2):
        for t in range(n.tiles):
            lanes = slice(t * LANES, (t + 1) * LANES)
            w_theta, w_phi = face_weights(n, v_ref, face, lanes)
            even, odd = (
                w_theta * slopes[k][t : t + 1, :] + w_phi * slopes[k + 1][t : t + 1, :] for k in (0, 2)
            )
            rows = [
                factor * even + turn(factor * odd) for factor in patch_factors(n, v_ref, face, lanes)
            ]
            faces[face].append(jnp.concatenate(rows, axis=0))
    dot = functools.partial(
        lax.dot_general,
        dimension_numbers=(((1,), (1,)), ((), ())),
        preferred_element_type=F32,
    )
    sums = []
    for face, rows in ((0, slice(0, 2 * n.x)), (1, slice(2 * n.x, 2 * n.x + 2 * n.z))):
        left = jnp.concatenate(faces[face], axis=1)
        sums.append(three_products(dot, left, hi_ref[rows, :], lo_ref[rows, :]))
    cap, wall = sums
    row8, lane = rows_iota((8, LANES)), lanes_iota((8, LANES))
    own_block = lane // PATCH == row8
    for y in range(n.y):
        at = slice(y * 8, y * 8 + 8)
        gradient = cap[at, : n.x] - turn(cap[at, n.x :])
        adjoint_out[n.walls + y * 8 : n.walls + y * 8 + 8, 0, :] = block_transpose(gradient)
        gradient = wall[at, : n.z] - turn(wall[at, n.z :])
        spread = jnp.concatenate([gradient] * (LANES // n.z), axis=1)
        adjoint_out[y, :, :] = jnp.sum(
            jnp.where(own_block, spread, 0.0), axis=0, keepdims=True
        )
    walls = [jnp.zeros((1, LANES), F32) for _ in range(n.walls)]
    rank = jnp.zeros((1, LANES), F32)
    for s in range(n.gz):
        at = pl.multiple_of((n.gz - 1 - (gz ^ s)) * block + n.far_rows, 8)
        rows = far_ref[pl.ds(at, 8), :]
        record, flag = rows[0:1, :], rows[1:2, :] > 0.5
        for r in range(n.walls):
            walls[r] = jnp.where(flag & (rank == float(r)), record, walls[r])
        rank = rank + rows[1:2, :]
    for r in range(n.walls):
        owned_out[r, :, :] = walls[r]
    for cap_at, s in enumerate((0, n.gz - 1)):
        at = pl.multiple_of((n.gz - 1 - (gz ^ s)) * block + n.far_rows, 8)
        rows = far_ref[pl.ds(at, n.chunk), :]
        owned_out[n.walls + cap_at * n.share : n.walls + (cap_at + 1) * n.share, 0, :] = rows[2 : 2 + n.share, :]


def partner(kind, i, n):
    up = (i % 2 == 0) == (kind == 0)
    return (i + 1) % n if up else (i - 1) % n


def exchange(values, axes, image):
    sizes = [lax.axis_size(a) for a in axes]
    pairs = []
    for source in range(math.prod(sizes)):
        rest, where = source, []
        for size in reversed(sizes):
            where.insert(0, rest % size)
            rest //= size
        target = 0
        for size, at in zip(sizes, image(*where)):
            target = target * size + at
        pairs.append((source, target))
    return lax.ppermute(values, axes if len(axes) > 1 else axes[0], pairs)


def local(
    fields, spectra, permittivity, phase_start, wall_owner, cap_owner, dir_index, target, aim_mask
):
    n = Sizes(permittivity.shape, dir_index.shape[0], cap_owner.shape[1])
    gz = lax.axis_index("gz")

    def out(*shape, dtype=F32):
        return jax.ShapeDtypeStruct(shape, dtype)

    def far_memory(values):
        return pltpu.with_memory_space_constraint(values, pltpu.HBM)

    def params(mebibytes):
        return pltpu.CompilerParams(vmem_limit_bytes=mebibytes << 20)

    block = tuple(permittivity.shape)
    own, *y_send = pl.pallas_call(
        functools.partial(pack_kernel, n),
        name="pack",
        out_shape=[out(7, *block)] + [out(n.y_rows, n.x)] * n.y_kinds,
        in_specs=[HBM] * 2,
        out_specs=[VMEM] * (1 + n.y_kinds),
        scratch_shapes=[pltpu.VMEM(block, F32), pltpu.SemaphoreType.DMA((2,))],
        compiler_params=params(4),
    )(far_memory(fields), far_memory(permittivity))
    own = own.reshape(7 * n.y * n.z, n.x)
    y_got = [
        exchange(v, ("dev",), lambda d, k=k: (partner(k, d, n.dev),)) for k, v in enumerate(y_send)
    ]
    other = exchange(own, ("xy",), lambda x: (x ^ 1,))
    z_send, *e_send = pl.pallas_call(
        functools.partial(edge_kernel, n),
        name="edges",
        out_shape=[out(2 * n.z_rows, n.x)] + [out(2 * n.e_rows, n.x)] * n.y_kinds,
        in_specs=[VMEM] * 2,
        out_specs=[VMEM] * (1 + n.y_kinds),
        compiler_params=params(4),
    )(own, other)
    z_got = exchange(z_send, ("gz", "xy"), lambda g, x: (partner(x, g, n.gz), x))
    e_got = [
        exchange(
            v,
            ("gz", "dev", "xy"),
            lambda g, d, x, k=k: (partner(x, g, n.gz), partner(k, d, n.dev), x),
        )
        for k, v in enumerate(e_send)
    ]

    table, v, place = pl.pallas_call(
        functools.partial(table_kernel, n),
        name="tables",
        out_shape=[
            out(2 * n.table_rows, n.dirs, dtype=BF16),
            out(16 * n.y + 32, n.dirs),
            out(n.caps + n.walls, dtype=jnp.int32),
        ],
        in_specs=[HBM] * 3,
        out_specs=[VMEM] * 2 + [SMEM],
        scratch_shapes=[
            pltpu.SMEM((n.gz,), jnp.int32),
            pltpu.VMEM((n.tiles, LANES), jnp.int32),
            pltpu.SMEM(cap_owner.shape, jnp.int32),
            pltpu.SMEM(wall_owner.shape, jnp.int32),
            pltpu.SemaphoreType.DMA((3,)),
        ],
        compiler_params=params(8),
        cost_estimate=pl.CostEstimate(flops=1 << 33, bytes_accessed=16 << 20, transcendentals=0),
    )(*map(far_memory, (dir_index.reshape(n.tiles, LANES), cap_owner, wall_owner)))
    (*y_got, z_got, place), e_got = lax.optimization_barrier(((*y_got, z_got, place), e_got))
    halo = jnp.concatenate([*y_got, z_got, *e_got])
    far_halo = exchange(halo, ("xy",), lambda x: (x ^ 1,))

    anywhere = pl.BlockSpec(memory_space=pl.ANY)
    fields_out, spectra_out, far, chunk = pl.pallas_call(
        functools.partial(main_kernel, n),
        name="window",
        out_shape=[
            out(6, *block),
            out(12, *block),
            out(n.far_rows, LANES),
            out(n.gz * n.chunk, LANES),
        ],
        in_specs=[VMEM] * 4 + [anywhere, SMEM, SMEM] + [VMEM] * 2,
        out_specs=[anywhere] * 2 + [VMEM] * 2,
        scratch_shapes=[
            pltpu.VMEM((7, n.rows, n.z + 8, n.nx), F32),
            pltpu.VMEM((n.caps, LANES), F32),
            pltpu.VMEM((6, *block), F32),
            pltpu.VMEM((12, *block), F32),
            pltpu.SemaphoreType.DMA((3,)),
        ],
        compiler_params=params(12),
    )(own, other, halo, far_halo, spectra, place, phase_start, table, v)

    for axis in ("xy", "dev"):
        size = lax.axis_size(axis)
        got = [exchange(far, (axis,), lambda i, k=k: (i ^ k,)) for k in range(1, size)]
        for term in got:
            far = far + term
    payload = [
        jnp.concatenate([far, lax.dynamic_slice_in_dim(chunk, (gz ^ k) * n.chunk, n.chunk)])
        for k in range(n.gz)
    ]
    got = [
        exchange(payload[k], ("gz",), lambda g, k=k: (g ^ k,)) for k in range(n.gz - 1, 0, -1)
    ]
    gathered = jnp.concatenate([*got, payload[0]])

    sliced = n.own_dirs % LANES == 0
    intensity, owned, adjoint = pl.pallas_call(
        functools.partial(adjoint_kernel, n),
        name="adjoint",
        out_shape=[
            out(n.own_dirs // LANES if sliced else n.tiles, LANES),
            out(n.walls + 2 * n.share, 1, LANES),
            out(n.walls + n.caps, 1, LANES),
        ],
        in_specs=[VMEM] * 5,
        out_specs=[VMEM] * 3,
        scratch_shapes=[pltpu.VMEM((n.tiles, LANES), F32)],
        compiler_params=params(8),
    )(gathered, target.reshape(n.tiles, LANES), aim_mask.reshape(n.tiles, LANES), table, v)
    intensity = intensity.reshape(-1)
    if not sliced:
        joined = (gz * n.dev + lax.axis_index("dev")) * n.xy + lax.axis_index("xy")
        intensity = lax.dynamic_slice_in_dim(intensity, joined * n.own_dirs, n.own_dirs)
    shape = (1, 1, 1, -1, LANES)
    return fields_out, spectra_out, owned.reshape(shape), intensity, adjoint.reshape(shape)


def solution(mesh):
    placed = (
        P("groups", "dev", "gz", "xy"),
        P("groups", "dev", "gz", "xy"),
        P(("groups", "dev"), "gz", "xy"),
        P("groups"),
        P("gz", None),
        P(),
        P(),
        P("groups"),
        P("groups"),
    )
    return jax.shard_map(
        local,
        mesh=mesh,
        in_specs=placed,
        out_specs=(
            P("groups", "dev", "gz", "xy"),
            P("groups", "dev", "gz", "xy"),
            P(("groups", "gz"), "dev", "xy", None, None),
            P(("groups", "gz", "dev", "xy")),
            P(("groups", "gz"), "dev", "xy", None, None),
        ),
        check_vma=False,
    )
```
